128 devices in a mesh: blk: 32 (over x, y, z_hi), head: 4 (over z_lo, core).
Axes of the slice: x: 4, y: 4, z: 4 (z_hi: 2, z_lo: 2; z = z_hi * 2 + z_lo), core: 2. Of those that a mesh axis runs over, the one named last changes fastest.
Arguments:
- x_video: bfloat16 [16384, 3072], P(('blk', 'head')), may hold values from -6 to 6
- x_text: bfloat16 [256, 3072], replicated, may hold values from -6 to 6
- w_qkv_video: bfloat16 [3072, 3, 1536], P(None, None, 'head'), may hold values from -0.109375 to 0.109375
- w_qkv_text: bfloat16 [3072, 3, 1536], P(None, None, 'head'), may hold values from -0.109375 to 0.109375
- w_out_video: bfloat16 [1536, 3072], P('head'), may hold values from -0.15625 to 0.15625
- w_out_text: bfloat16 [1536, 3072], P('head'), may hold values from -0.15625 to 0.15625
- qk_gains: float32 [4, 128], replicated, may hold values from 0.8 to 1.4
- modulation: float32 [50, 6, 3072], replicated, may hold values from -3 to 3
- text_len: int32 [1], replicated, may hold values from 64 to 256
- timestep: int32 [1], replicated, may hold values from 0 to 49
Outputs:
- video_out: bfloat16 [16384, 3072], P(('blk', 'head'))
- text_out: bfloat16 [256, 3072], P('head')
The draws below stay inside these ranges and needn't reach their ends.
All inputs are finite; a program needn't handle non-finite values.
Results may differ from the reference program's by a relative error of at most 0.0052.
Values may be sent and summed in bfloat16 or wider, within the bound.
A program may use at most 192 MiB of HBM per device.

```python
import math
import jax
import jax.numpy as jnp
from jax import lax

D = 3072
HEAD_DIM = 128
TXT = 256
STEPS = 50
TV = 16384
HC = 1536


def block_levels(stream_key, shape, cuts, smallest, largest):
    def one(position, shards_of):
        heights = jax.random.uniform(jax.random.fold_in(jax.random.fold_in(stream_key, 6), position), (shards_of,), jnp.float32, smallest / len(cuts), largest / len(cuts))
        return jnp.repeat(jnp.exp(heights), shape[position] // shards_of).reshape((-1,) + (1,) * (len(shape) - position - 1))

    level = one(*cuts[0])
    for cut in cuts[1:]:
        level = level * one(*cut)
    return level


def scatter_about(own_key, extent, spread, limit, cuts=(), held_as=jnp.bfloat16):
    values = spread * jax.random.normal(own_key, extent, jnp.float32)
    if cuts:
        values = values * block_levels(own_key, extent, cuts, -0.22, 0.18)
    return jnp.clip(values, -limit, limit).astype(held_as)


def setup_inputs(seed: int = 0) -> dict:
    arg_keys = jax.random.split(jax.random.key(seed), 11)
    x_video = scatter_about(arg_keys[0], (TV, D), 1.0, 6.0, ((0, 128),))
    x_text = scatter_about(arg_keys[1], (TXT, D), 1.0, 6.0)
    w_qkv_video = scatter_about(arg_keys[2], (D, 3, HC), D ** -0.5, 0.109375, ((2, 4),))
    w_qkv_text = scatter_about(arg_keys[3], (D, 3, HC), D ** -0.5, 0.109375, ((2, 4),))
    w_out_video = scatter_about(arg_keys[4], (HC, D), HC ** -0.5, 0.15625, ((0, 4),))
    w_out_text = scatter_about(arg_keys[5], (HC, D), HC ** -0.5, 0.15625, ((0, 4),))
    qk_gains = jnp.clip(jax.random.uniform(arg_keys[6], (4, HEAD_DIM), jnp.float32, 0.8, 1.4), 0.8, 1.4)
    modulation = scatter_about(arg_keys[7], (STEPS, 6, D), 0.5, 3.0, (), jnp.float32)
    text_len = jax.random.randint(arg_keys[8], (1,), TXT // 4, TXT + 1).astype(jnp.int32)
    timestep = jax.random.randint(arg_keys[9], (1,), 0, STEPS).astype(jnp.int32)
    return dict(x_video=x_video, x_text=x_text, w_qkv_video=w_qkv_video, w_qkv_text=w_qkv_text, w_out_video=w_out_video, w_out_text=w_out_text, qk_gains=qk_gains, modulation=modulation, text_len=text_len, timestep=timestep)


def norm_modulate(tokens, shift, scale):
    wide = tokens.astype(jnp.float32)
    centred = wide - lax.optimization_barrier(jnp.mean(wide, axis=-1, keepdims=True))
    variance = lax.optimization_barrier(jnp.mean(centred * centred, axis=-1, keepdims=True))
    return (centred * lax.rsqrt(variance + 1e-06) * (1.0 + scale) + shift).astype(jnp.bfloat16)

def head_norm(values, gain):
    count, width = values.shape
    split = values.reshape(count, width // HEAD_DIM, HEAD_DIM)
    meansq = lax.optimization_barrier(jnp.mean(split * split, axis=-1, keepdims=True))
    return (split * lax.rsqrt(meansq + 1e-06) * gain).reshape(count, width).astype(jnp.bfloat16)

def project(normed, weight, gain_query, gain_key):
    width = weight.shape[2]
    flat = jnp.dot(normed, weight.reshape(weight.shape[0], 3 * width), preferred_element_type=jnp.float32)
    queries = head_norm(flat[:, :width], gain_query)
    key_rows = head_norm(flat[:, width:2 * width], gain_key)
    value_rows = flat[:, 2 * width:].astype(jnp.bfloat16)
    return (queries, key_rows, value_rows)

def attend(queries, key_rows, value_rows, key_mask):
    count, width = queries.shape
    nheads = width // HEAD_DIM
    block_size = math.gcd(count, 512)
    blocks = queries.reshape(count // block_size, block_size, nheads, HEAD_DIM)
    keys_wide = key_rows.reshape(-1, nheads, HEAD_DIM).astype(jnp.float32)
    values_wide = value_rows.reshape(-1, nheads, HEAD_DIM).astype(jnp.float32)

    def one_block(block):
        scores = jnp.einsum('qhd,khd->hqk', block.astype(jnp.float32), keys_wide) * HEAD_DIM ** (-0.5)
        expo = jnp.exp(scores) * key_mask[None, None, :]
        weights = lax.optimization_barrier(expo.astype(jnp.bfloat16)).astype(jnp.float32)
        numer = jnp.einsum('hqk,khd->qhd', weights, values_wide)
        denom = lax.optimization_barrier(jnp.sum(expo, axis=2)).T
        return (numer / denom[:, :, None]).astype(jnp.bfloat16)
    return lax.map(one_block, blocks).reshape(count, width)

def reference(x_video, x_text, w_qkv_video, w_qkv_text, w_out_video, w_out_text, qk_gains, modulation, text_len, timestep):
    mods = modulation[timestep[0]]
    normed_video = norm_modulate(x_video, mods[0], mods[1])
    normed_text = norm_modulate(x_text, mods[3], mods[4])
    q_video, k_video, v_video = project(normed_video, w_qkv_video, qk_gains[0], qk_gains[1])
    q_text, k_text, v_text = project(normed_text, w_qkv_text, qk_gains[2], qk_gains[3])
    text_valid = jnp.arange(TXT, dtype=jnp.int32) < text_len[0]
    key_mask = jnp.concatenate([text_valid.astype(jnp.float32), jnp.ones((TV,), jnp.float32)])
    joint_keys = jnp.concatenate([k_text, k_video], axis=0)
    joint_values = jnp.concatenate([v_text, v_video], axis=0)
    attn_video = attend(q_video, joint_keys, joint_values, key_mask)
    attn_text = attend(q_text, joint_keys, joint_values, key_mask)
    video_out = (mods[2] * jnp.dot(attn_video, w_out_video, preferred_element_type=jnp.float32)).astype(jnp.bfloat16)
    text_full = mods[5] * jnp.dot(attn_text, w_out_text, preferred_element_type=jnp.float32)
    text_out = jnp.where(text_valid[:, None], text_full, 0.0).astype(jnp.bfloat16)
    return (video_out, text_out)
```

```python
import functools
import math

import jax
import jax.numpy as jnp
from jax import lax
from jax.experimental import pallas as pl
from jax.experimental.pallas import tpu as pltpu
from jax.sharding import Mesh, PartitionSpec as P

AXES = ("x", "y", "zh", "zl", "c")
MESH = pl.DeviceIdType.MESH
BF16, F32 = jnp.bfloat16, jnp.float32
D = 3072
HD = 128
NH = 3
W = NH * HD
BLK = 512
TXT = 256
TQ = 32
OWN = BLK + TQ
QROWS = 4 * BLK + TQ
EXP_SCALE = math.log2(math.e) / math.sqrt(HD)
VMEM_LIMIT = 60 << 20


def coords():
    x, y, zh, zl, c = (lax.axis_index(a) for a in AXES)
    return x, y, zh * 2 + zl, c


def dev(x, y, z, c):
    z = lax.rem(z + 4, 4)
    return (lax.rem(x + 4, 4), lax.rem(y + 4, 4), z // 2, lax.rem(z, 2), c)


class Sends:
    def __init__(self, sems, peer):
        self.sems, self.peer, self.count, self.pending = sems, peer, 0, []

    def start(self, src, dst, recv_sem, device, pred=None):
        slot = self.count
        self.count += 1
        get = src if callable(src) else (lambda: src)

        pltpu.make_async_remote_copy(
            src_ref=get(), dst_ref=dst, send_sem=self.sems.at[slot], recv_sem=recv_sem,
            device_id=device, device_id_type=MESH).start()

        def wait():
            pltpu.make_async_remote_copy(
                src_ref=get(), dst_ref=get(), send_sem=self.sems.at[slot], recv_sem=self.sems.at[slot],
                device_id=self.peer, device_id_type=MESH).wait_send()

        self.pending.append((pred, wait))

    def finish(self):
        for pred, wait in self.pending:
            if pred is None:
                wait()
            else:
                pl.when(pred)(wait)


def signal(sem, device):
    pl.semaphore_signal(sem, inc=1, device_id=device, device_id_type=MESH)


def norm_rows(src, dst, dst_row, count, shift, scale1):
    def strip(i, carry):
        wide = src[pl.ds(pl.multiple_of(i * 16, 16), 16), :].astype(F32)
        centred = wide - jnp.mean(wide, axis=-1, keepdims=True)
        variance = jnp.mean(centred * centred, axis=-1, keepdims=True)
        out = centred * lax.rsqrt(variance + 1e-06) * scale1 + shift
        dst[pl.ds(pl.multiple_of(dst_row + i * 16, 16), 16), :] = out.astype(BF16)
        return carry

    lax.fori_loop(0, count // 16, strip, 0, unroll=2)


def project(rows, weight, out, out_row, gain_query, gain_key):
    flat = jnp.dot(rows, weight[...], preferred_element_type=F32)
    count = rows.shape[0]
    for part in range(3):
        for h in range(NH):
            u = flat[:, part * W + h * HD : part * W + (h + 1) * HD]
            if part < 2:
                gain = gain_query if part == 0 else gain_key
                meansq = jnp.mean(u * u, axis=-1, keepdims=True)
                u = u * lax.rsqrt(meansq + 1e-06) * gain
            out[part, out_row : out_row + count, h * HD : (h + 1) * HD] = u.astype(BF16)


def qkv_kernel(x_ref, xt_ref, wv_ref, wt_ref, mod_ref, gains_ref, wov_ref, wot_ref, step_ref,
               qkv_ref, tqkv_ref, wsv_ref, wst_ref,
               xb, xtb, wvb, wtb, modb, nb, load_sem, send_sem, x_sem, w_sem):
    x, y, z, c = coords()
    zh = z // 2
    role = lax.rem(c + zh, 2)
    sibling = dev(x, y, z, 1 - c)
    toward = z + 2 * c - 1
    loads = [
        pltpu.make_async_copy(x_ref, xb.at[c], load_sem.at[0]),
        pltpu.make_async_copy(mod_ref, modb, load_sem.at[1]),
        pltpu.make_async_copy(xt_ref, xtb, load_sem.at[2]),
    ]
    for part in range(3):
        loads.append(pltpu.make_async_copy(
            wt_ref.at[part], wtb.at[:, part * W : (part + 1) * W], load_sem.at[3 + part]))
    for part in range(3):
        loads.append(pltpu.make_async_copy(
            wv_ref.at[part], wvb.at[:, part * W : (part + 1) * W], load_sem.at[6 + part]))
    for copy in loads:
        copy.start()

    barrier = pltpu.get_barrier_semaphore()
    signal(barrier, sibling)
    signal(barrier, dev(x, y, z + 1, 0))
    signal(barrier, dev(x, y, z - 1, 1))
    pl.semaphore_wait(barrier, 3)

    sends = Sends(send_sem, sibling)
    for half in range(2):
        rows = pl.ds(half * 64, 64)
        sends.start(x_ref.at[rows], xb.at[2 + c, rows], x_sem.at[1 + c], dev(x, y, toward, half))
    sends.start(x_ref, xb.at[c], x_sem.at[0], sibling)
    sends.start(wov_ref, wsv_ref, w_sem.at[0], sibling)
    sends.start(wot_ref, wst_ref, w_sem.at[1], sibling)

    def arrived(dst, sem):
        pltpu.make_async_remote_copy(
            src_ref=dst, dst_ref=dst, send_sem=send_sem.at[0], recv_sem=sem,
            device_id=sibling, device_id_type=MESH).wait_recv()

    step = step_ref[0]
    loads[1].wait()
    loads[2].wait()
    for part in range(3):
        loads[3 + part].wait()

    @pl.when(role == 0)
    def _():
        norm_rows(xtb, nb, 0, TXT, modb[3, pl.ds(step, 1), :], 1.0 + modb[4, pl.ds(step, 1), :])
        project(nb[0:TXT, :], wtb, tqkv_ref, 0, gains_ref[2:3, :], gains_ref[3:4, :])

    shift, scale1 = modb[0, pl.ds(step, 1), :], 1.0 + modb[1, pl.ds(step, 1), :]
    loads[0].wait()
    arrived(xb.at[1 - c], x_sem.at[0])
    norm_rows(xb.at[0], nb, 0, 128, shift, scale1)
    norm_rows(xb.at[1], nb, 128, 128, shift, scale1)
    for part in range(3):
        loads[6 + part].wait()
    project(nb[0:256, :], wvb, qkv_ref, 0, gains_ref[0:1, :], gains_ref[1:2, :])

    mine = pl.ds(pl.multiple_of(c * 64, 64), 64)
    other = pl.ds(pl.multiple_of((1 - c) * 64, 64), 64)
    for slot in (2, 3):
        arrived(xb.at[slot, mine], x_sem.at[slot - 1])
        sends.start(xb.at[slot, mine], xb.at[slot, mine], x_sem.at[slot + 1], sibling)
    for slot in (2, 3):
        arrived(xb.at[slot, other], x_sem.at[slot + 1])
        norm_rows(xb.at[slot], nb, 128 * slot, 128, shift, scale1)
    project(nb[256:512, :], wvb, qkv_ref, 256, gains_ref[0:1, :], gains_ref[1:2, :])
    arrived(wsv_ref, w_sem.at[0])
    arrived(wst_ref, w_sem.at[1])
    sends.finish()


def attend(qb, q0, count, keys, values, acc, first, mask=None):
    for h in range(NH):
        lanes = slice(h * HD, (h + 1) * HD)
        query = qb[pl.ds(q0, count), lanes]
        total = None
        for key_ref, value_ref in zip(keys, values):
            scores = lax.dot_general(
                query, key_ref[:, lanes], (((1,), (1,)), ((), ())), preferred_element_type=F32)
            expo = jnp.exp2(scores * EXP_SCALE)
            if mask is not None:
                expo = jnp.where(mask, expo, 0.0)
            value = value_ref[:, lanes]
            wide = jnp.concatenate([value, jnp.ones_like(value)], axis=1)
            part = jnp.dot(expo.astype(BF16), wide, preferred_element_type=F32)
            total = part if total is None else total + part
        if first:
            acc[h, pl.ds(q0, count), :] = total
        else:
            acc[h, pl.ds(q0, count), :] += total


def coded_denoms(acc, rows):
    parts = [acc[h, rows, HD:] for h in range(NH)]
    lane = lax.broadcasted_iota(jnp.int32, parts[0].shape, 1)
    return jnp.where(lane < 8, parts[0], jnp.where(lane < 16, parts[1], parts[2]))


def attention_kernel(qkv_ref, tqkv_ref, len_ref, attn_ref, text_ref,
                     qb, kvb, tkv, acc, osend, dsend, orecv, drecv, tsend, trecv, afin, tfin,
                     send_sem, kv_sem, q_sem, t_sem, o_sem, tr_sem, out_sem):
    x, y, z, c = coords()
    zh = z // 2
    zl = lax.rem(z, 2)
    role = lax.rem(c + zh, 2)
    is0, is1 = role == 0, role == 1
    sibling = dev(x, y, z, 1 - c)
    xp, xm = dev(x + 1, y, z, c), dev(x - 1, y, z, c)
    yps = {1: dev(x, y + 1, z, c), 2: dev(x, y - 1, z, c), 3: dev(x, y + 2, z, c)}
    owner = role == y // 2
    owner_self = jnp.logical_and(owner, lax.rem(x, 2) == c)

    barrier = pltpu.get_barrier_semaphore()
    for device in (sibling, xp, xm, yps[1], yps[2], yps[3], dev(x, y, z + 2, zh)):
        signal(barrier, device)

    @pl.when(is1)
    def _():
        signal(barrier, dev(x, y, z + 2, 1 - zh))

    for xi in range(2):
        for sy in range(4):
            for sz in range(2):
                source_core = (sz + sy // 2) % 2
                sx = c + 2 * xi
                same = jnp.logical_and(
                    jnp.logical_and(sx == x, sy == y), jnp.logical_and(sz == zh, source_core == c))

                @pl.when(jnp.logical_not(same))
                def _():
                    signal(barrier, (sx, sy, sz, zl, source_core))

    pl.semaphore_wait(
        barrier, 7 + role + jnp.where(owner, 32, 0) - jnp.where(owner_self, 1, 0))

    sends = Sends(send_sem, sibling)

    def arrived(dst, sem):
        pltpu.make_async_remote_copy(
            src_ref=dst, dst_ref=dst, send_sem=send_sem.at[0], recv_sem=sem,
            device_id=sibling, device_id_type=MESH).wait_recv()

    q_own = qb.at[pl.ds(0, BLK)]
    tq_own = qb.at[pl.ds(BLK, TQ)]

    def q_slot(pos):
        return qb.at[pl.ds(OWN + (pos - 1) * BLK, BLK)]

    tq_row = pl.multiple_of(64 * x, 64)
    tq_other = tqkv_ref.at[0, pl.ds(pl.multiple_of(64 * x + TQ, TQ), TQ)]
    tkv_src = tqkv_ref.at[pl.ds(1, 2)]
    kv_src = qkv_ref.at[pl.ds(1, 2)]
    q_src = qkv_ref.at[0]
    partner = dev(x, y, z + 2, 1 - c)
    local = [
        (q_src, q_own, q_sem.at[0]),
        (kv_src, kvb.at[0, 0], kv_sem.at[0, 0, 0]),
        (tqkv_ref.at[0, pl.ds(tq_row, TQ)], tq_own, t_sem.at[0]),
        (tkv_src, tkv, t_sem.at[1]),
    ]

    def send_queries(pred):
        for pos, back in ((1, 2), (2, 1), (3, 3)):
            sends.start(q_own, q_slot(back), q_sem.at[back], yps[pos], pred)

    def send_own(r, pred):
        def block():
            return kvb.at[r, 0]

        sends.start(block, kvb.at[r, 2], kv_sem.at[r, 2, 0], xp, pred)
        sends.start(block, kvb.at[r, 1], kv_sem.at[r, 1, 0], xm, pred)
        sends.start(block, block(), kv_sem.at[r, 0, 0], sibling, pred)

    def pass_on(r, pred):
        arrived(kvb.at[r, 1], kv_sem.at[r, 1, 0])
        sends.start(lambda: kvb.at[r, 1, 0], kvb.at[r, 3, 0], kv_sem.at[r, 3, 0], xm, pred)
        arrived(kvb.at[r, 2], kv_sem.at[r, 2, 0])
        sends.start(lambda: kvb.at[r, 2, 1], kvb.at[r, 3, 1], kv_sem.at[r, 3, 1], xp, pred)
        for pos in (1, 2):
            sends.start(lambda pos=pos: kvb.at[r, pos], kvb.at[r, pos], kv_sem.at[r, pos, 0], sibling, pred)

    def pass_last(r, pred):
        for part in range(2):
            arrived(kvb.at[r, 3, part], kv_sem.at[r, 3, part])
        sends.start(lambda: kvb.at[r, 3], kvb.at[r, 3], kv_sem.at[r, 3, 0], sibling, pred)

    @pl.when(is0)
    def _():
        for src, dst, sem in local:
            pltpu.make_async_copy(src, dst, sem).start()
        sends.start(tq_other, tq_own, t_sem.at[0], sibling, is0)
        sends.start(tkv_src, tkv, t_sem.at[1], sibling, is0)
        for src, dst, sem in local:
            pltpu.make_async_copy(src, dst, sem).wait()
        send_own(0, is0)
        send_queries(is0)

    @pl.when(is1)
    def _():
        sends.start(q_src, q_own, q_sem.at[0], partner, is1)
        sends.start(kv_src, kvb.at[1, 0], kv_sem.at[1, 0, 0], partner, is1)
        arrived(q_own, q_sem.at[0])
        send_queries(is1)
        arrived(tq_own, t_sem.at[0])
        arrived(tkv, t_sem.at[1])

    shape = (OWN, TXT)
    row = lax.broadcasted_iota(jnp.int32, shape, 0)
    col = lax.broadcasted_iota(jnp.int32, shape, 1)
    row_limit = jnp.where(y == 0, OWN, BLK)
    mask = jnp.logical_and(col < len_ref[0], row < row_limit)
    attend(qb, 0, OWN, [tkv.at[0]], [tkv.at[1]], acc, True, mask)

    @pl.when(is1)
    def _():
        arrived(kvb.at[0, 0], kv_sem.at[0, 0, 0])

    attend(qb, 0, OWN, [kvb.at[0, 0, 0]], [kvb.at[0, 0, 1]], acc, False)

    @pl.when(is1)
    def _():
        arrived(kvb.at[1, 0], kv_sem.at[1, 0, 0])
        send_own(1, is1)

    arrived(q_slot(1), q_sem.at[1])
    arrived(q_slot(2), q_sem.at[2])
    attend(qb, OWN, 2 * BLK, [kvb.at[0, 0, 0]], [kvb.at[0, 0, 1]], acc, True)

    @pl.when(is0)
    def _():
        pass_on(0, is0)

    arrived(q_slot(3), q_sem.at[3])
    attend(qb, OWN + 2 * BLK, BLK, [kvb.at[0, 0, 0]], [kvb.at[0, 0, 1]], acc, True)

    def middle(n, carry):
        block = 1 + n // 2
        r, pos = block // 4, lax.rem(block, 4)
        half = lax.rem(n, 2)

        for when, want in ((0, 1), (2, 2), (4, 3)):
            @pl.when(jnp.logical_and(n == when, is1))
            def _(want=want):
                arrived(kvb.at[0, want], kv_sem.at[0, want, 0])

        @pl.when(jnp.logical_and(n == 2, is0))
        def _():
            pass_last(0, is0)

        @pl.when(jnp.logical_and(n == 2, is1))
        def _():
            pass_on(1, is1)

        @pl.when(jnp.logical_and(n == 6, is1))
        def _():
            pass_last(1, is1)

        @pl.when(jnp.logical_and(n == 6, is0))
        def _():
            arrived(kvb.at[1, 0], kv_sem.at[1, 0, 0])

        q0 = pl.multiple_of(half * (QROWS // 2), 16)
        attend(qb, q0, QROWS // 2, [kvb.at[r, pos, 0]], [kvb.at[r, pos, 1]], acc, False)
        return carry

    lax.fori_loop(0, 8, middle, 0)

    @pl.when(is0)
    def _():
        for pos in (1, 2, 3):
            arrived(kvb.at[1, pos], kv_sem.at[1, pos, 0])

    last_keys = [kvb.at[1, pos, 0] for pos in (1, 2, 3)]
    last_values = [kvb.at[1, pos, 1] for pos in (1, 2, 3)]
    for pos, back in ((3, 3), (1, 2), (2, 1)):
        q0 = OWN + (pos - 1) * BLK
        rows = pl.ds(q0, BLK)
        attend(qb, q0, BLK, last_keys, last_values, acc, False)
        for h in range(NH):
            osend[pos - 1, :, h * HD : (h + 1) * HD] = acc[h, rows, :HD].astype(BF16)
        dsend[pos - 1] = jnp.transpose(coded_denoms(acc, rows))[:24]
        sends.start(osend.at[pos - 1], orecv.at[back - 1], o_sem.at[back - 1, 0], yps[pos])
        sends.start(dsend.at[pos - 1], drecv.at[back - 1], o_sem.at[back - 1, 1], yps[pos])
    attend(qb, 0, OWN, last_keys, last_values, acc, False)

    for p in range(2):
        rows = pl.ds(BLK + 16 * p, 16)
        target = 2 * role + p
        for h in range(NH):
            tsend[p, :, h * HD : (h + 1) * HD] = acc[h, rows, :HD]
        tsend[p, :, W:] = coded_denoms(acc, rows)

        elsewhere = target != y

        @pl.when(elsewhere)
        def _():
            sends.start(lambda p=p: tsend.at[p], trecv.at[y], tr_sem.at[y], dev(x, target, z, c), elsewhere)

    core = lax.rem(x, 2)
    to_sibling = jnp.logical_and(owner, core != c)

    @pl.when(owner)
    def _():
        for sy in range(4):
            @pl.when(sy != y)
            def _():
                arrived(trecv.at[sy], tr_sem.at[sy])

        total = tsend[y - 2 * role]
        for sy in range(4):
            total = total + jnp.where(sy != y, trecv[sy], 0.0)
        for h in range(NH):
            denom = total[:, W + 8 * h : W + 8 * h + 1]
            tfin[:, h * HD : (h + 1) * HD] = (total[:, h * HD : (h + 1) * HD] / denom).astype(BF16)
        trow = pl.multiple_of(lax.rem(x // 2, 2) * 64 + 16 * y, 16)
        tcol = pl.multiple_of(zh * W, HD)
        place = text_ref.at[pl.ds(trow, 16), pl.ds(tcol, W)]
        for dx in range(4):
            for dy in range(4):
                for dz in range(2):
                    if dx + dy + dz == 0:
                        continue
                    sends.start(tfin, place, out_sem.at[1], dev(x + dx, y + dy, z + 2 * dz, core), owner)

        @pl.when(core == c)
        def _():
            pltpu.make_async_copy(tfin, place, out_sem.at[1]).start()

        @pl.when(core != c)
        def _():
            sends.start(tfin, place, out_sem.at[1], sibling, to_sibling)

    for pos in (3, 1, 2):
        arrived(orecv.at[pos - 1], o_sem.at[pos - 1, 0])
        arrived(drecv.at[pos - 1], o_sem.at[pos - 1, 1])
    denoms = drecv[0] + drecv[1] + drecv[2]
    for h in range(NH):
        lanes = slice(h * HD, (h + 1) * HD)
        numer = acc[h, 0:BLK, :HD]
        for pos in range(3):
            numer = numer + orecv[pos, :, lanes].astype(F32)
        denom = acc[h, 0:BLK, HD:] + jnp.transpose(
            jnp.broadcast_to(denoms[8 * h : 8 * h + 1, :], (HD, BLK)))
        afin[:, lanes] = (numer / denom).astype(BF16)

    acol = pl.ds(pl.multiple_of(zh * W, HD), W)
    for core in range(2):
        for slot in range(2):
            src = afin.at[pl.ds((2 * slot + core) * 128, 128)]
            dst = attn_ref.at[slot, :, acol]
            across = jnp.logical_and(is0, c != core)

            @pl.when(is1)
            def _():
                sends.start(src, dst, out_sem.at[0], dev(x, y, z + 2, core), is1)

            @pl.when(jnp.logical_and(is0, c == core))
            def _():
                pltpu.make_async_copy(src, dst, out_sem.at[0]).start()

            @pl.when(across)
            def _():
                sends.start(src, dst, out_sem.at[0], sibling, across)

    arrived(text_ref, out_sem.at[1])
    arrived(attn_ref, out_sem.at[0])
    sends.finish()


CH = 768
NCH = D // CH


def output_kernel(attn_ref, text_ref, wv_ref, wsv_ref, wt_ref, wst_ref, mod_ref, len_ref, step_ref,
                  video_out_ref, text_out_ref,
                  wvb, wtb, modb, fsend, frecv, tsend, trecv, load_sem, send_sem, recv_sem):
    x, y, z, c = coords()
    zl = lax.rem(z, 2)
    ours = pl.ds(pl.multiple_of(c * W, 16), W)
    theirs = pl.ds(pl.multiple_of((1 - c) * W, 16), W)
    loads = [
        pltpu.make_async_copy(wv_ref, wvb.at[ours], load_sem.at[0]),
        pltpu.make_async_copy(wsv_ref, wvb.at[theirs], load_sem.at[1]),
        pltpu.make_async_copy(wt_ref, wtb.at[ours], load_sem.at[2]),
        pltpu.make_async_copy(wst_ref, wtb.at[theirs], load_sem.at[3]),
        pltpu.make_async_copy(mod_ref.at[2], modb.at[0], load_sem.at[4]),
        pltpu.make_async_copy(mod_ref.at[5], modb.at[1], load_sem.at[5]),
    ]
    for copy in loads:
        copy.start()
    toward = 1 - 2 * c
    target = dev(x, y, z + toward, c)
    barrier = pltpu.get_barrier_semaphore()
    signal(barrier, dev(x, y, z - toward, c))
    pl.semaphore_wait(barrier, 1)
    sends = Sends(send_sem, target)
    loads[0].wait()
    loads[1].wait()
    for i in range(NCH):
        cols = slice(i * CH, (i + 1) * CH)
        fsend[i] = jnp.dot(attn_ref[1], wvb[:, cols], preferred_element_type=F32).astype(BF16)
        sends.start(fsend.at[i], frecv.at[i], recv_sem.at[0, i], target)
    loads[2].wait()
    loads[3].wait()
    own_row = pl.multiple_of(zl * 64, 64)
    far_row = pl.multiple_of((1 - zl) * 64, 64)
    for i in range(NCH):
        cols = slice(i * CH, (i + 1) * CH)
        tsend[i] = jnp.dot(
            text_ref[pl.ds(far_row, 64), :], wtb[:, cols], preferred_element_type=F32).astype(BF16)
        sends.start(tsend.at[i], trecv.at[i], recv_sem.at[1, i], target)
    loads[4].wait()
    loads[5].wait()
    step = step_ref[0]

    def arrived(dst, sem):
        pltpu.make_async_remote_copy(
            src_ref=dst, dst_ref=dst, send_sem=send_sem.at[0], recv_sem=sem,
            device_id=target, device_id_type=MESH).wait_recv()

    for i in range(NCH):
        cols = slice(i * CH, (i + 1) * CH)
        own = jnp.dot(attn_ref[0], wvb[:, cols], preferred_element_type=F32)
        arrived(frecv.at[i], recv_sem.at[0, i])
        gate = modb[0, pl.ds(step, 1), cols]
        video_out_ref[:, cols] = (gate * (own + frecv[i].astype(F32))).astype(BF16)
    row = lax.broadcasted_iota(jnp.int32, (64, CH), 0) + (zl * 2 + c) * 64
    valid = row < len_ref[0]
    for i in range(NCH):
        cols = slice(i * CH, (i + 1) * CH)
        own = jnp.dot(text_ref[pl.ds(own_row, 64), :], wtb[:, cols], preferred_element_type=F32)
        arrived(trecv.at[i], recv_sem.at[1, i])
        gate = modb[1, pl.ds(step, 1), cols]
        text_out_ref[:, cols] = jnp.where(
            valid, gate * (own + trecv[i].astype(F32)), 0.0).astype(BF16)
    sends.finish()


ANY = pl.BlockSpec(memory_space=pl.ANY)
VMEM = pl.BlockSpec(memory_space=pltpu.VMEM)
SMEM = pl.BlockSpec(memory_space=pltpu.SMEM)
DMA = pltpu.SemaphoreType.DMA


def params(ident):
    return pltpu.CompilerParams(
        collective_id=ident, has_side_effects=True, vmem_limit_bytes=VMEM_LIMIT)


def body(x_video, x_text, w_qkv_video, w_qkv_text, w_out_video, w_out_text, qk_gains, modulation,
         text_len, timestep):
    wv = jnp.transpose(w_qkv_video, (1, 0, 2))
    wt = jnp.transpose(w_qkv_text, (1, 0, 2))
    mod = jnp.transpose(modulation, (1, 0, 2))
    shape = jax.ShapeDtypeStruct
    steps = modulation.shape[0]
    qkv, tqkv, wsv, wst = pl.pallas_call(
        qkv_kernel,
        name="qkv",
        in_specs=[ANY, ANY, ANY, ANY, ANY, VMEM, ANY, ANY, SMEM],
        out_specs=[VMEM, VMEM, ANY, ANY],
        out_shape=[shape((3, BLK, W), BF16), shape((3, TXT, W), BF16),
                   shape((W, D), BF16), shape((W, D), BF16)],
        scratch_shapes=[
            pltpu.VMEM((4, 128, D), BF16), pltpu.VMEM((TXT, D), BF16),
            pltpu.VMEM((D, 3 * W), BF16), pltpu.VMEM((D, 3 * W), BF16),
            pltpu.VMEM((6, steps, D), F32), pltpu.VMEM((BLK, D), BF16),
            DMA((9,)), DMA((8,)), DMA((5,)), DMA((2,))],
        compiler_params=params(1),
    )(x_video, x_text, wv, wt, mod, qk_gains, w_out_video, w_out_text, timestep)
    attn, text = pl.pallas_call(
        attention_kernel,
        name="attention",
        in_specs=[ANY, ANY, SMEM],
        out_specs=[ANY, ANY],
        out_shape=[shape((2, 128, 2 * W), BF16), shape((128, 2 * W), BF16)],
        scratch_shapes=[
            pltpu.VMEM((QROWS, W), BF16), pltpu.VMEM((2, 4, 2, BLK, W), BF16),
            pltpu.VMEM((2, TXT, W), BF16), pltpu.VMEM((NH, QROWS, 2 * HD), F32),
            pltpu.VMEM((3, BLK, W), BF16), pltpu.VMEM((3, 24, BLK), F32),
            pltpu.VMEM((3, BLK, W), BF16), pltpu.VMEM((3, 24, BLK), F32),
            pltpu.VMEM((2, 16, W + HD), F32), pltpu.VMEM((4, 16, W + HD), F32),
            pltpu.VMEM((BLK, W), BF16), pltpu.VMEM((16, W), BF16),
            DMA((80,)), DMA((2, 4, 2)), DMA((4,)), DMA((2,)), DMA((3, 2)), DMA((4,)), DMA((2,))],
        compiler_params=params(2),
    )(qkv, tqkv, text_len)
    return tuple(pl.pallas_call(
        output_kernel,
        name="output",
        in_specs=[VMEM, VMEM, ANY, ANY, ANY, ANY, ANY, SMEM, SMEM],
        out_specs=[VMEM, VMEM],
        out_shape=[shape((128, D), BF16), shape((64, D), BF16)],
        scratch_shapes=[
            pltpu.VMEM((2 * W, D), BF16), pltpu.VMEM((2 * W, D), BF16),
            pltpu.VMEM((2, steps, D), F32),
            pltpu.VMEM((NCH, 128, CH), BF16), pltpu.VMEM((NCH, 128, CH), BF16),
            pltpu.VMEM((NCH, 64, CH), BF16), pltpu.VMEM((NCH, 64, CH), BF16),
            DMA((6,)), DMA((2 * NCH,)), DMA((2, NCH))],
        compiler_params=params(3),
    )(attn, text, w_out_video, wsv, w_out_text, wst, mod, text_len, timestep))


def solution(mesh):
    grid = Mesh(mesh.devices.reshape(4, 4, 2, 2, 2), AXES)
    head = ("zl", "c")
    return jax.shard_map(
        body,
        mesh=grid,
        in_specs=(P(AXES, None), P(), P(None, None, head), P(None, None, head),
                  P(head, None), P(head, None), P(), P(), P(), P()),
        out_specs=(P(AXES, None), P(head, None)),
        check_vma=False,
    )
```

```python
import functools
import math

import jax
import jax.numpy as jnp
from jax import lax
from jax.experimental import pallas as pl
from jax.experimental.pallas import tpu as pltpu
from jax.sharding import Mesh, PartitionSpec as P

AXES = ("x", "y", "zh", "zl", "c")
MESH = pl.DeviceIdType.MESH
BF16, F32 = jnp.bfloat16, jnp.float32
D = 3072
HD = 128
NH = 3
W = NH * HD
HALF = 256
TXT = 256
TQ = 32
QROWS = 8 * HALF + TQ
ORDER = (3, 1, 2, 0)
CH = 768
NCH = D // CH
EXP_SCALE = math.log2(math.e) / math.sqrt(HD)
VMEM_LIMIT = 60 << 20


def coords():
    x, y, zh, zl, c = (lax.axis_index(a) for a in AXES)
    return x, y, zh * 2 + zl, c


def dev(x, y, z, c):
    z = lax.rem(z + 4, 4)
    return (lax.rem(x + 4, 4), lax.rem(y + 4, 4), z // 2, lax.rem(z, 2), c)


class Sends:
    def __init__(self, sems, peer):
        self.sems, self.peer, self.count, self.pending = sems, peer, 0, []

    def start(self, src, dst, recv_sem, device, pred=None):
        slot = self.count
        self.count += 1
        get = src if callable(src) else (lambda: src)

        pltpu.make_async_remote_copy(
            src_ref=get(), dst_ref=dst, send_sem=self.sems.at[slot], recv_sem=recv_sem,
            device_id=device, device_id_type=MESH).start()

        def wait():
            pltpu.make_async_remote_copy(
                src_ref=get(), dst_ref=get(), send_sem=self.sems.at[slot], recv_sem=self.sems.at[slot],
                device_id=self.peer, device_id_type=MESH).wait_send()

        self.pending.append((pred, wait))

    def finish(self):
        for pred, wait in self.pending:
            if pred is None:
                wait()
            else:
                pl.when(pred)(wait)


def signal(sem, device):
    pl.semaphore_signal(sem, inc=1, device_id=device, device_id_type=MESH)


def norm_rows(src, dst, dst_row, count, shift, scale1):
    def strip(i, carry):
        wide = src[pl.ds(pl.multiple_of(i * 16, 16), 16), :].astype(F32)
        centred = wide - jnp.mean(wide, axis=-1, keepdims=True)
        variance = jnp.mean(centred * centred, axis=-1, keepdims=True)
        out = centred * lax.rsqrt(variance + 1e-06) * scale1 + shift
        dst[pl.ds(pl.multiple_of(dst_row + i * 16, 16), 16), :] = out.astype(BF16)
        return carry

    lax.fori_loop(0, count // 16, strip, 0, unroll=2)


def project(rows, weights, outs, gain_query, gain_key):
    for part in range(3):
        flat = jnp.dot(rows, weights[part][...], preferred_element_type=F32)
        for h in range(NH):
            lanes = slice(h * HD, (h + 1) * HD)
            u = flat[:, lanes]
            if part < 2:
                gain = gain_query if part == 0 else gain_key
                meansq = jnp.mean(u * u, axis=-1, keepdims=True)
                u = u * lax.rsqrt(meansq + 1e-06) * gain
            outs[part][:, lanes] = u.astype(BF16)


def project_wide(rows, weight, out, gain_query, gain_key):
    flat = jnp.dot(rows, weight[...], preferred_element_type=F32)
    for part in range(3):
        for h in range(NH):
            u = flat[:, part * W + h * HD : part * W + (h + 1) * HD]
            if part < 2:
                gain = gain_query if part == 0 else gain_key
                meansq = jnp.mean(u * u, axis=-1, keepdims=True)
                u = u * lax.rsqrt(meansq + 1e-06) * gain
            out[part, :, h * HD : (h + 1) * HD] = u.astype(BF16)


def attend(qb, q0, count, keys, values, acc, first, mask=None):
    for h in range(NH):
        lanes = slice(h * HD, (h + 1) * HD)
        query = qb[pl.ds(q0, count), lanes]
        total = None
        for key_ref, value_ref in zip(keys, values):
            scores = lax.dot_general(
                query, key_ref[:, lanes], (((1,), (1,)), ((), ())), preferred_element_type=F32)
            expo = jnp.exp2(scores * EXP_SCALE)
            if mask is not None:
                expo = jnp.where(mask, expo, 0.0)
            value = value_ref[:, lanes]
            wide = jnp.concatenate([value, jnp.ones_like(value)], axis=1)
            part = jnp.dot(expo.astype(BF16), wide, preferred_element_type=F32)
            total = part if total is None else total + part
        if first:
            acc[h, pl.ds(q0, count), :] = total
        else:
            acc[h, pl.ds(q0, count), :] += total


def coded_denoms(acc, rows):
    parts = [acc[h, rows, HD:] for h in range(NH)]
    lane = lax.broadcasted_iota(jnp.int32, parts[0].shape, 1)
    return jnp.where(lane < 8, parts[0], jnp.where(lane < 16, parts[1], parts[2]))


def q_row(pos, half):
    return TQ + ORDER.index(pos) * HALF + (0 if half else 4 * HALF)


TROW = 0


def block_kernel(x_ref, xt_ref, wv_ref, wt_ref, mod_ref, gains_ref, wov_ref, wot_ref, len_ref, step_ref,
                 video_out_ref, text_out_ref, wst_ref,
                 xb, xtb, wvb, wtb, mod0, mod1, mod2, nb, stg, tqst, qb, kvb, tkv, acc, osend, dsend, orecv, drecv,
                 tsend, trecv, afin, tfin, attn, text, wob, fsend, frecv, gsend, grecv,
                 load_sem, send_sem, x_sem, w_sem, own_sem, kv_sem, q_sem, t_sem, o_sem, tr_sem,
                 attn_sem, text_sem, out_sem):
    x, y, z, c = coords()
    zh, zl = z // 2, lax.rem(z, 2)
    role = lax.rem(c + zh, 2)
    is0, is1 = role == 0, role == 1
    sibling = dev(x, y, z, 1 - c)
    partner = dev(x, y, z + 2, 1 - c)
    xp, xm = dev(x + 1, y, z, c), dev(x - 1, y, z, c)
    yps = {1: dev(x, y + 1, z, c), 2: dev(x, y - 1, z, c), 3: dev(x, y + 2, z, c)}
    zp, zm = dev(x, y, z + 1, c), dev(x, y, z - 1, c)
    owner = role == y // 2

    load_x = pltpu.make_async_copy(x_ref, xb.at[c], load_sem.at[0])
    load_mod = [
        pltpu.make_async_copy(mod_ref.at[pl.ds(2 * i, 2)], part, load_sem.at[1 + i])
        for i, part in enumerate((mod0, mod1, mod2))]
    load_wv = [
        pltpu.make_async_copy(wv_ref.at[part], wvb.at[:, part * W : (part + 1) * W], load_sem.at[4 + part])
        for part in range(3)]
    load_xt = pltpu.make_async_copy(xt_ref, xtb, load_sem.at[7])
    load_wt = [
        pltpu.make_async_copy(wt_ref.at[part], wtb.at[pl.ds(part * D, D)], load_sem.at[8 + part])
        for part in range(3)]
    for copy in [load_x, load_mod[0]] + load_wv:
        copy.start()

    @pl.when(is0)
    def _():
        for copy in [load_xt] + load_wt:
            copy.start()

    load_mod[1].start()
    load_mod[2].start()

    barrier = pltpu.get_barrier_semaphore()
    for device in (sibling, xp, xm, yps[1], yps[2], yps[3], zp, zm, dev(x, y, z + 2, zh)):
        signal(barrier, device)

    @pl.when(is1)
    def _():
        signal(barrier, dev(x, y, z + 2, 1 - zh))

    step = step_ref[0]
    load_x.wait()
    load_mod[0].wait()
    shift, scale1 = mod0[0, pl.ds(step, 1), :], 1.0 + mod0[1, pl.ds(step, 1), :]
    norm_rows(xb.at[c], nb, 128 * c, 128, shift, scale1)
    pl.semaphore_wait(barrier, 9 + role)

    sends = Sends(send_sem, sibling)

    def arrived(dst, sem):
        pltpu.make_async_remote_copy(
            src_ref=dst, dst_ref=dst, send_sem=send_sem.at[0], recv_sem=sem,
            device_id=sibling, device_id_type=MESH).wait_recv()

    for rows, device, sem in ((pl.ds(0, 64), zm, x_sem.at[1]), (pl.ds(64, 64), zp, x_sem.at[2])):
        sends.start(lambda rows=rows: x_ref.at[rows], xb.at[2 + c, rows], sem, device)
    sends.start(x_ref, xb.at[c], x_sem.at[0], sibling)

    def q_half(pos, half):
        return qb.at[pl.ds(q_row(pos, half), HALF)]

    def send_queries(src, half, pred):
        for pos, back in ((3, 3), (1, 2), (2, 1)):
            sends.start(src, q_half(back, half), q_sem.at[back, half], yps[pos], pred)

    def send_keys(src, r, half, pred):
        sends.start(src, kvb.at[r, 2, half], kv_sem.at[r, 2, half, 0], xp, pred)
        sends.start(src, kvb.at[r, 1, half], kv_sem.at[r, 1, half, 0], xm, pred)
        sends.start(src, kvb.at[r, 0, half], kv_sem.at[r, 0, half, 0], sibling, pred)

    def stage_q(half):
        return stg.at[half, 0]

    def stage_kv(half):
        return stg.at[half, pl.ds(1, 2)]

    def send_half(half):
        copies = [
            pltpu.make_async_copy(stage_q(half), q_half(0, half), own_sem.at[half, 0]),
            pltpu.make_async_copy(stage_kv(half), kvb.at[0, 0, half], own_sem.at[half, 1])]
        for copy in copies:
            copy.start()
        send_keys(lambda: stage_kv(half), 0, half, is0)
        send_queries(lambda: stage_q(half), half, is0)
        for copy in copies:
            copy.wait()

    def swap_q(half):
        sends.start(lambda: stage_q(half), q_half(0, half), q_sem.at[0, half], partner, is1)

    def swap_kv(half):
        sends.start(lambda: stage_kv(half), kvb.at[1, 0, half], kv_sem.at[1, 0, half, 0], partner, is1)

    def swapped_q(half):
        arrived(q_half(0, half), q_sem.at[0, half])
        send_queries(lambda: q_half(0, half), half, is1)

    def swapped_kv(half):
        arrived(kvb.at[1, 0, half], kv_sem.at[1, 0, half, 0])
        send_keys(lambda: kvb.at[1, 0, half], 1, half, is1)

    def pass_on(r, half, pred):
        arrived(kvb.at[r, 1, half], kv_sem.at[r, 1, half, 0])
        sends.start(lambda: kvb.at[r, 1, half, 0], kvb.at[r, 3, half, 0], kv_sem.at[r, 3, half, 0], xm, pred)
        arrived(kvb.at[r, 2, half], kv_sem.at[r, 2, half, 0])
        sends.start(lambda: kvb.at[r, 2, half, 1], kvb.at[r, 3, half, 1], kv_sem.at[r, 3, half, 1], xp, pred)
        for pos in (1, 2):
            sends.start(lambda pos=pos: kvb.at[r, pos, half], kvb.at[r, pos, half],
                        kv_sem.at[r, pos, half, 0], sibling, pred)

    def pass_last(r, half, pred):
        for part in range(2):
            arrived(kvb.at[r, 3, half, part], kv_sem.at[r, 3, half, part])
        sends.start(lambda: kvb.at[r, 3, half], kvb.at[r, 3, half], kv_sem.at[r, 3, half, 0], sibling, pred)

    def from_sibling(r, blocks):
        for pos, half in blocks:
            arrived(kvb.at[r, pos, half], kv_sem.at[r, pos, half, 0])

    def on(pred, *steps):
        @pl.when(pred)
        def _():
            for step in steps:
                step()

    def over(blocks, q0, count, first=False):
        attend(qb, q0, count, [kvb.at[r, p, f, 0] for r, p, f in blocks],
               [kvb.at[r, p, f, 1] for r, p, f in blocks], acc, first)

    arrived(xb.at[1 - c], x_sem.at[0])
    norm_rows(xb.at[1 - c], nb, 128 * (1 - c), 128, shift, scale1)
    for copy in load_wv:
        copy.wait()
    project_wide(nb[...], wvb, stg.at[0], gains_ref[0:1, :], gains_ref[1:2, :])
    on(is0, lambda: send_half(0))
    on(is1, lambda: swap_q(0))
    ours = pl.ds(pl.multiple_of(c * W, 16), W)
    theirs = pl.ds(pl.multiple_of((1 - c) * W, 16), W)
    sends.start(wot_ref, wst_ref, w_sem.at[1], sibling)
    load_wo = pltpu.make_async_copy(wov_ref, wob.at[ours], load_sem.at[11])
    load_wo.start()
    load_mod[1].wait()
    load_mod[2].wait()

    arrived(xb.at[2 + c, pl.ds(0, 64)], x_sem.at[1])
    arrived(xb.at[2 + c, pl.ds(64, 64)], x_sem.at[2])
    sends.start(xb.at[2 + c], xb.at[2 + c], x_sem.at[3], sibling)
    on(is1, lambda: swap_kv(0), lambda: swapped_q(0))
    norm_rows(xb.at[2 + c], nb, 128 * c, 128, shift, scale1)
    arrived(xb.at[3 - c], x_sem.at[3])
    norm_rows(xb.at[3 - c], nb, 128 * (1 - c), 128, shift, scale1)
    on(is0, lambda: pass_on(0, 0, is0))
    project_wide(nb[...], wvb, stg.at[1], gains_ref[0:1, :], gains_ref[1:2, :])
    on(is0, lambda: send_half(1))
    on(is1, lambda: swap_q(1), lambda: swap_kv(1), lambda: swapped_kv(0))

    tq_row = pl.multiple_of(64 * x, 64)
    tq_other = tqst.at[pl.ds(pl.multiple_of(64 * x + TQ, TQ), TQ)]
    tq_own = qb.at[pl.ds(TROW, TQ)]

    @pl.when(is0)
    def _():
        load_xt.wait()
        for copy in load_wt:
            copy.wait()
        norm_rows(xtb, nb, 0, TXT, mod1[1, pl.ds(step, 1), :], 1.0 + mod2[0, pl.ds(step, 1), :])
        project(nb[...], [wtb.at[pl.ds(part * D, D)] for part in range(3)],
                [tqst, tkv.at[0], tkv.at[1]], gains_ref[2:3, :], gains_ref[3:4, :])
        copy = pltpu.make_async_copy(tqst.at[pl.ds(tq_row, TQ)], tq_own, own_sem.at[2, 0])
        copy.start()
        sends.start(tq_other, tq_own, t_sem.at[0], sibling, is0)
        sends.start(tkv, tkv, t_sem.at[1], sibling, is0)
        copy.wait()

    on(is0, lambda: pass_last(0, 0, is0))

    first_rows = q_row(ORDER[0], 0)

    def rows_of(base, size, i):
        return pl.multiple_of(base + i * size, 16)

    on(is1, lambda: from_sibling(0, [(0, 0), (1, 0), (2, 0)]))
    for pos in (1, 2, 3):
        arrived(q_half(pos, 0), q_sem.at[pos, 0])

    def first(i, carry):
        over([(0, 0, 0), (0, 1, 0), (0, 2, 0)], rows_of(first_rows, 512, i), 512, True)
        return carry

    lax.fori_loop(0, 2, first, 0)
    on(is0, lambda: from_sibling(1, [(0, 0)]))
    on(is1, lambda: swapped_q(1), lambda: from_sibling(0, [(0, 1)]))

    def second(i, carry):
        over([(0, 0, 1), (1, 0, 0)], rows_of(first_rows, 512, i), 512)
        return carry

    lax.fori_loop(0, 2, second, 0)
    on(is0, lambda: pass_on(0, 1, is0))
    on(is1, lambda: swapped_kv(1), lambda: pass_on(1, 0, is1),
       lambda: arrived(tq_own, t_sem.at[0]), lambda: arrived(tkv, t_sem.at[1]))
    sends.start(wov_ref, wob.at[ours], w_sem.at[0], sibling)

    arrived(wst_ref, w_sem.at[1])
    load_wo_text = []
    for i in range(8):
        cols = slice(i * W, (i + 1) * W)
        for k, (src, place) in enumerate(((wot_ref, c), (wst_ref, 1 - c))):
            rows = pl.ds(pl.multiple_of(i * 2 * W + place * W, 16), W)
            load_wo_text.append(pltpu.make_async_copy(
                src.at[:, cols], wtb.at[rows], load_sem.at[12 + 2 * i + k]))
    for copy in load_wo_text:
        copy.start()
    for pos in (1, 2, 3):
        arrived(q_half(pos, 1), q_sem.at[pos, 1])

    def third(i, carry):
        over([(0, 0, 0), (0, 1, 0), (0, 2, 0), (0, 0, 1), (1, 0, 0)], rows_of(0, 528, i), 528, True)
        return carry

    lax.fori_loop(0, 2, third, 0)
    on(is1, lambda: pass_last(1, 0, is1), lambda: pass_on(1, 1, is1),
       lambda: from_sibling(0, [(3, 0), (1, 1), (2, 1)]))
    on(is0, lambda: pass_last(0, 1, is0), lambda: from_sibling(1, [(1, 0), (2, 0), (0, 1)]))

    limit = len_ref[0]
    text_limit = jnp.where(y == 0, limit, 0)
    for q0, count, most in ((TROW, TQ, text_limit), (q_row(0, 1), HALF, limit), (q_row(0, 0), HALF, limit)):
        mask = lax.broadcasted_iota(jnp.int32, (count, TXT), 1) < most
        attend(qb, q0, count, [tkv.at[0]], [tkv.at[1]], acc, False, mask)

    middle_blocks = [(0, 3, 0), (0, 1, 1), (0, 2, 1), (1, 1, 0), (1, 2, 0), (1, 0, 1)]
    last_blocks = [(0, 3, 1), (1, 3, 0), (1, 1, 1), (1, 2, 1), (1, 3, 1)]

    def middle(i, carry):
        over(middle_blocks, rows_of(0, 528, i), 528)
        return carry

    lax.fori_loop(0, 2, middle, 0)
    on(is1, lambda: pass_last(1, 1, is1), lambda: from_sibling(0, [(3, 1)]))
    on(is0, lambda: from_sibling(1, [(3, 0), (1, 1), (2, 1), (3, 1)]))

    def send_sums(pos, half):
        back = {1: 2, 2: 1, 3: 3}[pos]
        rows = pl.ds(q_row(pos, half), HALF)
        for h in range(NH):
            osend[pos - 1, half, :, h * HD : (h + 1) * HD] = acc[h, rows, :HD].astype(BF16)
        dsend[pos - 1, half] = jnp.transpose(coded_denoms(acc, rows))[:24]
        sends.start(lambda: osend.at[pos - 1, half], orecv.at[back - 1, half],
                    o_sem.at[back - 1, half, 0], yps[pos])
        sends.start(lambda: dsend.at[pos - 1, half], drecv.at[back - 1, half],
                    o_sem.at[back - 1, half, 1], yps[pos])

    acol = pl.ds(pl.multiple_of(zh * W, HD), W)

    def combine(half):
        for pos in (3, 1, 2):
            arrived(orecv.at[pos - 1, half], o_sem.at[pos - 1, half, 0])
            arrived(drecv.at[pos - 1, half], o_sem.at[pos - 1, half, 1])
        rows = pl.ds(q_row(0, half), HALF)
        denoms = drecv[0, half] + drecv[1, half] + drecv[2, half]
        for h in range(NH):
            lanes = slice(h * HD, (h + 1) * HD)
            numer = acc[h, rows, :HD]
            for pos in range(3):
                numer = numer + orecv[pos, half, :, lanes].astype(F32)
            denom = acc[h, rows, HD:] + jnp.transpose(
                jnp.broadcast_to(denoms[8 * h : 8 * h + 1, :], (HD, HALF)))
            afin[half, :, lanes] = (numer / denom).astype(BF16)
        for core in range(2):
            dst = attn.at[half, :, acol]
            across = jnp.logical_and(is0, c != core)

            def src(core=core):
                return afin.at[half, pl.ds(core * 128, 128)]

            @pl.when(is1)
            def _():
                sends.start(src, dst, attn_sem.at[half], dev(x, y, z + 2, core), is1)

            @pl.when(jnp.logical_and(is0, c == core))
            def _():
                pltpu.make_async_copy(src(), dst, attn_sem.at[half]).start()

            @pl.when(across)
            def _():
                sends.start(src, dst, attn_sem.at[half], sibling, across)

    over(last_blocks, TROW, TQ + 512)

    for p in range(2):
        rows = pl.ds(TROW + 16 * p, 16)
        target = 2 * role + p
        for h in range(NH):
            tsend[p, :, h * HD : (h + 1) * HD] = acc[h, rows, :HD]
        tsend[p, :, W:] = coded_denoms(acc, rows)
        elsewhere = target != y

        @pl.when(elsewhere)
        def _():
            sends.start(lambda p=p: tsend.at[p], trecv.at[y], tr_sem.at[y], dev(x, target, z, c), elsewhere)

    send_sums(3, 1)
    send_sums(1, 1)
    over(last_blocks, q_row(2, 1), 512)
    send_sums(2, 1)
    over(middle_blocks + last_blocks, q_row(3, 0), 512)

    core_of = lax.rem(x, 2)
    to_sibling = jnp.logical_and(owner, core_of != c)

    @pl.when(owner)
    def _():
        for sy in range(4):
            @pl.when(sy != y)
            def _():
                arrived(trecv.at[sy], tr_sem.at[sy])

        total = tsend[y - 2 * role]
        for sy in range(4):
            total = total + jnp.where(sy != y, trecv[sy], 0.0)
        for h in range(NH):
            denom = total[:, W + 8 * h : W + 8 * h + 1]
            tfin[:, h * HD : (h + 1) * HD] = (total[:, h * HD : (h + 1) * HD] / denom).astype(BF16)
        trow = pl.multiple_of(lax.rem(x // 2, 2) * 64 + 16 * y, 16)
        tcol = pl.multiple_of(zh * W, HD)
        place = text.at[pl.ds(trow, 16), pl.ds(tcol, W)]
        for dx in range(4):
            for dy in range(4):
                for dz in range(2):
                    if dx + dy + dz == 0:
                        continue
                    sends.start(tfin, place, text_sem.at[0], dev(x + dx, y + dy, z + 2 * dz, core_of), owner)

        @pl.when(core_of == c)
        def _():
            pltpu.make_async_copy(tfin, place, text_sem.at[0]).start()

        @pl.when(core_of != c)
        def _():
            sends.start(tfin, place, text_sem.at[0], sibling, to_sibling)

    send_sums(3, 0)
    send_sums(1, 0)
    over(middle_blocks + last_blocks, q_row(2, 0), HALF)
    send_sums(2, 0)
    combine(1)
    over(middle_blocks + last_blocks, q_row(0, 0), HALF)

    for copy in load_wo_text:
        copy.wait()
    arrived(text, text_sem.at[0])
    far_row = pl.multiple_of((1 - zl) * 64, 64)
    own_row = pl.multiple_of(zl * 64, 64)
    for i in range(8):
        weight = wtb[i * 2 * W : (i + 1) * 2 * W, :]
        gsend[:, i * W : (i + 1) * W] = jnp.dot(
            text[pl.ds(far_row, 64), :], weight, preferred_element_type=F32).astype(BF16)
    low, high = pl.ds(0, 32), pl.ds(32, 32)
    sends.start(gsend.at[low], grecv.at[low], out_sem.at[NCH], zp)
    sends.start(gsend.at[high], grecv.at[high], out_sem.at[NCH], zm)
    load_wo.wait()
    arrived(wob.at[theirs], w_sem.at[0])
    arrived(attn.at[1], attn_sem.at[1])
    for i in range(NCH):
        cols = slice(i * CH, (i + 1) * CH)
        fsend[i] = jnp.dot(attn[1], wob[:, cols], preferred_element_type=F32).astype(BF16)
        for rows, device in ((pl.ds(0, 64), zp), (pl.ds(64, 64), zm)):
            sends.start(lambda i=i, rows=rows: fsend.at[i, rows], frecv.at[i, rows], out_sem.at[i], device)
    combine(0)
    row = lax.broadcasted_iota(jnp.int32, (64, W), 0) + (zl * 2 + c) * 64
    valid = row < len_ref[0]
    for i in range(8):
        cols = slice(i * W, (i + 1) * W)
        weight = wtb[i * 2 * W : (i + 1) * 2 * W, :]
        own = jnp.dot(text[pl.ds(own_row, 64), :], weight, preferred_element_type=F32)
        if i == 0:
            arrived(grecv, out_sem.at[NCH])
        gate = mod2[1, pl.ds(step, 1), cols]
        text_out_ref[:, cols] = jnp.where(
            valid, gate * (own + grecv[:, cols].astype(F32)), 0.0).astype(BF16)
    arrived(attn.at[0], attn_sem.at[0])
    for i in range(NCH):
        cols = slice(i * CH, (i + 1) * CH)
        own = jnp.dot(attn[0], wob[:, cols], preferred_element_type=F32)
        arrived(frecv.at[i], out_sem.at[i])
        gate = mod1[0, pl.ds(step, 1), cols]
        video_out_ref[:, cols] = (gate * (own + frecv[i].astype(F32))).astype(BF16)
    sends.finish()


def place_kernel(video_ref, text_ref, video_out_ref, text_out_ref):
    video_out_ref[...] = video_ref[...]
    text_out_ref[...] = text_ref[...]


ANY = pl.BlockSpec(memory_space=pl.ANY)
VMEM = pl.BlockSpec(memory_space=pltpu.VMEM)
SMEM = pl.BlockSpec(memory_space=pltpu.SMEM)
DMA = pltpu.SemaphoreType.DMA


def body(x_video, x_text, w_qkv_video, w_qkv_text, w_out_video, w_out_text, qk_gains, modulation,
         text_len, timestep):
    wv = jnp.transpose(w_qkv_video, (1, 0, 2))
    wt = jnp.transpose(w_qkv_text, (1, 0, 2))
    mod = jnp.transpose(modulation, (1, 0, 2))
    shape = jax.ShapeDtypeStruct
    steps = modulation.shape[0]
    results = [shape((128, D), BF16), shape((64, D), BF16)]
    video, text, unused = pl.pallas_call(
        block_kernel,
        name="block",
        in_specs=[ANY, ANY, ANY, ANY, ANY, VMEM, ANY, ANY, SMEM, SMEM],
        out_specs=[VMEM, VMEM, ANY],
        out_shape=results + [shape((W, D), BF16)],
        scratch_shapes=[
            pltpu.VMEM((4, 128, D), BF16), pltpu.VMEM((TXT, D), BF16),
            pltpu.VMEM((D, 3 * W), BF16), pltpu.VMEM((3 * D, W), BF16),
            pltpu.VMEM((2, steps, D), F32), pltpu.VMEM((2, steps, D), F32), pltpu.VMEM((2, steps, D), F32),
            pltpu.VMEM((HALF, D), BF16),
            pltpu.VMEM((2, 3, HALF, W), BF16), pltpu.VMEM((TXT, W), BF16),
            pltpu.VMEM((QROWS, W), BF16), pltpu.VMEM((2, 4, 2, 2, HALF, W), BF16),
            pltpu.VMEM((2, TXT, W), BF16), pltpu.VMEM((NH, QROWS, 2 * HD), F32),
            pltpu.VMEM((3, 2, HALF, W), BF16), pltpu.VMEM((3, 2, 24, HALF), F32),
            pltpu.VMEM((3, 2, HALF, W), BF16), pltpu.VMEM((3, 2, 24, HALF), F32),
            pltpu.VMEM((2, 16, W + HD), F32), pltpu.VMEM((4, 16, W + HD), F32),
            pltpu.VMEM((2, HALF, W), BF16), pltpu.VMEM((16, W), BF16),
            pltpu.VMEM((2, 128, 2 * W), BF16), pltpu.VMEM((128, 2 * W), BF16),
            pltpu.VMEM((2 * W, D), BF16),
            pltpu.VMEM((NCH, 128, CH), BF16), pltpu.VMEM((NCH, 128, CH), BF16),
            pltpu.VMEM((64, D), BF16), pltpu.VMEM((64, D), BF16),
            DMA((28,)), DMA((136,)), DMA((4,)), DMA((2,)), DMA((3, 2)), DMA((2, 4, 2, 2)), DMA((4, 2)),
            DMA((2,)), DMA((3, 2, 2)), DMA((4,)), DMA((2,)), DMA((1,)), DMA((NCH + 1,))],
        compiler_params=pltpu.CompilerParams(
            collective_id=1, has_side_effects=True, vmem_limit_bytes=VMEM_LIMIT),
    )(x_video, x_text, wv, wt, mod, qk_gains, w_out_video, w_out_text, text_len, timestep)
    return tuple(pl.pallas_call(
        place_kernel,
        name="place",
        in_specs=[VMEM, VMEM],
        out_specs=[VMEM, VMEM],
        out_shape=results,
    )(video, text))


def solution(mesh):
    grid = Mesh(mesh.devices.reshape(4, 4, 2, 2, 2), AXES)
    head = ("zl", "c")
    return jax.shard_map(
        body,
        mesh=grid,
        in_specs=(P(AXES, None), P(), P(None, None, head), P(None, None, head),
                  P(head, None), P(head, None), P(), P(), P(), P()),
        out_specs=(P(AXES, None), P(head, None)),
        check_vma=False,
    )
```

```python
import functools
import math

import jax
import jax.numpy as jnp
from jax import lax
from jax.experimental import pallas as pl
from jax.experimental.pallas import tpu as pltpu
from jax.sharding import Mesh, PartitionSpec as P

AXES = ("x", "y", "zh", "zl", "c")
MESH = pl.DeviceIdType.MESH
BF16, F32 = jnp.bfloat16, jnp.float32
D = 3072
HD = 128
NH = 3
W = NH * HD
HALF = 256
TXT = 256
TQ = 32
QROWS = 8 * HALF + TQ
ORDER = (3, 1, 2, 0)
CH = 768
NCH = D // CH
EXP_SCALE = math.log2(math.e) / math.sqrt(HD)
VMEM_LIMIT = 60 << 20


def coords():
    x, y, zh, zl, c = (lax.axis_index(a) for a in AXES)
    return x, y, zh * 2 + zl, c


def dev(x, y, z, c):
    z = lax.rem(z + 4, 4)
    return (lax.rem(x + 4, 4), lax.rem(y + 4, 4), z // 2, lax.rem(z, 2), c)


class Sends:
    def __init__(self, sems, peer):
        self.sems, self.peer, self.count, self.pending = sems, peer, 0, []

    def start(self, src, dst, recv_sem, device, pred=None):
        slot = self.count
        self.count += 1
        get = src if callable(src) else (lambda: src)

        pltpu.make_async_remote_copy(
            src_ref=get(), dst_ref=dst, send_sem=self.sems.at[slot], recv_sem=recv_sem,
            device_id=device, device_id_type=MESH).start()

        def wait():
            pltpu.make_async_remote_copy(
                src_ref=get(), dst_ref=get(), send_sem=self.sems.at[slot], recv_sem=self.sems.at[slot],
                device_id=self.peer, device_id_type=MESH).wait_send()

        self.pending.append((pred, wait))

    def finish(self):
        for pred, wait in self.pending:
            if pred is None:
                wait()
            else:
                pl.when(pred)(wait)


def signal(sem, device):
    pl.semaphore_signal(sem, inc=1, device_id=device, device_id_type=MESH)


def norm_rows(src, dst, dst_row, count, shift, scale1):
    def strip(i, carry):
        wide = src[pl.ds(pl.multiple_of(i * 16, 16), 16), :].astype(F32)
        centred = wide - jnp.mean(wide, axis=-1, keepdims=True)
        variance = jnp.mean(centred * centred, axis=-1, keepdims=True)
        out = centred * lax.rsqrt(variance + 1e-06) * scale1 + shift
        dst[pl.ds(pl.multiple_of(dst_row + i * 16, 16), 16), :] = out.astype(BF16)
        return carry

    lax.fori_loop(0, count // 16, strip, 0, unroll=2)


def project(rows, weights, outs, gain_query, gain_key):
    for part in range(3):
        flat = jnp.dot(rows, weights[part][...], preferred_element_type=F32)
        for h in range(NH):
            lanes = slice(h * HD, (h + 1) * HD)
            u = flat[:, lanes]
            if part < 2:
                gain = gain_query if part == 0 else gain_key
                meansq = jnp.mean(u * u, axis=-1, keepdims=True)
                u = u * lax.rsqrt(meansq + 1e-06) * gain
            outs[part][:, lanes] = u.astype(BF16)


def project_wide(rows, weight, out, gain_query, gain_key):
    flat = jnp.dot(rows, weight[...], preferred_element_type=F32)
    for part in range(3):
        for h in range(NH):
            u = flat[:, part * W + h * HD : part * W + (h + 1) * HD]
            if part < 2:
                gain = gain_query if part == 0 else gain_key
                meansq = jnp.mean(u * u, axis=-1, keepdims=True)
                u = u * lax.rsqrt(meansq + 1e-06) * gain
            out[part, :, h * HD : (h + 1) * HD] = u.astype(BF16)


def attend(qb, q0, count, keys, values, acc, first, mask=None):
    for h in range(NH):
        lanes = slice(h * HD, (h + 1) * HD)
        query = qb[pl.ds(q0, count), lanes]
        total = None
        for key_ref, value_ref in zip(keys, values):
            scores = lax.dot_general(
                query, key_ref[:, lanes], (((1,), (1,)), ((), ())), preferred_element_type=F32)
            expo = jnp.exp2(scores * EXP_SCALE)
            if mask is not None:
                expo = jnp.where(mask, expo, 0.0)
            value = value_ref[:, lanes]
            wide = jnp.concatenate([value, jnp.ones_like(value)], axis=1)
            part = jnp.dot(expo.astype(BF16), wide, preferred_element_type=F32)
            total = part if total is None else total + part
        if first:
            acc[h, pl.ds(q0, count), :] = total
        else:
            acc[h, pl.ds(q0, count), :] += total


def coded_denoms(acc, rows):
    parts = [acc[h, rows, HD:] for h in range(NH)]
    lane = lax.broadcasted_iota(jnp.int32, parts[0].shape, 1)
    return jnp.where(lane < 8, parts[0], jnp.where(lane < 16, parts[1], parts[2]))


def q_row(pos, half):
    return TQ + ORDER.index(pos) * HALF + (0 if half else 4 * HALF)


TROW = 0


def block_kernel(x_ref, xt_ref, wv_ref, wt_ref, mod_ref, gains_ref, wov_ref, wot_ref, len_ref, step_ref,
                 video_out_ref, text_out_ref, wst_ref,
                 xb, xtb, wvb, wtb, mod0, mod1, mod2, nb, stg, tqst, qb, kvb, tkv, acc, osend, dsend, orecv, drecv,
                 tsend, trecv, afin, tfin, attn, text, wob, gsend, grecv,
                 load_sem, send_sem, x_sem, w_sem, own_sem, kv_sem, q_sem, t_sem, o_sem, tr_sem,
                 attn_sem, text_sem, out_sem):
    x, y, z, c = coords()
    zh, zl = z // 2, lax.rem(z, 2)
    role = lax.rem(c + zh, 2)
    is0, is1 = role == 0, role == 1
    sibling = dev(x, y, z, 1 - c)
    partner = dev(x, y, z + 2, 1 - c)
    xp, xm = dev(x + 1, y, z, c), dev(x - 1, y, z, c)
    yps = {1: dev(x, y + 1, z, c), 2: dev(x, y - 1, z, c), 3: dev(x, y + 2, z, c)}
    zp, zm = dev(x, y, z + 1, c), dev(x, y, z - 1, c)
    owner = role == y // 2

    load_x = pltpu.make_async_copy(x_ref, xb.at[c], load_sem.at[0])
    load_mod = [
        pltpu.make_async_copy(mod_ref.at[pl.ds(2 * i, 2)], part, load_sem.at[1 + i])
        for i, part in enumerate((mod0, mod1, mod2))]
    load_wv = [
        pltpu.make_async_copy(wv_ref.at[part], wvb.at[:, part * W : (part + 1) * W], load_sem.at[4 + part])
        for part in range(3)]
    load_xt = pltpu.make_async_copy(xt_ref, xtb, load_sem.at[7])
    load_wt = [
        pltpu.make_async_copy(wt_ref.at[part], wtb.at[pl.ds(part * D, D)], load_sem.at[8 + part])
        for part in range(3)]
    for copy in [load_x, load_mod[0]] + load_wv:
        copy.start()

    @pl.when(is0)
    def _():
        for copy in [load_xt] + load_wt:
            copy.start()

    load_mod[1].start()
    load_mod[2].start()

    barrier = pltpu.get_barrier_semaphore()
    for device in (sibling, xp, xm, yps[1], yps[2], yps[3], zp, zm, dev(x, y, z + 2, zh)):
        signal(barrier, device)

    @pl.when(is1)
    def _():
        signal(barrier, dev(x, y, z + 2, 1 - zh))

    step = step_ref[0]
    load_x.wait()
    load_mod[0].wait()
    shift, scale1 = mod0[0, pl.ds(step, 1), :], 1.0 + mod0[1, pl.ds(step, 1), :]
    norm_rows(xb.at[c], nb, 128 * c, 128, shift, scale1)
    pl.semaphore_wait(barrier, 9 + role)

    sends = Sends(send_sem, sibling)

    def arrived(dst, sem):
        pltpu.make_async_remote_copy(
            src_ref=dst, dst_ref=dst, send_sem=send_sem.at[0], recv_sem=sem,
            device_id=sibling, device_id_type=MESH).wait_recv()

    for rows, device, sem in ((pl.ds(0, 64), zm, x_sem.at[1]), (pl.ds(64, 64), zp, x_sem.at[2])):
        sends.start(lambda rows=rows: x_ref.at[rows], xb.at[2 + c, rows], sem, device)
    sends.start(x_ref, xb.at[c], x_sem.at[0], sibling)

    def q_half(pos, half):
        return qb.at[pl.ds(q_row(pos, half), HALF)]

    def send_queries(src, half, pred):
        for pos, back in ((3, 3), (1, 2), (2, 1)):
            sends.start(src, q_half(back, half), q_sem.at[back, half], yps[pos], pred)

    def send_keys(src, r, half, pred):
        sends.start(src, kvb.at[r, 2, half], kv_sem.at[r, 2, half, 0], xp, pred)
        sends.start(src, kvb.at[r, 1, half], kv_sem.at[r, 1, half, 0], xm, pred)
        sends.start(src, kvb.at[r, 0, half], kv_sem.at[r, 0, half, 0], sibling, pred)

    def stage_q(half):
        return stg.at[half, 0]

    def stage_kv(half):
        return stg.at[half, pl.ds(1, 2)]

    def send_half(half):
        copies = [
            pltpu.make_async_copy(stage_q(half), q_half(0, half), own_sem.at[half, 0]),
            pltpu.make_async_copy(stage_kv(half), kvb.at[0, 0, half], own_sem.at[half, 1])]
        for copy in copies:
            copy.start()
        send_keys(lambda: stage_kv(half), 0, half, is0)
        send_queries(lambda: stage_q(half), half, is0)
        for copy in copies:
            copy.wait()

    def swap_q(half):
        sends.start(lambda: stage_q(half), q_half(0, half), q_sem.at[0, half], partner, is1)

    def swap_kv(half):
        sends.start(lambda: stage_kv(half), kvb.at[1, 0, half], kv_sem.at[1, 0, half, 0], partner, is1)

    def swapped_q(half):
        arrived(q_half(0, half), q_sem.at[0, half])
        send_queries(lambda: q_half(0, half), half, is1)

    def swapped_kv(half):
        arrived(kvb.at[1, 0, half], kv_sem.at[1, 0, half, 0])
        send_keys(lambda: kvb.at[1, 0, half], 1, half, is1)

    def pass_on(r, half, pred):
        arrived(kvb.at[r, 1, half], kv_sem.at[r, 1, half, 0])
        sends.start(lambda: kvb.at[r, 1, half, 0], kvb.at[r, 3, half, 0], kv_sem.at[r, 3, half, 0], xm, pred)
        arrived(kvb.at[r, 2, half], kv_sem.at[r, 2, half, 0])
        sends.start(lambda: kvb.at[r, 2, half, 1], kvb.at[r, 3, half, 1], kv_sem.at[r, 3, half, 1], xp, pred)
        for pos in (1, 2):
            sends.start(lambda pos=pos: kvb.at[r, pos, half], kvb.at[r, pos, half],
                        kv_sem.at[r, pos, half, 0], sibling, pred)

    def pass_last(r, half, pred):
        for part in range(2):
            arrived(kvb.at[r, 3, half, part], kv_sem.at[r, 3, half, part])
        sends.start(lambda: kvb.at[r, 3, half], kvb.at[r, 3, half], kv_sem.at[r, 3, half, 0], sibling, pred)

    def from_sibling(r, blocks):
        for pos, half in blocks:
            arrived(kvb.at[r, pos, half], kv_sem.at[r, pos, half, 0])

    def on(pred, *steps):
        @pl.when(pred)
        def _():
            for step in steps:
                step()

    def over(blocks, q0, count, first=False):
        attend(qb, q0, count, [kvb.at[r, p, f, 0] for r, p, f in blocks],
               [kvb.at[r, p, f, 1] for r, p, f in blocks], acc, first)

    arrived(xb.at[1 - c], x_sem.at[0])
    norm_rows(xb.at[1 - c], nb, 128 * (1 - c), 128, shift, scale1)
    for copy in load_wv:
        copy.wait()
    project_wide(nb[...], wvb, stg.at[0], gains_ref[0:1, :], gains_ref[1:2, :])
    on(is0, lambda: send_half(0))
    on(is1, lambda: swap_q(0))
    ours = pl.ds(pl.multiple_of((2 * zl + c) * W, 16), W)
    theirs = pl.ds(pl.multiple_of((2 * zl + 1 - c) * W, 16), W)
    far = pl.ds(pl.multiple_of((2 - 2 * zl + c) * W, 16), W)
    far_theirs = pl.ds(pl.multiple_of((2 - 2 * zl + 1 - c) * W, 16), W)

    def send_weights(piece):
        for start, device in ((0, zp), (W // 2, zm)):
            first_row = start + piece * (W // 4)
            place = pl.multiple_of((2 * zl + c) * W + first_row, 16)
            sends.start(lambda first_row=first_row: wov_ref.at[pl.ds(first_row, W // 4)],
                        wob.at[pl.ds(place, W // 4)], w_sem.at[2], device)

    sends.start(wot_ref, wst_ref, w_sem.at[1], sibling)
    load_wo = pltpu.make_async_copy(wov_ref, wob.at[ours], load_sem.at[11])
    load_wo.start()
    load_mod[1].wait()
    load_mod[2].wait()

    arrived(xb.at[2 + c, pl.ds(0, 64)], x_sem.at[1])
    arrived(xb.at[2 + c, pl.ds(64, 64)], x_sem.at[2])
    sends.start(xb.at[2 + c], xb.at[2 + c], x_sem.at[3], sibling)
    on(is1, lambda: swap_kv(0), lambda: swapped_q(0))
    norm_rows(xb.at[2 + c], nb, 128 * c, 128, shift, scale1)
    arrived(xb.at[3 - c], x_sem.at[3])
    norm_rows(xb.at[3 - c], nb, 128 * (1 - c), 128, shift, scale1)
    on(is0, lambda: pass_on(0, 0, is0))
    project_wide(nb[...], wvb, stg.at[1], gains_ref[0:1, :], gains_ref[1:2, :])
    on(is0, lambda: send_half(1))
    on(is1, lambda: swap_q(1), lambda: swap_kv(1), lambda: swapped_kv(0))

    tq_row = pl.multiple_of(64 * x, 64)
    tq_other = tqst.at[pl.ds(pl.multiple_of(64 * x + TQ, TQ), TQ)]
    tq_own = qb.at[pl.ds(TROW, TQ)]

    @pl.when(is0)
    def _():
        load_xt.wait()
        for copy in load_wt:
            copy.wait()
        norm_rows(xtb, nb, 0, TXT, mod1[1, pl.ds(step, 1), :], 1.0 + mod2[0, pl.ds(step, 1), :])
        project(nb[...], [wtb.at[pl.ds(part * D, D)] for part in range(3)],
                [tqst, tkv.at[0], tkv.at[1]], gains_ref[2:3, :], gains_ref[3:4, :])
        copy = pltpu.make_async_copy(tqst.at[pl.ds(tq_row, TQ)], tq_own, own_sem.at[2, 0])
        copy.start()
        sends.start(tq_other, tq_own, t_sem.at[0], sibling, is0)
        sends.start(tkv, tkv, t_sem.at[1], sibling, is0)
        copy.wait()

    on(is0, lambda: pass_last(0, 0, is0))

    first_rows = q_row(ORDER[0], 0)

    def rows_of(base, size, i):
        return pl.multiple_of(base + i * size, 16)

    on(is1, lambda: from_sibling(0, [(0, 0), (1, 0), (2, 0)]))
    for pos in (1, 2, 3):
        arrived(q_half(pos, 0), q_sem.at[pos, 0])

    def first(i, carry):
        over([(0, 0, 0), (0, 1, 0), (0, 2, 0)], rows_of(first_rows, 512, i), 512, True)
        return carry

    lax.fori_loop(0, 2, first, 0)
    on(is0, lambda: from_sibling(1, [(0, 0)]))
    on(is1, lambda: swapped_q(1), lambda: from_sibling(0, [(0, 1)]))

    def second(i, carry):
        over([(0, 0, 1), (1, 0, 0)], rows_of(first_rows, 512, i), 512)
        return carry

    lax.fori_loop(0, 2, second, 0)
    on(is0, lambda: pass_on(0, 1, is0))
    on(is1, lambda: swapped_kv(1), lambda: pass_on(1, 0, is1),
       lambda: arrived(tq_own, t_sem.at[0]), lambda: arrived(tkv, t_sem.at[1]))
    send_weights(0)

    arrived(wst_ref, w_sem.at[1])
    load_wo_text = []
    for i in range(8):
        cols = slice(i * W, (i + 1) * W)
        for k, (src, place) in enumerate(((wot_ref, c), (wst_ref, 1 - c))):
            rows = pl.ds(pl.multiple_of(i * 2 * W + place * W, 16), W)
            load_wo_text.append(pltpu.make_async_copy(
                src.at[:, cols], wtb.at[rows], load_sem.at[12 + 2 * i + k]))
    for copy in load_wo_text:
        copy.start()
    for pos in (1, 2, 3):
        arrived(q_half(pos, 1), q_sem.at[pos, 1])

    def third(i, carry):
        over([(0, 0, 0), (0, 1, 0), (0, 2, 0), (0, 0, 1), (1, 0, 0)], rows_of(0, 528, i), 528, True)
        return carry

    lax.fori_loop(0, 2, third, 0)
    send_weights(1)
    sends.start(wov_ref, wob.at[ours], w_sem.at[0], sibling)
    on(is1, lambda: pass_last(1, 0, is1), lambda: pass_on(1, 1, is1),
       lambda: from_sibling(0, [(3, 0), (1, 1), (2, 1)]))
    on(is0, lambda: pass_last(0, 1, is0), lambda: from_sibling(1, [(1, 0), (2, 0), (0, 1)]))

    limit = len_ref[0]
    text_limit = jnp.where(y == 0, limit, 0)
    for q0, count, most in ((TROW, TQ, text_limit), (q_row(0, 1), HALF, limit), (q_row(0, 0), HALF, limit)):
        mask = lax.broadcasted_iota(jnp.int32, (count, TXT), 1) < most
        attend(qb, q0, count, [tkv.at[0]], [tkv.at[1]], acc, False, mask)

    middle_blocks = [(0, 3, 0), (0, 1, 1), (0, 2, 1), (1, 1, 0), (1, 2, 0), (1, 0, 1)]
    last_blocks = [(0, 3, 1), (1, 3, 0), (1, 1, 1), (1, 2, 1), (1, 3, 1)]

    def middle(i, carry):
        over(middle_blocks, rows_of(0, 528, i), 528)
        return carry

    lax.fori_loop(0, 2, middle, 0)
    on(is1, lambda: pass_last(1, 1, is1), lambda: from_sibling(0, [(3, 1)]))
    on(is0, lambda: from_sibling(1, [(3, 0), (1, 1), (2, 1), (3, 1)]))

    def send_sums(pos, half):
        back = {1: 2, 2: 1, 3: 3}[pos]
        rows = pl.ds(q_row(pos, half), HALF)
        for h in range(NH):
            osend[pos - 1, half, :, h * HD : (h + 1) * HD] = acc[h, rows, :HD].astype(BF16)
        dsend[pos - 1, half] = jnp.transpose(coded_denoms(acc, rows))[:24]
        sends.start(lambda: osend.at[pos - 1, half], orecv.at[back - 1, half],
                    o_sem.at[back - 1, half, 0], yps[pos])
        sends.start(lambda: dsend.at[pos - 1, half], drecv.at[back - 1, half],
                    o_sem.at[back - 1, half, 1], yps[pos])

    acol = pl.ds(pl.multiple_of((2 * zl + zh) * W, HD), W)
    ahead = 1 - 2 * role

    def combine(half):
        for pos in (3, 1, 2):
            arrived(orecv.at[pos - 1, half], o_sem.at[pos - 1, half, 0])
            arrived(drecv.at[pos - 1, half], o_sem.at[pos - 1, half, 1])
        rows = pl.ds(q_row(0, half), HALF)
        denoms = drecv[0, half] + drecv[1, half] + drecv[2, half]
        for h in range(NH):
            lanes = slice(h * HD, (h + 1) * HD)
            numer = acc[h, rows, :HD]
            for pos in range(3):
                numer = numer + orecv[pos, half, :, lanes].astype(F32)
            denom = acc[h, rows, HD:] + jnp.transpose(
                jnp.broadcast_to(denoms[8 * h : 8 * h + 1, :], (HD, HALF)))
            afin[half, :, lanes] = (numer / denom).astype(BF16)
        if half:
            for core in range(2):
                for first_row, step_z in ((0, ahead), (64, -ahead)):
                    rows = pl.ds(core * 128 + first_row, 64)
                    sends.start(lambda rows=rows: afin.at[half, rows],
                                attn.at[pl.ds(first_row, 64), acol], attn_sem.at[1],
                                dev(x, y, z + step_z, core))
            return
        for core in range(2):
            dst = attn.at[:, acol]
            across = jnp.logical_and(is0, c != core)

            def src(core=core):
                return afin.at[0, pl.ds(core * 128, 128)]

            @pl.when(is1)
            def _():
                sends.start(src, dst, attn_sem.at[0], dev(x, y, z + 2, core), is1)

            @pl.when(jnp.logical_and(is0, c == core))
            def _():
                pltpu.make_async_copy(src(), dst, attn_sem.at[0]).start()

            @pl.when(across)
            def _():
                sends.start(src, dst, attn_sem.at[0], sibling, across)

    over(last_blocks, TROW, TQ + 512)

    for p in range(2):
        rows = pl.ds(TROW + 16 * p, 16)
        target = 2 * role + p
        for h in range(NH):
            tsend[p, :, h * HD : (h + 1) * HD] = acc[h, rows, :HD]
        tsend[p, :, W:] = coded_denoms(acc, rows)
        elsewhere = target != y

        @pl.when(elsewhere)
        def _():
            sends.start(lambda p=p: tsend.at[p], trecv.at[y], tr_sem.at[y], dev(x, target, z, c), elsewhere)

    send_sums(3, 1)
    send_sums(1, 1)
    over(last_blocks, q_row(2, 1), 512)
    send_sums(2, 1)
    over(middle_blocks + last_blocks, q_row(3, 0), 512)

    core_of = lax.rem(x, 2)
    to_sibling = jnp.logical_and(owner, core_of != c)

    @pl.when(owner)
    def _():
        for sy in range(4):
            @pl.when(sy != y)
            def _():
                arrived(trecv.at[sy], tr_sem.at[sy])

        total = tsend[y - 2 * role]
        for sy in range(4):
            total = total + jnp.where(sy != y, trecv[sy], 0.0)
        for h in range(NH):
            denom = total[:, W + 8 * h : W + 8 * h + 1]
            tfin[:, h * HD : (h + 1) * HD] = (total[:, h * HD : (h + 1) * HD] / denom).astype(BF16)
        trow = pl.multiple_of(lax.rem(x // 2, 2) * 64 + 16 * y, 16)
        tcol = pl.multiple_of(zh * W, HD)
        place = text.at[pl.ds(trow, 16), pl.ds(tcol, W)]
        for dx in range(4):
            for dy in range(4):
                for dz in range(2):
                    if dx + dy + dz == 0:
                        continue
                    sends.start(tfin, place, text_sem.at[0], dev(x + dx, y + dy, z + 2 * dz, core_of), owner)

        @pl.when(core_of == c)
        def _():
            pltpu.make_async_copy(tfin, place, text_sem.at[0]).start()

        @pl.when(core_of != c)
        def _():
            sends.start(tfin, place, text_sem.at[0], sibling, to_sibling)

    send_sums(3, 0)
    send_sums(1, 0)
    over(middle_blocks + last_blocks, q_row(2, 0), HALF)
    send_sums(2, 0)
    over(middle_blocks + last_blocks, q_row(0, 0), HALF)
    arrived(wob.at[far], w_sem.at[2])
    sends.start(wob.at[far], wob.at[far], w_sem.at[3], sibling)

    for copy in load_wo_text:
        copy.wait()
    arrived(text, text_sem.at[0])
    far_row = pl.multiple_of((1 - zl) * 64, 64)
    own_row = pl.multiple_of(zl * 64, 64)
    for i in range(8):
        weight = wtb[i * 2 * W : (i + 1) * 2 * W, :]
        gsend[:, i * W : (i + 1) * W] = jnp.dot(
            text[pl.ds(far_row, 64), :], weight, preferred_element_type=F32).astype(BF16)
    low, high = pl.ds(0, 32), pl.ds(32, 32)
    sends.start(gsend.at[low], grecv.at[low], out_sem.at[0], zp)
    sends.start(gsend.at[high], grecv.at[high], out_sem.at[0], zm)
    combine(1)
    combine(0)
    row = lax.broadcasted_iota(jnp.int32, (64, W), 0) + (zl * 2 + c) * 64
    valid = row < len_ref[0]
    for i in range(8):
        cols = slice(i * W, (i + 1) * W)
        weight = wtb[i * 2 * W : (i + 1) * 2 * W, :]
        own = jnp.dot(text[pl.ds(own_row, 64), :], weight, preferred_element_type=F32)
        if i == 0:
            arrived(grecv, out_sem.at[0])
        gate = mod2[1, pl.ds(step, 1), cols]
        text_out_ref[:, cols] = jnp.where(
            valid, gate * (own + grecv[:, cols].astype(F32)), 0.0).astype(BF16)
    load_wo.wait()
    arrived(wob.at[theirs], w_sem.at[0])
    arrived(wob.at[far_theirs], w_sem.at[3])
    for part, group in ((1, 1 - zl), (0, zl)):
        arrived(attn.at[:, pl.ds(pl.multiple_of(group * 2 * W, HD), 2 * W)], attn_sem.at[part])
    for i in range(NCH):
        cols = slice(i * CH, (i + 1) * CH)
        out = jnp.dot(attn[...], wob[:, cols], preferred_element_type=F32)
        video_out_ref[:, cols] = (mod1[0, pl.ds(step, 1), cols] * out).astype(BF16)
    sends.finish()


def place_kernel(video_ref, text_ref, video_out_ref, text_out_ref):
    video_out_ref[...] = video_ref[...]
    text_out_ref[...] = text_ref[...]


ANY = pl.BlockSpec(memory_space=pl.ANY)
VMEM = pl.BlockSpec(memory_space=pltpu.VMEM)
SMEM = pl.BlockSpec(memory_space=pltpu.SMEM)
DMA = pltpu.SemaphoreType.DMA


def body(x_video, x_text, w_qkv_video, w_qkv_text, w_out_video, w_out_text, qk_gains, modulation,
         text_len, timestep):
    wv = jnp.transpose(w_qkv_video, (1, 0, 2))
    wt = jnp.transpose(w_qkv_text, (1, 0, 2))
    mod = jnp.transpose(modulation, (1, 0, 2))
    shape = jax.ShapeDtypeStruct
    steps = modulation.shape[0]
    results = [shape((128, D), BF16), shape((64, D), BF16)]
    video, text, unused = pl.pallas_call(
        block_kernel,
        name="block",
        in_specs=[ANY, ANY, ANY, ANY, ANY, VMEM, ANY, ANY, SMEM, SMEM],
        out_specs=[VMEM, VMEM, ANY],
        out_shape=results + [shape((W, D), BF16)],
        scratch_shapes=[
            pltpu.VMEM((4, 128, D), BF16), pltpu.VMEM((TXT, D), BF16),
            pltpu.VMEM((D, 3 * W), BF16), pltpu.VMEM((3 * D, W), BF16),
            pltpu.VMEM((2, steps, D), F32), pltpu.VMEM((2, steps, D), F32), pltpu.VMEM((2, steps, D), F32),
            pltpu.VMEM((HALF, D), BF16),
            pltpu.VMEM((2, 3, HALF, W), BF16), pltpu.VMEM((TXT, W), BF16),
            pltpu.VMEM((QROWS, W), BF16), pltpu.VMEM((2, 4, 2, 2, HALF, W), BF16),
            pltpu.VMEM((2, TXT, W), BF16), pltpu.VMEM((NH, QROWS, 2 * HD), F32),
            pltpu.VMEM((3, 2, HALF, W), BF16), pltpu.VMEM((3, 2, 24, HALF), F32),
            pltpu.VMEM((3, 2, HALF, W), BF16), pltpu.VMEM((3, 2, 24, HALF), F32),
            pltpu.VMEM((2, 16, W + HD), F32), pltpu.VMEM((4, 16, W + HD), F32),
            pltpu.VMEM((2, HALF, W), BF16), pltpu.VMEM((16, W), BF16),
            pltpu.VMEM((128, 4 * W), BF16), pltpu.VMEM((128, 2 * W), BF16), pltpu.VMEM((4 * W, D), BF16),
            pltpu.VMEM((64, D), BF16), pltpu.VMEM((64, D), BF16),
            DMA((28,)), DMA((136,)), DMA((4,)), DMA((4,)), DMA((3, 2)), DMA((2, 4, 2, 2)), DMA((4, 2)),
            DMA((2,)), DMA((3, 2, 2)), DMA((4,)), DMA((2,)), DMA((1,)), DMA((1,))],
        compiler_params=pltpu.CompilerParams(
            collective_id=1, has_side_effects=True, vmem_limit_bytes=VMEM_LIMIT),
    )(x_video, x_text, wv, wt, mod, qk_gains, w_out_video, w_out_text, text_len, timestep)
    return tuple(pl.pallas_call(
        place_kernel,
        name="place",
        in_specs=[VMEM, VMEM],
        out_specs=[VMEM, VMEM],
        out_shape=results,
    )(video, text))


def solution(mesh):
    grid = Mesh(mesh.devices.reshape(4, 4, 2, 2, 2), AXES)
    head = ("zl", "c")
    return jax.shard_map(
        body,
        mesh=grid,
        in_specs=(P(AXES, None), P(), P(None, None, head), P(None, None, head),
                  P(head, None), P(head, None), P(), P(), P(), P()),
        out_specs=(P(AXES, None), P(head, None)),
        check_vma=False,
    )
```

```python
import functools
import math

import jax
import jax.numpy as jnp
from jax import lax
from jax.experimental import pallas as pl
from jax.experimental.pallas import tpu as pltpu
from jax.sharding import Mesh, PartitionSpec as P

AXES = ("x", "y", "zh", "zl", "c")
MESH = pl.DeviceIdType.MESH
BF16, F32 = jnp.bfloat16, jnp.float32
D = 3072
HD = 128
NH = 3
W = NH * HD
HALF = 256
TXT = 256
TQ = 32
QROWS = 8 * HALF + TQ
ORDER = (3, 1, 2, 0)
CH = 768
NCH = D // CH
EXP_SCALE = math.log2(math.e) / math.sqrt(HD)
VMEM_LIMIT = 60 << 20


def coords():
    x, y, zh, zl, c = (lax.axis_index(a) for a in AXES)
    return x, y, zh * 2 + zl, c


def dev(x, y, z, c):
    z = lax.rem(z + 4, 4)
    return (lax.rem(x + 4, 4), lax.rem(y + 4, 4), z // 2, lax.rem(z, 2), c)


class Sends:
    def __init__(self, sems, peer):
        self.sems, self.peer, self.count, self.pending = sems, peer, 0, []

    def start(self, src, dst, recv_sem, device, pred=None):
        slot = self.count
        self.count += 1
        get = src if callable(src) else (lambda: src)

        pltpu.make_async_remote_copy(
            src_ref=get(), dst_ref=dst, send_sem=self.sems.at[slot], recv_sem=recv_sem,
            device_id=device, device_id_type=MESH).start()

        def wait():
            pltpu.make_async_remote_copy(
                src_ref=get(), dst_ref=get(), send_sem=self.sems.at[slot], recv_sem=self.sems.at[slot],
                device_id=self.peer, device_id_type=MESH).wait_send()

        self.pending.append((pred, wait))

    def finish(self):
        for pred, wait in self.pending:
            if pred is None:
                wait()
            else:
                pl.when(pred)(wait)


def signal(sem, device):
    pl.semaphore_signal(sem, inc=1, device_id=device, device_id_type=MESH)


def norm_rows(src, dst, dst_row, count, shift, scale1):
    def strip(i, carry):
        wide = src[pl.ds(pl.multiple_of(i * 16, 16), 16), :].astype(F32)
        centred = wide - jnp.mean(wide, axis=-1, keepdims=True)
        variance = jnp.mean(centred * centred, axis=-1, keepdims=True)
        out = centred * lax.rsqrt(variance + 1e-06) * scale1 + shift
        dst[pl.ds(pl.multiple_of(dst_row + i * 16, 16), 16), :] = out.astype(BF16)
        return carry

    lax.fori_loop(0, count // 16, strip, 0, unroll=4)


def project(rows, weights, outs, gain_query, gain_key):
    for part in range(3):
        flat = jnp.dot(rows, weights[part][...], preferred_element_type=F32)
        for h in range(NH):
            lanes = slice(h * HD, (h + 1) * HD)
            u = flat[:, lanes]
            if part < 2:
                gain = gain_query if part == 0 else gain_key
                meansq = jnp.mean(u * u, axis=-1, keepdims=True)
                u = u * lax.rsqrt(meansq + 1e-06) * gain
            outs[part][:, lanes] = u.astype(BF16)


def project_wide(rows, weight, out, gain_query, gain_key):
    flat = jnp.dot(rows, weight[...], preferred_element_type=F32)
    for part in range(3):
        for h in range(NH):
            u = flat[:, part * W + h * HD : part * W + (h + 1) * HD]
            if part < 2:
                gain = gain_query if part == 0 else gain_key
                meansq = jnp.mean(u * u, axis=-1, keepdims=True)
                u = u * lax.rsqrt(meansq + 1e-06) * gain
            out[part, :, h * HD : (h + 1) * HD] = u.astype(BF16)


def attend(qb, q0, count, keys, values, acc, first, mask=None):
    for h in range(NH):
        lanes = slice(h * HD, (h + 1) * HD)
        query = qb[pl.ds(q0, count), lanes]
        total = None
        for key_ref, value_ref in zip(keys, values):
            scores = lax.dot_general(
                query, key_ref[:, lanes], (((1,), (1,)), ((), ())), preferred_element_type=F32)
            expo = jnp.exp2(scores * EXP_SCALE)
            if mask is not None:
                expo = jnp.where(mask, expo, 0.0)
            value = value_ref[:, lanes]
            wide = jnp.concatenate([value, jnp.ones_like(value)], axis=1)
            part = jnp.dot(expo.astype(BF16), wide, preferred_element_type=F32)
            total = part if total is None else total + part
        if first:
            acc[h, pl.ds(q0, count), :] = total
        else:
            acc[h, pl.ds(q0, count), :] += total


def coded_denoms(acc, rows):
    parts = [acc[h, rows, HD:] for h in range(NH)]
    lane = lax.broadcasted_iota(jnp.int32, parts[0].shape, 1)
    return jnp.where(lane < 8, parts[0], jnp.where(lane < 16, parts[1], parts[2]))


def q_row(pos, half):
    return TQ + ORDER.index(pos) * HALF + (0 if half else 4 * HALF)


TROW = 0


def block_kernel(x_ref, xt_ref, wv_ref, wt_ref, mod_ref, gains_ref, wov_ref, wot_ref, len_ref, step_ref,
                 video_out_ref, text_out_ref, wst_ref,
                 xb, xtb, wvb, wtb, mod0, mod1, mod2, nb, stg, tqst, qb, kvb, tkv, acc, osend, dsend, orecv, drecv,
                 rrecv, rden, tsend, tden, trecv, tdrecv, afin, tfin, attn, text, wob, gsend, grecv,
                 load_sem, send_sem, x_sem, w_sem, own_sem, kv_sem, q_sem, t_sem, o_sem, r_sem, tr_sem,
                 attn_sem, text_sem, out_sem):
    x, y, z, c = coords()
    zh, zl = z // 2, lax.rem(z, 2)
    role = lax.rem(c + zh, 2)
    is0, is1 = role == 0, role == 1
    sibling = dev(x, y, z, 1 - c)
    partner = dev(x, y, z + 2, 1 - c)
    xp, xm = dev(x + 1, y, z, c), dev(x - 1, y, z, c)
    yps = {1: dev(x, y + 1, z, c), 2: dev(x, y - 1, z, c), 3: dev(x, y + 2, z, c)}
    zp, zm = dev(x, y, z + 1, c), dev(x, y, z - 1, c)

    load_x = pltpu.make_async_copy(x_ref, xb.at[c], load_sem.at[0])
    load_mod = [
        pltpu.make_async_copy(mod_ref.at[pl.ds(2 * i, 2)], part, load_sem.at[1 + i])
        for i, part in enumerate((mod0, mod1, mod2))]
    load_wv = [
        pltpu.make_async_copy(wv_ref.at[part], wvb.at[:, part * W : (part + 1) * W], load_sem.at[4 + part])
        for part in range(3)]
    load_xt = pltpu.make_async_copy(xt_ref, xtb, load_sem.at[7])
    load_wt = [
        pltpu.make_async_copy(wt_ref.at[part], wtb.at[pl.ds(part * D, D)], load_sem.at[8 + part])
        for part in range(3)]
    for copy in [load_x, load_mod[0]] + load_wv:
        copy.start()

    @pl.when(is0)
    def _():
        for copy in [load_xt] + load_wt:
            copy.start()

    load_mod[1].start()
    load_mod[2].start()

    barrier = pltpu.get_barrier_semaphore()
    for device in (sibling, xp, xm, yps[1], yps[2], yps[3], zp, zm, dev(x, y, z + 2, zh)):
        signal(barrier, device)

    @pl.when(is1)
    def _():
        signal(barrier, dev(x, y, z + 2, 1 - zh))

    step = step_ref[0]
    load_x.wait()
    load_mod[0].wait()
    shift, scale1 = mod0[0, pl.ds(step, 1), :], 1.0 + mod0[1, pl.ds(step, 1), :]
    norm_rows(xb.at[c], nb, 128 * c, 128, shift, scale1)
    pl.semaphore_wait(barrier, 9 + role)

    sends = Sends(send_sem, sibling)

    def arrived(dst, sem):
        pltpu.make_async_remote_copy(
            src_ref=dst, dst_ref=dst, send_sem=send_sem.at[0], recv_sem=sem,
            device_id=sibling, device_id_type=MESH).wait_recv()

    for rows, device, sem in ((pl.ds(0, 64), zm, x_sem.at[1]), (pl.ds(64, 64), zp, x_sem.at[2])):
        sends.start(lambda rows=rows: x_ref.at[rows], xb.at[2 + c, rows], sem, device)
    sends.start(x_ref, xb.at[c], x_sem.at[0], sibling)

    def q_half(pos, half):
        return qb.at[pl.ds(q_row(pos, half), HALF)]

    def send_queries(src, half, pred):
        for pos, back in ((3, 3), (1, 2), (2, 1)):
            sends.start(src, q_half(back, half), q_sem.at[back, half], yps[pos], pred)

    def send_keys(src, r, half, pred):
        sends.start(src, kvb.at[r, 2, half], kv_sem.at[r, 2, half, 0], xp, pred)
        sends.start(src, kvb.at[r, 1, half], kv_sem.at[r, 1, half, 0], xm, pred)
        sends.start(src, kvb.at[r, 0, half], kv_sem.at[r, 0, half, 0], sibling, pred)

    def stage_q(half):
        return stg.at[half, 0]

    def stage_kv(half):
        return stg.at[half, pl.ds(1, 2)]

    def send_half(half):
        copies = [
            pltpu.make_async_copy(stage_q(half), q_half(0, half), own_sem.at[half, 0]),
            pltpu.make_async_copy(stage_kv(half), kvb.at[0, 0, half], own_sem.at[half, 1])]
        for copy in copies:
            copy.start()
        send_keys(lambda: stage_kv(half), 0, half, is0)
        send_queries(lambda: stage_q(half), half, is0)
        for copy in copies:
            copy.wait()

    def swap_q(half):
        sends.start(lambda: stage_q(half), q_half(0, half), q_sem.at[0, half], partner, is1)

    def swap_kv(half):
        sends.start(lambda: stage_kv(half), kvb.at[1, 0, half], kv_sem.at[1, 0, half, 0], partner, is1)

    def swapped_q(half):
        arrived(q_half(0, half), q_sem.at[0, half])
        send_queries(lambda: q_half(0, half), half, is1)

    def swapped_kv(half):
        arrived(kvb.at[1, 0, half], kv_sem.at[1, 0, half, 0])
        send_keys(lambda: kvb.at[1, 0, half], 1, half, is1)

    def pass_on(r, half, pred):
        arrived(kvb.at[r, 1, half], kv_sem.at[r, 1, half, 0])
        sends.start(lambda: kvb.at[r, 1, half, 0], kvb.at[r, 3, half, 0], kv_sem.at[r, 3, half, 0], xm, pred)
        arrived(kvb.at[r, 2, half], kv_sem.at[r, 2, half, 0])
        sends.start(lambda: kvb.at[r, 2, half, 1], kvb.at[r, 3, half, 1], kv_sem.at[r, 3, half, 1], xp, pred)
        for pos in (1, 2):
            sends.start(lambda pos=pos: kvb.at[r, pos, half], kvb.at[r, pos, half],
                        kv_sem.at[r, pos, half, 0], sibling, pred)

    def pass_last(r, half, pred):
        for part in range(2):
            arrived(kvb.at[r, 3, half, part], kv_sem.at[r, 3, half, part])
        sends.start(lambda: kvb.at[r, 3, half], kvb.at[r, 3, half], kv_sem.at[r, 3, half, 0], sibling, pred)

    def from_sibling(r, blocks):
        for pos, half in blocks:
            arrived(kvb.at[r, pos, half], kv_sem.at[r, pos, half, 0])

    def on(pred, *steps):
        @pl.when(pred)
        def _():
            for step in steps:
                step()

    def over(blocks, q0, count, first=False):
        attend(qb, q0, count, [kvb.at[r, p, f, 0] for r, p, f in blocks],
               [kvb.at[r, p, f, 1] for r, p, f in blocks], acc, first)

    arrived(xb.at[1 - c], x_sem.at[0])
    norm_rows(xb.at[1 - c], nb, 128 * (1 - c), 128, shift, scale1)
    for copy in load_wv:
        copy.wait()
    project_wide(nb[...], wvb, stg.at[0], gains_ref[0:1, :], gains_ref[1:2, :])
    on(is0, lambda: send_half(0))
    on(is1, lambda: swap_q(0))
    ours = pl.ds(pl.multiple_of((2 * zl + c) * W, 16), W)
    theirs = pl.ds(pl.multiple_of((2 * zl + 1 - c) * W, 16), W)
    quarter = W // 4

    def send_weights(piece):
        for side, device in ((0, zp), (1, zm)):
            first_row = (2 * side + piece) * quarter
            place = pl.multiple_of((2 * zl + c) * W + first_row, 16)
            sends.start(lambda first_row=first_row: wov_ref.at[pl.ds(first_row, quarter)],
                        wob.at[pl.ds(place, quarter)], w_sem.at[2 + 2 * side + piece], device)

    def far_piece(core, k):
        return wob.at[pl.ds(pl.multiple_of((2 - 2 * zl + core) * W + k * quarter, 16), quarter)]

    def pass_weights(piece):
        for k in (piece, 2 + piece):
            arrived(far_piece(c, k), w_sem.at[2 + k])
            sends.start(lambda k=k: far_piece(c, k), far_piece(c, k), w_sem.at[6 + k], sibling)

    sends.start(wot_ref, wst_ref, w_sem.at[1], sibling)
    load_wo = pltpu.make_async_copy(wov_ref, wob.at[ours], load_sem.at[11])
    load_wo.start()
    load_mod[1].wait()
    load_mod[2].wait()

    tq_row = pl.multiple_of(64 * x, 64)
    tq_other = tqst.at[pl.ds(pl.multiple_of(64 * x + TQ, TQ), TQ)]
    tq_own = qb.at[pl.ds(TROW, TQ)]

    @pl.when(is0)
    def _():
        load_xt.wait()
        for copy in load_wt:
            copy.wait()
        norm_rows(xtb, nb, 0, TXT, mod1[1, pl.ds(step, 1), :], 1.0 + mod2[0, pl.ds(step, 1), :])
        project(nb[...], [wtb.at[pl.ds(part * D, D)] for part in range(3)],
                [tqst, tkv.at[0], tkv.at[1]], gains_ref[2:3, :], gains_ref[3:4, :])
        copy = pltpu.make_async_copy(tqst.at[pl.ds(tq_row, TQ)], tq_own, own_sem.at[2, 0])
        copy.start()
        sends.start(tq_other, tq_own, t_sem.at[0], sibling, is0)
        sends.start(tkv, tkv, t_sem.at[1], sibling, is0)
        copy.wait()

    arrived(xb.at[2 + c, pl.ds(0, 64)], x_sem.at[1])
    arrived(xb.at[2 + c, pl.ds(64, 64)], x_sem.at[2])
    sends.start(xb.at[2 + c], xb.at[2 + c], x_sem.at[3], sibling)
    on(is1, lambda: swap_kv(0), lambda: swapped_q(0))
    norm_rows(xb.at[2 + c], nb, 128 * c, 128, shift, scale1)
    arrived(xb.at[3 - c], x_sem.at[3])
    norm_rows(xb.at[3 - c], nb, 128 * (1 - c), 128, shift, scale1)
    on(is0, lambda: pass_on(0, 0, is0))
    project_wide(nb[...], wvb, stg.at[1], gains_ref[0:1, :], gains_ref[1:2, :])
    on(is0, lambda: send_half(1))
    on(is1, lambda: swap_q(1), lambda: swap_kv(1), lambda: swapped_kv(0))

    on(is0, lambda: pass_last(0, 0, is0))

    first_rows = q_row(ORDER[0], 0)

    def rows_of(base, size, i):
        return pl.multiple_of(base + i * size, 16)

    on(is1, lambda: from_sibling(0, [(0, 0), (1, 0), (2, 0)]))
    for pos in (1, 2, 3):
        arrived(q_half(pos, 0), q_sem.at[pos, 0])

    def first(i, carry):
        over([(0, 0, 0), (0, 1, 0), (0, 2, 0)], rows_of(first_rows, 512, i), 512, True)
        return carry

    lax.fori_loop(0, 2, first, 0)
    on(is0, lambda: from_sibling(1, [(0, 0)]))
    on(is1, lambda: swapped_q(1), lambda: from_sibling(0, [(0, 1)]))

    def second(i, carry):
        over([(0, 0, 1), (1, 0, 0)], rows_of(first_rows, 512, i), 512)
        return carry

    lax.fori_loop(0, 2, second, 0)
    on(is0, lambda: pass_on(0, 1, is0))
    on(is1, lambda: pass_on(1, 0, is1),
       lambda: arrived(tq_own, t_sem.at[0]), lambda: arrived(tkv, t_sem.at[1]))
    send_weights(0)

    arrived(wst_ref, w_sem.at[1])
    load_wo_text = []
    for i in range(8):
        cols = slice(i * W, (i + 1) * W)
        for k, (src, place) in enumerate(((wot_ref, c), (wst_ref, 1 - c))):
            rows = pl.ds(pl.multiple_of(i * 2 * W + place * W, 16), W)
            load_wo_text.append(pltpu.make_async_copy(
                src.at[:, cols], wtb.at[rows], load_sem.at[12 + 2 * i + k]))
    for copy in load_wo_text:
        copy.start()
    for pos in (1, 2, 3):
        arrived(q_half(pos, 1), q_sem.at[pos, 1])

    def third(i, carry):
        on(jnp.logical_and(i == 1, is1), lambda: swapped_kv(1))
        over([(0, 0, 0), (0, 1, 0), (0, 2, 0), (0, 0, 1), (1, 0, 0)], rows_of(0, 528, i), 528, True)
        return carry

    lax.fori_loop(0, 2, third, 0)
    send_weights(1)
    sends.start(wov_ref, wob.at[ours], w_sem.at[0], sibling)
    on(is1, lambda: pass_last(1, 0, is1),
       lambda: from_sibling(0, [(3, 0), (1, 1), (2, 1)]))
    on(is0, lambda: pass_last(0, 1, is0), lambda: from_sibling(1, [(1, 0), (2, 0), (0, 1)]))

    limit = len_ref[0]
    text_limit = jnp.where(y == 0, limit, 0)
    for q0, count, most in ((TROW, TQ, text_limit), (q_row(0, 1), HALF, limit), (q_row(0, 0), HALF, limit)):
        mask = lax.broadcasted_iota(jnp.int32, (count, TXT), 1) < most
        attend(qb, q0, count, [tkv.at[0]], [tkv.at[1]], acc, False, mask)

    middle_blocks = [(0, 3, 0), (0, 1, 1), (0, 2, 1), (1, 1, 0), (1, 2, 0), (1, 0, 1)]
    last_blocks = [(0, 3, 1), (1, 3, 0), (1, 1, 1), (1, 2, 1), (1, 3, 1)]

    def middle(i, carry):
        on(jnp.logical_and(i == 1, is1), lambda: pass_on(1, 1, is1))
        over(middle_blocks, rows_of(0, 528, i), 528)
        return carry

    lax.fori_loop(0, 2, middle, 0)
    on(is1, lambda: pass_last(1, 1, is1), lambda: from_sibling(0, [(3, 1)]))
    on(is0, lambda: from_sibling(1, [(3, 0), (1, 1), (2, 1), (3, 1)]))

    def fill_sums(pos, half):
        rows = pl.ds(q_row(pos, half), HALF)
        for h in range(NH):
            osend[pos - 1, half, :, h * HD : (h + 1) * HD] = acc[h, rows, :HD].astype(BF16)
        dsend[pos - 1, half] = jnp.transpose(coded_denoms(acc, rows))[:24]

    def send_far(half):
        fill_sums(3, half)
        for part, device in ((0, yps[1]), (1, yps[2])):
            cut = pl.ds(128 * part, 128)
            sends.start(lambda cut=cut: osend.at[2, half, cut], rrecv.at[part, half],
                        r_sem.at[part, half, 0], device)
            sends.start(lambda cut=cut: dsend.at[2, half, :, cut], rden.at[part, half],
                        r_sem.at[part, half, 1], device)

    def send_near(half):
        for pos, part in ((1, 0), (2, 1)):
            back = 1 - part
            fill_sums(pos, half)
            arrived(rrecv.at[part, half], r_sem.at[part, half, 0])
            arrived(rden.at[part, half], r_sem.at[part, half, 1])
            cut = slice(128 * part, 128 * part + 128)
            rows = pl.ds(q_row(pos, half) + 128 * part, 128)
            for h in range(NH):
                lanes = slice(h * HD, (h + 1) * HD)
                osend[pos - 1, half, cut, lanes] = (
                    acc[h, rows, :HD] + rrecv[part, half, :, lanes].astype(F32)).astype(BF16)
            dsend[pos - 1, half, :, cut] = dsend[pos - 1, half, :, cut] + rden[part, half]
            sends.start(lambda pos=pos: osend.at[pos - 1, half], orecv.at[back, half],
                        o_sem.at[back, half, 0], yps[pos])
            sends.start(lambda pos=pos: dsend.at[pos - 1, half], drecv.at[back, half],
                        o_sem.at[back, half, 1], yps[pos])

    acol = pl.ds(pl.multiple_of((2 * zl + zh) * W, HD), W)
    ahead = 1 - 2 * role

    def combine(half):
        for part in range(2):
            arrived(orecv.at[part, half], o_sem.at[part, half, 0])
            arrived(drecv.at[part, half], o_sem.at[part, half, 1])
        rows = pl.ds(q_row(0, half), HALF)
        denoms = drecv[0, half] + drecv[1, half]
        for h in range(NH):
            lanes = slice(h * HD, (h + 1) * HD)
            numer = acc[h, rows, :HD]
            for part in range(2):
                numer = numer + orecv[part, half, :, lanes].astype(F32)
            denom = acc[h, rows, HD:] + jnp.transpose(
                jnp.broadcast_to(denoms[8 * h : 8 * h + 1, :], (HD, HALF)))
            afin[half, :, lanes] = (numer / denom).astype(BF16)
        if half:
            for core in range(2):
                for first_row, step_z in ((0, ahead), (64, -ahead)):
                    rows = pl.ds(core * 128 + first_row, 64)
                    sends.start(lambda rows=rows: afin.at[half, rows],
                                attn.at[pl.ds(first_row, 64), acol], attn_sem.at[1],
                                dev(x, y, z + step_z, core))
            return
        for core in range(2):
            dst = attn.at[:, acol]
            across = jnp.logical_and(is0, c != core)

            def src(core=core):
                return afin.at[0, pl.ds(core * 128, 128)]

            @pl.when(is1)
            def _():
                sends.start(src, dst, attn_sem.at[0], dev(x, y, z + 2, core), is1)

            @pl.when(jnp.logical_and(is0, c == core))
            def _():
                pltpu.make_async_copy(src(), dst, attn_sem.at[0]).start()

            @pl.when(across)
            def _():
                sends.start(src, dst, attn_sem.at[0], sibling, across)

    over(last_blocks, TROW, TQ + HALF)

    trows = pl.ds(TROW, TQ)
    for h in range(NH):
        tsend[:, h * HD : (h + 1) * HD] = acc[h, trows, :HD].astype(BF16)
    tden[...] = coded_denoms(acc, trows)
    for pos, back in ((3, 3), (1, 2), (2, 1)):
        sends.start(tsend, trecv.at[back - 1], tr_sem.at[back - 1, 0], yps[pos])
        sends.start(tden, tdrecv.at[back - 1], tr_sem.at[back - 1, 1], yps[pos])
    send_far(1)
    over(last_blocks, q_row(1, 1), 512)
    over(last_blocks, q_row(0, 1), HALF)
    send_near(1)

    for pos in range(3):
        arrived(trecv.at[pos], tr_sem.at[pos, 0])
        arrived(tdrecv.at[pos], tr_sem.at[pos, 1])
    denoms = tden[...] + tdrecv[0] + tdrecv[1] + tdrecv[2]
    for h in range(NH):
        lanes = slice(h * HD, (h + 1) * HD)
        numer = acc[h, trows, :HD]
        for pos in range(3):
            numer = numer + trecv[pos, :, lanes].astype(F32)
        tfin[:, lanes] = (numer / denoms[:, 8 * h : 8 * h + 1]).astype(BF16)
    place = text.at[pl.ds(pl.multiple_of(lax.rem(x // 2, 2) * 64 + 32 * role, 32), TQ),
                    pl.ds(pl.multiple_of(zh * W, HD), W)]
    core_of = lax.rem(x, 2)
    for dx in range(4):
        for dz in range(2):
            if dx + dz:
                sends.start(tfin, place, text_sem.at[0], dev(x + dx, y, z + 2 * dz, core_of))
    elsewhere = core_of != c

    @pl.when(core_of == c)
    def _():
        pltpu.make_async_copy(tfin, place, text_sem.at[0]).start()

    @pl.when(elsewhere)
    def _():
        sends.start(tfin, place, text_sem.at[0], sibling, elsewhere)

    pass_weights(0)
    over(middle_blocks + last_blocks, q_row(3, 0), HALF)
    send_far(0)
    pass_weights(1)
    over(middle_blocks + last_blocks, q_row(1, 0), 512)
    send_near(0)
    combine(1)

    for copy in load_wo_text:
        copy.wait()
    arrived(text, text_sem.at[0])
    far_row = pl.multiple_of((1 - zl) * 64, 64)
    own_row = pl.multiple_of(zl * 64, 64)
    for i in range(8):
        weight = wtb[i * 2 * W : (i + 1) * 2 * W, :]
        gsend[:, i * W : (i + 1) * W] = jnp.dot(
            text[pl.ds(far_row, 64), :], weight, preferred_element_type=F32).astype(BF16)
    low, high = pl.ds(0, 32), pl.ds(32, 32)
    sends.start(gsend.at[low], grecv.at[low], out_sem.at[0], zp)
    sends.start(gsend.at[high], grecv.at[high], out_sem.at[0], zm)
    over(middle_blocks + last_blocks, q_row(0, 0), HALF)
    combine(0)
    row = lax.broadcasted_iota(jnp.int32, (64, W), 0) + (zl * 2 + c) * 64
    valid = row < len_ref[0]
    for i in range(8):
        cols = slice(i * W, (i + 1) * W)
        weight = wtb[i * 2 * W : (i + 1) * 2 * W, :]
        own = jnp.dot(text[pl.ds(own_row, 64), :], weight, preferred_element_type=F32)
        if i == 0:
            arrived(grecv, out_sem.at[0])
        gate = mod2[1, pl.ds(step, 1), cols]
        text_out_ref[:, cols] = jnp.where(
            valid, gate * (own + grecv[:, cols].astype(F32)), 0.0).astype(BF16)
    load_wo.wait()
    arrived(wob.at[theirs], w_sem.at[0])
    for k in range(4):
        arrived(far_piece(1 - c, k), w_sem.at[6 + k])
    for part, group in ((1, 1 - zl), (0, zl)):
        arrived(attn.at[:, pl.ds(pl.multiple_of(group * 2 * W, HD), 2 * W)], attn_sem.at[part])
    for i in range(NCH):
        cols = slice(i * CH, (i + 1) * CH)
        out = jnp.dot(attn[...], wob[:, cols], preferred_element_type=F32)
        video_out_ref[:, cols] = (mod1[0, pl.ds(step, 1), cols] * out).astype(BF16)
    sends.finish()


def place_kernel(video_ref, text_ref, video_out_ref, text_out_ref):
    video_out_ref[...] = video_ref[...]
    text_out_ref[...] = text_ref[...]


ANY = pl.BlockSpec(memory_space=pl.ANY)
VMEM = pl.BlockSpec(memory_space=pltpu.VMEM)
SMEM = pl.BlockSpec(memory_space=pltpu.SMEM)
DMA = pltpu.SemaphoreType.DMA


def body(x_video, x_text, w_qkv_video, w_qkv_text, w_out_video, w_out_text, qk_gains, modulation,
         text_len, timestep):
    wv = jnp.transpose(w_qkv_video, (1, 0, 2))
    wt = jnp.transpose(w_qkv_text, (1, 0, 2))
    mod = jnp.transpose(modulation, (1, 0, 2))
    shape = jax.ShapeDtypeStruct
    steps = modulation.shape[0]
    results = [shape((128, D), BF16), shape((64, D), BF16)]
    video, text, unused = pl.pallas_call(
        block_kernel,
        name="block",
        in_specs=[ANY, ANY, ANY, ANY, ANY, VMEM, ANY, ANY, SMEM, SMEM],
        out_specs=[VMEM, VMEM, ANY],
        out_shape=results + [shape((W, D), BF16)],
        scratch_shapes=[
            pltpu.VMEM((4, 128, D), BF16), pltpu.VMEM((TXT, D), BF16),
            pltpu.VMEM((D, 3 * W), BF16), pltpu.VMEM((3 * D, W), BF16),
            pltpu.VMEM((2, steps, D), F32), pltpu.VMEM((2, steps, D), F32), pltpu.VMEM((2, steps, D), F32),
            pltpu.VMEM((HALF, D), BF16),
            pltpu.VMEM((2, 3, HALF, W), BF16), pltpu.VMEM((TXT, W), BF16),
            pltpu.VMEM((QROWS, W), BF16), pltpu.VMEM((2, 4, 2, 2, HALF, W), BF16),
            pltpu.VMEM((2, TXT, W), BF16), pltpu.VMEM((NH, QROWS, 2 * HD), F32),
            pltpu.VMEM((3, 2, HALF, W), BF16), pltpu.VMEM((3, 2, 24, HALF), F32),
            pltpu.VMEM((2, 2, HALF, W), BF16), pltpu.VMEM((2, 2, 24, HALF), F32),
            pltpu.VMEM((2, 2, 128, W), BF16), pltpu.VMEM((2, 2, 24, 128), F32),
            pltpu.VMEM((TQ, W), BF16), pltpu.VMEM((TQ, HD), F32),
            pltpu.VMEM((3, TQ, W), BF16), pltpu.VMEM((3, TQ, HD), F32),
            pltpu.VMEM((2, HALF, W), BF16), pltpu.VMEM((TQ, W), BF16),
            pltpu.VMEM((128, 4 * W), BF16), pltpu.VMEM((128, 2 * W), BF16), pltpu.VMEM((4 * W, D), BF16),
            pltpu.VMEM((64, D), BF16), pltpu.VMEM((64, D), BF16),
            DMA((28,)), DMA((136,)), DMA((4,)), DMA((10,)), DMA((3, 2)), DMA((2, 4, 2, 2)), DMA((4, 2)),
            DMA((2,)), DMA((2, 2, 2)), DMA((2, 2, 2)), DMA((3, 2)), DMA((2,)), DMA((1,)), DMA((1,))],
        compiler_params=pltpu.CompilerParams(
            collective_id=1, has_side_effects=True, vmem_limit_bytes=VMEM_LIMIT),
    )(x_video, x_text, wv, wt, mod, qk_gains, w_out_video, w_out_text, text_len, timestep)
    return tuple(pl.pallas_call(
        place_kernel,
        name="place",
        in_specs=[VMEM, VMEM],
        out_specs=[VMEM, VMEM],
        out_shape=results,
    )(video, text))


def solution(mesh):
    grid = Mesh(mesh.devices.reshape(4, 4, 2, 2, 2), AXES)
    head = ("zl", "c")
    return jax.shard_map(
        body,
        mesh=grid,
        in_specs=(P(AXES, None), P(), P(None, None, head), P(None, None, head),
                  P(head, None), P(head, None), P(), P(), P(), P()),
        out_specs=(P(AXES, None), P(head, None)),
        check_vma=False,
    )
```

```python
import functools
import math

import jax
import jax.numpy as jnp
from jax import lax
from jax.experimental import pallas as pl
from jax.experimental.pallas import tpu as pltpu
from jax.sharding import Mesh, PartitionSpec as P

AXES = ("x", "y", "zh", "zl", "c")
MESH = pl.DeviceIdType.MESH
BF16, F32 = jnp.bfloat16, jnp.float32
D = 3072
HD = 128
NH = 3
W = NH * HD
HALF = 256
TXT = 256
TQ = 32
QROWS = 8 * HALF + TQ
ORDER = (3, 1, 2, 0)
CH = 768
NCH = D // CH
EXP_SCALE = math.log2(math.e) / math.sqrt(HD)
VMEM_LIMIT = 60 << 20


def coords():
    x, y, zh, zl, c = (lax.axis_index(a) for a in AXES)
    return x, y, zh * 2 + zl, c


def dev(x, y, z, c):
    z = lax.rem(z + 4, 4)
    return (lax.rem(x + 4, 4), lax.rem(y + 4, 4), z // 2, lax.rem(z, 2), c)


class Sends:
    def __init__(self, sems, peer):
        self.sems, self.peer, self.count, self.pending = sems, peer, 0, []

    def start(self, src, dst, recv_sem, device, pred=None):
        slot = self.count
        self.count += 1
        get = src if callable(src) else (lambda: src)

        pltpu.make_async_remote_copy(
            src_ref=get(), dst_ref=dst, send_sem=self.sems.at[slot], recv_sem=recv_sem,
            device_id=device, device_id_type=MESH).start()

        def wait():
            pltpu.make_async_remote_copy(
                src_ref=get(), dst_ref=get(), send_sem=self.sems.at[slot], recv_sem=self.sems.at[slot],
                device_id=self.peer, device_id_type=MESH).wait_send()

        self.pending.append((pred, wait))

    def finish(self):
        for pred, wait in self.pending:
            if pred is None:
                wait()
            else:
                pl.when(pred)(wait)


def signal(sem, device):
    pl.semaphore_signal(sem, inc=1, device_id=device, device_id_type=MESH)


def norm_rows(src, dst, dst_row, count, shift, scale1):
    def strip(i, carry):
        wide = src[pl.ds(pl.multiple_of(i * 16, 16), 16), :].astype(F32)
        centred = wide - jnp.mean(wide, axis=-1, keepdims=True)
        variance = jnp.mean(centred * centred, axis=-1, keepdims=True)
        out = centred * lax.rsqrt(variance + 1e-06) * scale1 + shift
        dst[pl.ds(pl.multiple_of(dst_row + i * 16, 16), 16), :] = out.astype(BF16)
        return carry

    lax.fori_loop(0, count // 16, strip, 0, unroll=2)


def project(rows, weights, outs, gain_query, gain_key):
    for part in range(3):
        flat = jnp.dot(rows, weights[part][...], preferred_element_type=F32)
        for h in range(NH):
            lanes = slice(h * HD, (h + 1) * HD)
            u = flat[:, lanes]
            if part < 2:
                gain = gain_query if part == 0 else gain_key
                meansq = jnp.mean(u * u, axis=-1, keepdims=True)
                u = u * lax.rsqrt(meansq + 1e-06) * gain
            outs[part][:, lanes] = u.astype(BF16)


def project_wide(rows, weight, out, gain_query, gain_key):
    flat = jnp.dot(rows, weight[...], preferred_element_type=F32)
    for part in range(3):
        for h in range(NH):
            u = flat[:, part * W + h * HD : part * W + (h + 1) * HD]
            if part < 2:
                gain = gain_query if part == 0 else gain_key
                meansq = jnp.mean(u * u, axis=-1, keepdims=True)
                u = u * lax.rsqrt(meansq + 1e-06) * gain
            out[part, :, h * HD : (h + 1) * HD] = u.astype(BF16)


def attend(qb, q0, count, keys, values, acc, first, mask=None):
    for h in range(NH):
        lanes = slice(h * HD, (h + 1) * HD)
        query = qb[pl.ds(q0, count), lanes]
        total = None
        for key_ref, value_ref in zip(keys, values):
            scores = lax.dot_general(
                query, key_ref[:, lanes], (((1,), (1,)), ((), ())), preferred_element_type=F32)
            expo = jnp.exp2(scores * EXP_SCALE)
            if mask is not None:
                expo = jnp.where(mask, expo, 0.0)
            value = value_ref[:, lanes]
            wide = jnp.concatenate([value, jnp.ones_like(value)], axis=1)
            part = jnp.dot(expo.astype(BF16), wide, preferred_element_type=F32)
            total = part if total is None else total + part
        if first:
            acc[h, pl.ds(q0, count), :] = total
        else:
            acc[h, pl.ds(q0, count), :] += total


def coded_denoms(acc, rows):
    parts = [acc[h, rows, HD:] for h in range(NH)]
    lane = lax.broadcasted_iota(jnp.int32, parts[0].shape, 1)
    return jnp.where(lane < 8, parts[0], jnp.where(lane < 16, parts[1], parts[2]))


def q_row(pos, half):
    return TQ + ORDER.index(pos) * HALF + (0 if half else 4 * HALF)


TROW = 0


def block_kernel(x_ref, xt_ref, wv_ref, wt_ref, mod_ref, gains_ref, wov_ref, wot_ref, len_ref, step_ref,
                 video_out_ref, text_out_ref, wst_ref,
                 xb, xtb, wvb, wtb, mod0, mod1, mod2, nb, stg, tqst, qb, kvb, tkv, acc, osend, dsend, orecv, drecv,
                 rrecv, rden, tsend, tden, trecv, tdrecv, afin, tfin, attn, text, wob, gsend, grecv,
                 load_sem, send_sem, x_sem, w_sem, own_sem, kv_sem, q_sem, t_sem, o_sem, r_sem, tr_sem,
                 attn_sem, text_sem, out_sem):
    x, y, z, c = coords()
    zh, zl = z // 2, lax.rem(z, 2)
    role = lax.rem(c + zh, 2)
    is0, is1 = role == 0, role == 1
    sibling = dev(x, y, z, 1 - c)
    partner = dev(x, y, z + 2, 1 - c)
    xp, xm = dev(x + 1, y, z, c), dev(x - 1, y, z, c)
    yps = {1: dev(x, y + 1, z, c), 2: dev(x, y - 1, z, c), 3: dev(x, y + 2, z, c)}
    zp, zm = dev(x, y, z + 1, c), dev(x, y, z - 1, c)

    load_x = pltpu.make_async_copy(x_ref, xb.at[c], load_sem.at[0])
    load_mod = [
        pltpu.make_async_copy(mod_ref.at[pl.ds(2 * i, 2)], part, load_sem.at[1 + i])
        for i, part in enumerate((mod0, mod1, mod2))]
    load_wv = [
        pltpu.make_async_copy(wv_ref.at[part], wvb.at[:, part * W : (part + 1) * W], load_sem.at[4 + part])
        for part in range(3)]
    load_xt = pltpu.make_async_copy(xt_ref, xtb, load_sem.at[7])
    load_wt = [
        pltpu.make_async_copy(wt_ref.at[part], wtb.at[pl.ds(part * D, D)], load_sem.at[8 + part])
        for part in range(3)]
    for copy in [load_x, load_mod[0]] + load_wv:
        copy.start()

    @pl.when(is0)
    def _():
        for copy in [load_xt] + load_wt:
            copy.start()

    load_mod[1].start()
    load_mod[2].start()

    barrier = pltpu.get_barrier_semaphore()
    for device in (sibling, xp, xm, yps[1], yps[2], yps[3], zp, zm, dev(x, y, z + 2, zh)):
        signal(barrier, device)

    @pl.when(is1)
    def _():
        signal(barrier, dev(x, y, z + 2, 1 - zh))

    step = step_ref[0]
    load_x.wait()
    load_mod[0].wait()
    shift, scale1 = mod0[0, pl.ds(step, 1), :], 1.0 + mod0[1, pl.ds(step, 1), :]
    norm_rows(xb.at[c], nb, 128 * c, 128, shift, scale1)
    pl.semaphore_wait(barrier, 9 + role)

    sends = Sends(send_sem, sibling)

    def arrived(dst, sem):
        pltpu.make_async_remote_copy(
            src_ref=dst, dst_ref=dst, send_sem=send_sem.at[0], recv_sem=sem,
            device_id=sibling, device_id_type=MESH).wait_recv()

    for rows, device, sem in ((pl.ds(0, 64), zm, x_sem.at[1]), (pl.ds(64, 64), zp, x_sem.at[2])):
        sends.start(lambda rows=rows: x_ref.at[rows], xb.at[2 + c, rows], sem, device)
    sends.start(x_ref, xb.at[c], x_sem.at[0], sibling)

    def q_half(pos, half):
        return qb.at[pl.ds(q_row(pos, half), HALF)]

    def send_queries(src, half, pred):
        for pos, back in ((3, 3), (1, 2), (2, 1)):
            sends.start(src, q_half(back, half), q_sem.at[back, half], yps[pos], pred)

    def send_keys(src, r, half, pred):
        sends.start(src, kvb.at[r, 2, half], kv_sem.at[r, 2, half, 0], xp, pred)
        sends.start(src, kvb.at[r, 1, half], kv_sem.at[r, 1, half, 0], xm, pred)
        sends.start(src, kvb.at[r, 0, half], kv_sem.at[r, 0, half, 0], sibling, pred)

    def stage_q(half):
        return stg.at[half, 0]

    def stage_kv(half):
        return stg.at[half, pl.ds(1, 2)]

    def send_half(half):
        copies = [
            pltpu.make_async_copy(stage_q(half), q_half(0, half), own_sem.at[half, 0]),
            pltpu.make_async_copy(stage_kv(half), kvb.at[0, 0, half], own_sem.at[half, 1])]
        for copy in copies:
            copy.start()
        send_keys(lambda: stage_kv(half), 0, half, is0)
        if half == 0:
            send_queries(lambda: stage_q(half), half, is0)
        for copy in copies:
            copy.wait()

    def swap_q(half):
        sends.start(lambda: stage_q(half), q_half(0, half), q_sem.at[0, half], partner, is1)

    def swap_kv(half):
        sends.start(lambda: stage_kv(half), kvb.at[1, 0, half], kv_sem.at[1, 0, half, 0], partner, is1)

    def swapped_q(half):
        arrived(q_half(0, half), q_sem.at[0, half])
        send_queries(lambda: q_half(0, half), half, is1)

    def swapped_kv(half):
        arrived(kvb.at[1, 0, half], kv_sem.at[1, 0, half, 0])
        send_keys(lambda: kvb.at[1, 0, half], 1, half, is1)

    def pass_on(r, half, pred):
        arrived(kvb.at[r, 1, half], kv_sem.at[r, 1, half, 0])
        sends.start(lambda: kvb.at[r, 1, half, 0], kvb.at[r, 3, half, 0], kv_sem.at[r, 3, half, 0], xm, pred)
        arrived(kvb.at[r, 2, half], kv_sem.at[r, 2, half, 0])
        sends.start(lambda: kvb.at[r, 2, half, 1], kvb.at[r, 3, half, 1], kv_sem.at[r, 3, half, 1], xp, pred)
        for pos in (1, 2):
            sends.start(lambda pos=pos: kvb.at[r, pos, half], kvb.at[r, pos, half],
                        kv_sem.at[r, pos, half, 0], sibling, pred)

    def pass_last(r, half, pred):
        for part in range(2):
            arrived(kvb.at[r, 3, half, part], kv_sem.at[r, 3, half, part])
        sends.start(lambda: kvb.at[r, 3, half], kvb.at[r, 3, half], kv_sem.at[r, 3, half, 0], sibling, pred)

    def from_sibling(r, blocks):
        for pos, half in blocks:
            arrived(kvb.at[r, pos, half], kv_sem.at[r, pos, half, 0])

    def on(pred, *steps):
        @pl.when(pred)
        def _():
            for step in steps:
                step()

    def over(blocks, q0, count, first=False):
        attend(qb, q0, count, [kvb.at[r, p, f, 0] for r, p, f in blocks],
               [kvb.at[r, p, f, 1] for r, p, f in blocks], acc, first)

    arrived(xb.at[1 - c], x_sem.at[0])
    norm_rows(xb.at[1 - c], nb, 128 * (1 - c), 128, shift, scale1)
    for copy in load_wv:
        copy.wait()
    project_wide(nb[...], wvb, stg.at[0], gains_ref[0:1, :], gains_ref[1:2, :])
    on(is0, lambda: send_half(0))
    on(is1, lambda: swap_q(0))
    ours = pl.ds(pl.multiple_of((2 * zl + c) * W, 16), W)
    theirs = pl.ds(pl.multiple_of((2 * zl + 1 - c) * W, 16), W)
    quarter = W // 4

    def send_weights(piece):
        for side, device in ((0, zp), (1, zm)):
            first_row = (2 * side + piece) * quarter
            place = pl.multiple_of((2 * zl + c) * W + first_row, 16)
            sends.start(lambda first_row=first_row: wov_ref.at[pl.ds(first_row, quarter)],
                        wob.at[pl.ds(place, quarter)], w_sem.at[2 + 2 * side + piece], device)

    def far_piece(core, k):
        return wob.at[pl.ds(pl.multiple_of((2 - 2 * zl + core) * W + k * quarter, 16), quarter)]

    def pass_weights(piece):
        for k in (piece, 2 + piece):
            arrived(far_piece(c, k), w_sem.at[2 + k])
            sends.start(lambda k=k: far_piece(c, k), far_piece(c, k), w_sem.at[6 + k], sibling)

    sends.start(wot_ref, wst_ref, w_sem.at[1], sibling)
    load_wo = pltpu.make_async_copy(wov_ref, wob.at[ours], load_sem.at[11])
    load_wo.start()
    load_mod[1].wait()
    load_mod[2].wait()

    tq_row = pl.multiple_of(64 * x, 64)
    tq_other = tqst.at[pl.ds(pl.multiple_of(64 * x + TQ, TQ), TQ)]
    tq_own = qb.at[pl.ds(TROW, TQ)]

    @pl.when(is0)
    def _():
        load_xt.wait()
        for copy in load_wt:
            copy.wait()
        norm_rows(xtb, nb, 0, TXT, mod1[1, pl.ds(step, 1), :], 1.0 + mod2[0, pl.ds(step, 1), :])
        project(nb[...], [wtb.at[pl.ds(part * D, D)] for part in range(3)],
                [tqst, tkv.at[0], tkv.at[1]], gains_ref[2:3, :], gains_ref[3:4, :])
        copy = pltpu.make_async_copy(tqst.at[pl.ds(tq_row, TQ)], tq_own, own_sem.at[2, 0])
        copy.start()
        sends.start(tq_other, tq_own, t_sem.at[0], sibling, is0)
        sends.start(tkv, tkv, t_sem.at[1], sibling, is0)
        copy.wait()

    arrived(xb.at[2 + c, pl.ds(0, 64)], x_sem.at[1])
    arrived(xb.at[2 + c, pl.ds(64, 64)], x_sem.at[2])
    sends.start(xb.at[2 + c], xb.at[2 + c], x_sem.at[3], sibling)
    on(is1, lambda: swap_kv(0))
    norm_rows(xb.at[2 + c], nb, 128 * c, 128, shift, scale1)
    on(is1, lambda: swapped_q(0))
    arrived(xb.at[3 - c], x_sem.at[3])
    norm_rows(xb.at[3 - c], nb, 128 * (1 - c), 128, shift, scale1)
    on(is0, lambda: pass_on(0, 0, is0))
    project_wide(nb[...], wvb, stg.at[1], gains_ref[0:1, :], gains_ref[1:2, :])
    on(is0, lambda: send_half(1))
    on(is1, lambda: swap_q(1), lambda: swap_kv(1), lambda: swapped_kv(0))

    first_rows = q_row(ORDER[0], 0)

    def rows_of(base, size, i):
        return pl.multiple_of(base + i * size, 16)

    on(is1, lambda: from_sibling(0, [(0, 0), (1, 0), (2, 0)]))
    for pos in (1, 2, 3):
        arrived(q_half(pos, 0), q_sem.at[pos, 0])

    def first(i, carry):
        on(jnp.logical_and(i == 1, is0), lambda: send_queries(lambda: stage_q(1), 1, is0),
           lambda: pass_last(0, 0, is0))
        on(jnp.logical_and(i == 1, is1), lambda: swapped_q(1))
        over([(0, 0, 0), (0, 1, 0), (0, 2, 0)], rows_of(first_rows, 512, i), 512, True)
        return carry

    lax.fori_loop(0, 2, first, 0)
    on(is0, lambda: from_sibling(1, [(0, 0)]))
    on(is1, lambda: from_sibling(0, [(3, 0), (0, 1)]))

    def second(i, carry):
        over([(0, 3, 0), (0, 0, 1), (1, 0, 0)], rows_of(first_rows, 512, i), 512)
        return carry

    lax.fori_loop(0, 2, second, 0)
    on(is0, lambda: pass_on(0, 1, is0))
    on(is1, lambda: pass_on(1, 0, is1),
       lambda: arrived(tq_own, t_sem.at[0]), lambda: arrived(tkv, t_sem.at[1]))
    send_weights(0)

    arrived(wst_ref, w_sem.at[1])
    load_wo_text = []
    for i in range(8):
        cols = slice(i * W, (i + 1) * W)
        for k, (src, place) in enumerate(((wot_ref, c), (wst_ref, 1 - c))):
            rows = pl.ds(pl.multiple_of(i * 2 * W + place * W, 16), W)
            load_wo_text.append(pltpu.make_async_copy(
                src.at[:, cols], wtb.at[rows], load_sem.at[12 + 2 * i + k]))
    for copy in load_wo_text:
        copy.start()
    for pos in (1, 2, 3):
        arrived(q_half(pos, 1), q_sem.at[pos, 1])

    def third(i, carry):
        on(jnp.logical_and(i == 1, is1), lambda: swapped_kv(1))
        over([(0, 0, 0), (0, 1, 0), (0, 2, 0), (0, 3, 0), (0, 0, 1), (1, 0, 0)],
             rows_of(0, 528, i), 528, True)
        return carry

    lax.fori_loop(0, 2, third, 0)
    send_weights(1)
    sends.start(wov_ref, wob.at[ours], w_sem.at[0], sibling)
    on(is1, lambda: pass_last(1, 0, is1),
       lambda: from_sibling(0, [(1, 1), (2, 1)]))
    on(is0, lambda: pass_last(0, 1, is0), lambda: from_sibling(1, [(1, 0), (2, 0), (0, 1)]))

    limit = len_ref[0]
    text_limit = jnp.where(y == 0, limit, 0)
    for q0, count, most in ((TROW, TQ, text_limit), (q_row(0, 1), HALF, limit), (q_row(0, 0), HALF, limit)):
        mask = lax.broadcasted_iota(jnp.int32, (count, TXT), 1) < most
        attend(qb, q0, count, [tkv.at[0]], [tkv.at[1]], acc, False, mask)

    middle_blocks = [(0, 1, 1), (0, 2, 1), (1, 1, 0), (1, 2, 0), (1, 0, 1)]
    last_blocks = [(0, 3, 1), (1, 3, 0), (1, 1, 1), (1, 2, 1), (1, 3, 1)]

    def middle(i, carry):
        on(jnp.logical_and(i == 1, is1), lambda: pass_on(1, 1, is1))
        over(middle_blocks, rows_of(0, 528, i), 528)
        return carry

    lax.fori_loop(0, 2, middle, 0)
    on(is1, lambda: pass_last(1, 1, is1), lambda: from_sibling(0, [(3, 1)]))
    on(is0, lambda: from_sibling(1, [(3, 0), (1, 1), (2, 1), (3, 1)]))

    def fill_sums(pos, half):
        rows = pl.ds(q_row(pos, half), HALF)
        for h in range(NH):
            osend[pos - 1, half, :, h * HD : (h + 1) * HD] = acc[h, rows, :HD].astype(BF16)
        dsend[pos - 1, half] = jnp.transpose(coded_denoms(acc, rows))[:24]

    def send_far(half):
        fill_sums(3, half)
        for part, device in ((0, yps[1]), (1, yps[2])):
            cut = pl.ds(128 * part, 128)
            sends.start(lambda cut=cut: osend.at[2, half, cut], rrecv.at[part, half],
                        r_sem.at[part, half, 0], device)
            sends.start(lambda cut=cut: dsend.at[2, half, :, cut], rden.at[part, half],
                        r_sem.at[part, half, 1], device)

    def send_near(half):
        for pos, part in ((1, 0), (2, 1)):
            back = 1 - part
            fill_sums(pos, half)
            arrived(rrecv.at[part, half], r_sem.at[part, half, 0])
            arrived(rden.at[part, half], r_sem.at[part, half, 1])
            cut = slice(128 * part, 128 * part + 128)
            rows = pl.ds(q_row(pos, half) + 128 * part, 128)
            for h in range(NH):
                lanes = slice(h * HD, (h + 1) * HD)
                osend[pos - 1, half, cut, lanes] = (
                    acc[h, rows, :HD] + rrecv[part, half, :, lanes].astype(F32)).astype(BF16)
            dsend[pos - 1, half, :, cut] = dsend[pos - 1, half, :, cut] + rden[part, half]
            sends.start(lambda pos=pos: osend.at[pos - 1, half], orecv.at[back, half],
                        o_sem.at[back, half, 0], yps[pos])
            sends.start(lambda pos=pos: dsend.at[pos - 1, half], drecv.at[back, half],
                        o_sem.at[back, half, 1], yps[pos])

    acol = pl.ds(pl.multiple_of((2 * zl + zh) * W, HD), W)
    ahead = 1 - 2 * role

    def combine(half):
        for part in range(2):
            arrived(orecv.at[part, half], o_sem.at[part, half, 0])
            arrived(drecv.at[part, half], o_sem.at[part, half, 1])
        rows = pl.ds(q_row(0, half), HALF)
        denoms = drecv[0, half] + drecv[1, half]
        for h in range(NH):
            lanes = slice(h * HD, (h + 1) * HD)
            numer = acc[h, rows, :HD]
            for part in range(2):
                numer = numer + orecv[part, half, :, lanes].astype(F32)
            denom = acc[h, rows, HD:] + jnp.transpose(
                jnp.broadcast_to(denoms[8 * h : 8 * h + 1, :], (HD, HALF)))
            afin[half, :, lanes] = (numer / denom).astype(BF16)
        if half:
            for core in range(2):
                for first_row, step_z in ((0, ahead), (64, -ahead)):
                    rows = pl.ds(core * 128 + first_row, 64)
                    sends.start(lambda rows=rows: afin.at[half, rows],
                                attn.at[pl.ds(first_row, 64), acol], attn_sem.at[1],
                                dev(x, y, z + step_z, core))
            return
        for core in range(2):
            dst = attn.at[:, acol]
            across = jnp.logical_and(is0, c != core)

            def src(core=core):
                return afin.at[0, pl.ds(core * 128, 128)]

            @pl.when(is1)
            def _():
                sends.start(src, dst, attn_sem.at[0], dev(x, y, z + 2, core), is1)

            @pl.when(jnp.logical_and(is0, c == core))
            def _():
                pltpu.make_async_copy(src(), dst, attn_sem.at[0]).start()

            @pl.when(across)
            def _():
                sends.start(src, dst, attn_sem.at[0], sibling, across)

    over(last_blocks, TROW, TQ + HALF)

    trows = pl.ds(TROW, TQ)
    for h in range(NH):
        tsend[:, h * HD : (h + 1) * HD] = acc[h, trows, :HD].astype(BF16)
    tden[...] = coded_denoms(acc, trows)
    for pos, back in ((3, 3), (1, 2), (2, 1)):
        sends.start(tsend, trecv.at[back - 1], tr_sem.at[back - 1, 0], yps[pos])
        sends.start(tden, tdrecv.at[back - 1], tr_sem.at[back - 1, 1], yps[pos])
    send_far(1)
    over(last_blocks, q_row(1, 1), 512)
    over(last_blocks, q_row(0, 1), HALF)
    send_near(1)

    for pos in range(3):
        arrived(trecv.at[pos], tr_sem.at[pos, 0])
        arrived(tdrecv.at[pos], tr_sem.at[pos, 1])
    denoms = tden[...] + tdrecv[0] + tdrecv[1] + tdrecv[2]
    for h in range(NH):
        lanes = slice(h * HD, (h + 1) * HD)
        numer = acc[h, trows, :HD]
        for pos in range(3):
            numer = numer + trecv[pos, :, lanes].astype(F32)
        tfin[:, lanes] = (numer / denoms[:, 8 * h : 8 * h + 1]).astype(BF16)
    place = text.at[pl.ds(pl.multiple_of(lax.rem(x // 2, 2) * 64 + 32 * role, 32), TQ),
                    pl.ds(pl.multiple_of(zh * W, HD), W)]
    core_of = lax.rem(x, 2)
    for dx in range(4):
        for dz in range(2):
            if dx + dz:
                sends.start(tfin, place, text_sem.at[0], dev(x + dx, y, z + 2 * dz, core_of))
    elsewhere = core_of != c

    @pl.when(core_of == c)
    def _():
        pltpu.make_async_copy(tfin, place, text_sem.at[0]).start()

    @pl.when(elsewhere)
    def _():
        sends.start(tfin, place, text_sem.at[0], sibling, elsewhere)

    pass_weights(0)
    over(middle_blocks + last_blocks, q_row(3, 0), HALF)
    send_far(0)
    pass_weights(1)
    over(middle_blocks + last_blocks, q_row(1, 0), 512)
    send_near(0)
    combine(1)

    for copy in load_wo_text:
        copy.wait()
    arrived(text, text_sem.at[0])
    far_row = pl.multiple_of((1 - zl) * 64, 64)
    own_row = pl.multiple_of(zl * 64, 64)
    for i in range(8):
        weight = wtb[i * 2 * W : (i + 1) * 2 * W, :]
        gsend[:, i * W : (i + 1) * W] = jnp.dot(
            text[pl.ds(far_row, 64), :], weight, preferred_element_type=F32).astype(BF16)
    low, high = pl.ds(0, 32), pl.ds(32, 32)
    sends.start(gsend.at[low], grecv.at[low], out_sem.at[0], zp)
    sends.start(gsend.at[high], grecv.at[high], out_sem.at[0], zm)
    over(middle_blocks + last_blocks, q_row(0, 0), HALF)
    combine(0)
    row = lax.broadcasted_iota(jnp.int32, (64, W), 0) + (zl * 2 + c) * 64
    valid = row < len_ref[0]
    for i in range(8):
        cols = slice(i * W, (i + 1) * W)
        weight = wtb[i * 2 * W : (i + 1) * 2 * W, :]
        own = jnp.dot(text[pl.ds(own_row, 64), :], weight, preferred_element_type=F32)
        if i == 0:
            arrived(grecv, out_sem.at[0])
        gate = mod2[1, pl.ds(step, 1), cols]
        text_out_ref[:, cols] = jnp.where(
            valid, gate * (own + grecv[:, cols].astype(F32)), 0.0).astype(BF16)
    load_wo.wait()
    arrived(wob.at[theirs], w_sem.at[0])
    for k in range(4):
        arrived(far_piece(1 - c, k), w_sem.at[6 + k])
    for part, group in ((1, 1 - zl), (0, zl)):
        arrived(attn.at[:, pl.ds(pl.multiple_of(group * 2 * W, HD), 2 * W)], attn_sem.at[part])
    for i in range(NCH):
        cols = slice(i * CH, (i + 1) * CH)
        out = jnp.dot(attn[...], wob[:, cols], preferred_element_type=F32)
        video_out_ref[:, cols] = (mod1[0, pl.ds(step, 1), cols] * out).astype(BF16)
    sends.finish()


def place_kernel(video_ref, text_ref, video_out_ref, text_out_ref):
    video_out_ref[...] = video_ref[...]
    text_out_ref[...] = text_ref[...]


ANY = pl.BlockSpec(memory_space=pl.ANY)
VMEM = pl.BlockSpec(memory_space=pltpu.VMEM)
SMEM = pl.BlockSpec(memory_space=pltpu.SMEM)
DMA = pltpu.SemaphoreType.DMA


def body(x_video, x_text, w_qkv_video, w_qkv_text, w_out_video, w_out_text, qk_gains, modulation,
         text_len, timestep):
    wv = jnp.transpose(w_qkv_video, (1, 0, 2))
    wt = jnp.transpose(w_qkv_text, (1, 0, 2))
    mod = jnp.transpose(modulation, (1, 0, 2))
    shape = jax.ShapeDtypeStruct
    steps = modulation.shape[0]
    results = [shape((128, D), BF16), shape((64, D), BF16)]
    video, text, unused = pl.pallas_call(
        block_kernel,
        name="block",
        in_specs=[ANY, ANY, ANY, ANY, ANY, VMEM, ANY, ANY, SMEM, SMEM],
        out_specs=[VMEM, VMEM, ANY],
        out_shape=results + [shape((W, D), BF16)],
        scratch_shapes=[
            pltpu.VMEM((4, 128, D), BF16), pltpu.VMEM((TXT, D), BF16),
            pltpu.VMEM((D, 3 * W), BF16), pltpu.VMEM((3 * D, W), BF16),
            pltpu.VMEM((2, steps, D), F32), pltpu.VMEM((2, steps, D), F32), pltpu.VMEM((2, steps, D), F32),
            pltpu.VMEM((HALF, D), BF16),
            pltpu.VMEM((2, 3, HALF, W), BF16), pltpu.VMEM((TXT, W), BF16),
            pltpu.VMEM((QROWS, W), BF16), pltpu.VMEM((2, 4, 2, 2, HALF, W), BF16),
            pltpu.VMEM((2, TXT, W), BF16), pltpu.VMEM((NH, QROWS, 2 * HD), F32),
            pltpu.VMEM((3, 2, HALF, W), BF16), pltpu.VMEM((3, 2, 24, HALF), F32),
            pltpu.VMEM((2, 2, HALF, W), BF16), pltpu.VMEM((2, 2, 24, HALF), F32),
            pltpu.VMEM((2, 2, 128, W), BF16), pltpu.VMEM((2, 2, 24, 128), F32),
            pltpu.VMEM((TQ, W), BF16), pltpu.VMEM((TQ, HD), F32),
            pltpu.VMEM((3, TQ, W), BF16), pltpu.VMEM((3, TQ, HD), F32),
            pltpu.VMEM((2, HALF, W), BF16), pltpu.VMEM((TQ, W), BF16),
            pltpu.VMEM((128, 4 * W), BF16), pltpu.VMEM((128, 2 * W), BF16), pltpu.VMEM((4 * W, D), BF16),
            pltpu.VMEM((64, D), BF16), pltpu.VMEM((64, D), BF16),
            DMA((28,)), DMA((136,)), DMA((4,)), DMA((10,)), DMA((3, 2)), DMA((2, 4, 2, 2)), DMA((4, 2)),
            DMA((2,)), DMA((2, 2, 2)), DMA((2, 2, 2)), DMA((3, 2)), DMA((2,)), DMA((1,)), DMA((1,))],
        compiler_params=pltpu.CompilerParams(
            collective_id=1, has_side_effects=True, vmem_limit_bytes=VMEM_LIMIT),
    )(x_video, x_text, wv, wt, mod, qk_gains, w_out_video, w_out_text, text_len, timestep)
    return tuple(pl.pallas_call(
        place_kernel,
        name="place",
        in_specs=[VMEM, VMEM],
        out_specs=[VMEM, VMEM],
        out_shape=results,
    )(video, text))


def solution(mesh):
    grid = Mesh(mesh.devices.reshape(4, 4, 2, 2, 2), AXES)
    head = ("zl", "c")
    return jax.shard_map(
        body,
        mesh=grid,
        in_specs=(P(AXES, None), P(), P(None, None, head), P(None, None, head),
                  P(head, None), P(head, None), P(), P(), P(), P()),
        out_specs=(P(AXES, None), P(head, None)),
        check_vma=False,
    )
```

```python
import functools
import math

import jax
import jax.numpy as jnp
from jax import lax
from jax.experimental import pallas as pl
from jax.experimental.pallas import tpu as pltpu
from jax.sharding import Mesh, PartitionSpec as P

AXES = ("x", "y", "zh", "zl", "c")
MESH = pl.DeviceIdType.MESH
BF16, F32 = jnp.bfloat16, jnp.float32
D = 3072
HD = 128
NH = 3
W = NH * HD
HALF = 256
TXT = 256
TQ = 32
QROWS = 8 * HALF + TQ
ORDER = (3, 1, 2, 0)
CH = 768
NCH = D // CH
EXP_SCALE = math.log2(math.e) / math.sqrt(HD)
VMEM_LIMIT = 60 << 20


def coords():
    x, y, zh, zl, c = (lax.axis_index(a) for a in AXES)
    return x, y, zh * 2 + zl, c


def dev(x, y, z, c):
    z = lax.rem(z + 4, 4)
    return (lax.rem(x + 4, 4), lax.rem(y + 4, 4), z // 2, lax.rem(z, 2), c)


class Sends:
    def __init__(self, sems, peer):
        self.sems, self.peer, self.count, self.pending = sems, peer, 0, []

    def start(self, src, dst, recv_sem, device, pred=None):
        slot = self.count
        self.count += 1
        get = src if callable(src) else (lambda: src)

        pltpu.make_async_remote_copy(
            src_ref=get(), dst_ref=dst, send_sem=self.sems.at[slot], recv_sem=recv_sem,
            device_id=device, device_id_type=MESH).start()

        def wait():
            pltpu.make_async_remote_copy(
                src_ref=get(), dst_ref=get(), send_sem=self.sems.at[slot], recv_sem=self.sems.at[slot],
                device_id=self.peer, device_id_type=MESH).wait_send()

        self.pending.append((pred, wait))

    def finish(self):
        for pred, wait in self.pending:
            if pred is None:
                wait()
            else:
                pl.when(pred)(wait)


def signal(sem, device):
    pl.semaphore_signal(sem, inc=1, device_id=device, device_id_type=MESH)


def norm_rows(src, dst, dst_row, count, shift, scale1):
    def strip(i, carry):
        wide = src[pl.ds(pl.multiple_of(i * 16, 16), 16), :].astype(F32)
        centred = wide - jnp.mean(wide, axis=-1, keepdims=True)
        variance = jnp.mean(centred * centred, axis=-1, keepdims=True)
        out = centred * lax.rsqrt(variance + 1e-06) * scale1 + shift
        dst[pl.ds(pl.multiple_of(dst_row + i * 16, 16), 16), :] = out.astype(BF16)
        return carry

    lax.fori_loop(0, count // 16, strip, 0, unroll=2)


def project(rows, weights, outs, gain_query, gain_key):
    for part in range(3):
        flat = jnp.dot(rows, weights[part][...], preferred_element_type=F32)
        for h in range(NH):
            lanes = slice(h * HD, (h + 1) * HD)
            u = flat[:, lanes]
            if part < 2:
                gain = gain_query if part == 0 else gain_key
                meansq = jnp.mean(u * u, axis=-1, keepdims=True)
                u = u * lax.rsqrt(meansq + 1e-06) * gain
            outs[part][:, lanes] = u.astype(BF16)


def project_wide(rows, weight, out, gain_query, gain_key):
    flat = jnp.dot(rows, weight[...], preferred_element_type=F32)
    for part in range(3):
        for h in range(NH):
            u = flat[:, part * W + h * HD : part * W + (h + 1) * HD]
            if part < 2:
                gain = gain_query if part == 0 else gain_key
                meansq = jnp.mean(u * u, axis=-1, keepdims=True)
                u = u * lax.rsqrt(meansq + 1e-06) * gain
            out[part, :, h * HD : (h + 1) * HD] = u.astype(BF16)


def attend(qb, q0, count, keys, values, acc, first, mask=None):
    for h in range(NH):
        lanes = slice(h * HD, (h + 1) * HD)
        query = qb[pl.ds(q0, count), lanes]
        total = None
        for key_ref, value_ref in zip(keys, values):
            scores = lax.dot_general(
                query, key_ref[:, lanes], (((1,), (1,)), ((), ())), preferred_element_type=F32)
            expo = jnp.exp2(scores * EXP_SCALE)
            if mask is not None:
                expo = jnp.where(mask, expo, 0.0)
            value = value_ref[:, lanes]
            wide = jnp.concatenate([value, jnp.ones_like(value)], axis=1)
            part = jnp.dot(expo.astype(BF16), wide, preferred_element_type=F32)
            total = part if total is None else total + part
        if first:
            acc[h, pl.ds(q0, count), :] = total
        else:
            acc[h, pl.ds(q0, count), :] += total


def coded_denoms(acc, rows):
    parts = [acc[h, rows, HD:] for h in range(NH)]
    lane = lax.broadcasted_iota(jnp.int32, parts[0].shape, 1)
    return jnp.where(lane < 8, parts[0], jnp.where(lane < 16, parts[1], parts[2]))


def q_row(pos, half):
    return TQ + ORDER.index(pos) * HALF + (0 if half else 4 * HALF)


TROW = 0


def block_kernel(x_ref, xt_ref, wv_ref, wt_ref, mod_ref, gains_ref, wov_ref, wot_ref, len_ref, step_ref,
                 video_out_ref, text_out_ref, wst_ref,
                 xb, xtb, wvb, wtb, mod0, mod1, mod2, nb, stg, tqst, qb, kvb, tkv, acc, osend, dsend, orecv, drecv,
                 rrecv, rden, tsend, tden, trecv, tdrecv, afin, tfin, attn, text, wob, gsend, grecv, gown, vown,
                 load_sem, send_sem, x_sem, w_sem, own_sem, kv_sem, q_sem, t_sem, o_sem, r_sem, tr_sem,
                 attn_sem, text_sem, out_sem):
    x, y, z, c = coords()
    zh, zl = z // 2, lax.rem(z, 2)
    role = lax.rem(c + zh, 2)
    is0, is1 = role == 0, role == 1
    sibling = dev(x, y, z, 1 - c)
    partner = dev(x, y, z + 2, 1 - c)
    xp, xm = dev(x + 1, y, z, c), dev(x - 1, y, z, c)
    yps = {1: dev(x, y + 1, z, c), 2: dev(x, y - 1, z, c), 3: dev(x, y + 2, z, c)}
    zp, zm = dev(x, y, z + 1, c), dev(x, y, z - 1, c)

    load_x = pltpu.make_async_copy(x_ref, xb.at[c], load_sem.at[0])
    load_mod = [
        pltpu.make_async_copy(mod_ref.at[pl.ds(2 * i, 2)], part, load_sem.at[1 + i])
        for i, part in enumerate((mod0, mod1, mod2))]
    load_wv = [
        pltpu.make_async_copy(wv_ref.at[part], wvb.at[:, part * W : (part + 1) * W], load_sem.at[4 + part])
        for part in range(3)]
    load_xt = pltpu.make_async_copy(xt_ref, xtb, load_sem.at[7])
    load_wt = [
        pltpu.make_async_copy(wt_ref.at[part], wtb.at[pl.ds(part * D, D)], load_sem.at[8 + part])
        for part in range(3)]
    for copy in [load_x, load_mod[0]] + load_wv:
        copy.start()

    @pl.when(is0)
    def _():
        for copy in [load_xt] + load_wt:
            copy.start()

    load_mod[1].start()
    load_mod[2].start()

    barrier = pltpu.get_barrier_semaphore()
    for device in (sibling, xp, xm, yps[1], yps[2], yps[3], zp, zm, dev(x, y, z + 2, zh)):
        signal(barrier, device)

    @pl.when(is1)
    def _():
        signal(barrier, dev(x, y, z + 2, 1 - zh))

    step = step_ref[0]
    load_x.wait()
    load_mod[0].wait()
    shift, scale1 = mod0[0, pl.ds(step, 1), :], 1.0 + mod0[1, pl.ds(step, 1), :]
    norm_rows(xb.at[c], nb, 128 * c, 128, shift, scale1)
    pl.semaphore_wait(barrier, 9 + role)

    sends = Sends(send_sem, sibling)

    def arrived(dst, sem):
        pltpu.make_async_remote_copy(
            src_ref=dst, dst_ref=dst, send_sem=send_sem.at[0], recv_sem=sem,
            device_id=sibling, device_id_type=MESH).wait_recv()

    for rows, device, sem in ((pl.ds(0, 64), zm, x_sem.at[1]), (pl.ds(64, 64), zp, x_sem.at[2])):
        sends.start(lambda rows=rows: x_ref.at[rows], xb.at[2 + c, rows], sem, device)
    sends.start(x_ref, xb.at[c], x_sem.at[0], sibling)

    def q_half(pos, half):
        return qb.at[pl.ds(q_row(pos, half), HALF)]

    def send_queries(src, half, pred):
        for pos, back in ((3, 3), (1, 2), (2, 1)):
            sends.start(src, q_half(back, half), q_sem.at[back, half], yps[pos], pred)

    def send_keys(src, r, half, pred):
        sends.start(src, kvb.at[r, 2, half], kv_sem.at[r, 2, half, 0], xp, pred)
        sends.start(src, kvb.at[r, 1, half], kv_sem.at[r, 1, half, 0], xm, pred)
        sends.start(src, kvb.at[r, 0, half], kv_sem.at[r, 0, half, 0], sibling, pred)

    def stage_q(half):
        return stg.at[half, 0]

    def stage_kv(half):
        return stg.at[half, pl.ds(1, 2)]

    def send_half(half):
        copies = [
            pltpu.make_async_copy(stage_q(half), q_half(0, half), own_sem.at[half, 0]),
            pltpu.make_async_copy(stage_kv(half), kvb.at[0, 0, half], own_sem.at[half, 1])]
        for copy in copies:
            copy.start()
        send_keys(lambda: stage_kv(half), 0, half, is0)
        if half == 0:
            send_queries(lambda: stage_q(half), half, is0)
        for copy in copies:
            copy.wait()

    def swap_q(half):
        sends.start(lambda: stage_q(half), q_half(0, half), q_sem.at[0, half], partner, is1)

    def swap_kv(half):
        sends.start(lambda: stage_kv(half), kvb.at[1, 0, half], kv_sem.at[1, 0, half, 0], partner, is1)

    def swapped_q(half):
        arrived(q_half(0, half), q_sem.at[0, half])
        send_queries(lambda: q_half(0, half), half, is1)

    def swapped_kv(half):
        arrived(kvb.at[1, 0, half], kv_sem.at[1, 0, half, 0])
        send_keys(lambda: kvb.at[1, 0, half], 1, half, is1)

    def pass_on(r, half, pred):
        arrived(kvb.at[r, 1, half], kv_sem.at[r, 1, half, 0])
        sends.start(lambda: kvb.at[r, 1, half, 0], kvb.at[r, 3, half, 0], kv_sem.at[r, 3, half, 0], xm, pred)
        arrived(kvb.at[r, 2, half], kv_sem.at[r, 2, half, 0])
        sends.start(lambda: kvb.at[r, 2, half, 1], kvb.at[r, 3, half, 1], kv_sem.at[r, 3, half, 1], xp, pred)
        for pos in (1, 2):
            sends.start(lambda pos=pos: kvb.at[r, pos, half], kvb.at[r, pos, half],
                        kv_sem.at[r, pos, half, 0], sibling, pred)

    def pass_last(r, half, pred):
        for part in range(2):
            arrived(kvb.at[r, 3, half, part], kv_sem.at[r, 3, half, part])
        sends.start(lambda: kvb.at[r, 3, half], kvb.at[r, 3, half], kv_sem.at[r, 3, half, 0], sibling, pred)

    def from_sibling(r, blocks):
        for pos, half in blocks:
            arrived(kvb.at[r, pos, half], kv_sem.at[r, pos, half, 0])

    def on(pred, *steps):
        @pl.when(pred)
        def _():
            for step in steps:
                step()

    def over(blocks, q0, count, first=False):
        attend(qb, q0, count, [kvb.at[r, p, f, 0] for r, p, f in blocks],
               [kvb.at[r, p, f, 1] for r, p, f in blocks], acc, first)

    arrived(xb.at[1 - c], x_sem.at[0])
    norm_rows(xb.at[1 - c], nb, 128 * (1 - c), 128, shift, scale1)
    for copy in load_wv:
        copy.wait()
    project_wide(nb[...], wvb, stg.at[0], gains_ref[0:1, :], gains_ref[1:2, :])
    on(is0, lambda: send_half(0))
    on(is1, lambda: swap_q(0))
    ours = pl.ds(pl.multiple_of((2 * zl + c) * W, 16), W)
    theirs = pl.ds(pl.multiple_of((2 * zl + 1 - c) * W, 16), W)
    quarter = W // 4

    def send_weights(piece):
        for side, device in ((0, zp), (1, zm)):
            first_row = (2 * side + piece) * quarter
            place = pl.multiple_of((2 * zl + c) * W + first_row, 16)
            sends.start(lambda first_row=first_row: wov_ref.at[pl.ds(first_row, quarter)],
                        wob.at[pl.ds(place, quarter)], w_sem.at[2 + 2 * side + piece], device)

    def far_piece(core, k):
        return wob.at[pl.ds(pl.multiple_of((2 - 2 * zl + core) * W + k * quarter, 16), quarter)]

    def pass_weights(piece):
        for k in (piece, 2 + piece):
            arrived(far_piece(c, k), w_sem.at[2 + k])
            sends.start(lambda k=k: far_piece(c, k), far_piece(c, k), w_sem.at[6 + k], sibling)

    sends.start(wot_ref, wst_ref, w_sem.at[1], sibling)
    load_wo = pltpu.make_async_copy(wov_ref, wob.at[ours], load_sem.at[11])
    load_wo.start()
    load_mod[1].wait()
    load_mod[2].wait()

    tq_row = pl.multiple_of(64 * x, 64)
    tq_other = tqst.at[pl.ds(pl.multiple_of(64 * x + TQ, TQ), TQ)]
    tq_own = qb.at[pl.ds(TROW, TQ)]

    @pl.when(is0)
    def _():
        load_xt.wait()
        for copy in load_wt:
            copy.wait()
        norm_rows(xtb, nb, 0, TXT, mod1[1, pl.ds(step, 1), :], 1.0 + mod2[0, pl.ds(step, 1), :])
        project(nb[...], [wtb.at[pl.ds(part * D, D)] for part in range(3)],
                [tqst, tkv.at[0], tkv.at[1]], gains_ref[2:3, :], gains_ref[3:4, :])
        copy = pltpu.make_async_copy(tqst.at[pl.ds(tq_row, TQ)], tq_own, own_sem.at[2, 0])
        copy.start()
        sends.start(tq_other, tq_own, t_sem.at[0], sibling, is0)
        sends.start(tkv, tkv, t_sem.at[1], sibling, is0)
        copy.wait()

    arrived(xb.at[2 + c, pl.ds(0, 64)], x_sem.at[1])
    arrived(xb.at[2 + c, pl.ds(64, 64)], x_sem.at[2])
    sends.start(xb.at[2 + c], xb.at[2 + c], x_sem.at[3], sibling)
    on(is1, lambda: swap_kv(0))
    norm_rows(xb.at[2 + c], nb, 128 * c, 128, shift, scale1)
    on(is1, lambda: swapped_q(0))
    arrived(xb.at[3 - c], x_sem.at[3])
    norm_rows(xb.at[3 - c], nb, 128 * (1 - c), 128, shift, scale1)
    on(is0, lambda: pass_on(0, 0, is0))
    project_wide(nb[...], wvb, stg.at[1], gains_ref[0:1, :], gains_ref[1:2, :])
    on(is0, lambda: send_half(1))
    on(is1, lambda: swap_q(1), lambda: swap_kv(1), lambda: swapped_kv(0))

    first_rows = q_row(ORDER[0], 0)

    def rows_of(base, size, i):
        return pl.multiple_of(base + i * size, 16)

    on(is1, lambda: from_sibling(0, [(0, 0), (1, 0), (2, 0)]))
    for pos in (1, 2, 3):
        arrived(q_half(pos, 0), q_sem.at[pos, 0])

    def first(i, carry):
        on(jnp.logical_and(i == 1, is0), lambda: send_queries(lambda: stage_q(1), 1, is0),
           lambda: pass_last(0, 0, is0))
        on(jnp.logical_and(i == 1, is1), lambda: swapped_q(1))
        over([(0, 0, 0), (0, 1, 0), (0, 2, 0)], rows_of(first_rows, 512, i), 512, True)
        return carry

    lax.fori_loop(0, 2, first, 0)
    on(is0, lambda: from_sibling(1, [(0, 0)]))
    on(is1, lambda: from_sibling(0, [(3, 0), (0, 1)]))

    def second(i, carry):
        over([(0, 3, 0), (0, 0, 1), (1, 0, 0)], rows_of(first_rows, 512, i), 512)
        return carry

    lax.fori_loop(0, 2, second, 0)
    on(is0, lambda: pass_on(0, 1, is0))
    on(is1, lambda: pass_on(1, 0, is1),
       lambda: arrived(tq_own, t_sem.at[0]), lambda: arrived(tkv, t_sem.at[1]))
    send_weights(0)

    arrived(wst_ref, w_sem.at[1])
    load_wo_text = []
    for i in range(8):
        cols = slice(i * W, (i + 1) * W)
        for k, (src, place) in enumerate(((wot_ref, c), (wst_ref, 1 - c))):
            rows = pl.ds(pl.multiple_of(i * 2 * W + place * W, 16), W)
            load_wo_text.append(pltpu.make_async_copy(
                src.at[:, cols], wtb.at[rows], load_sem.at[12 + 2 * i + k]))
    for copy in load_wo_text:
        copy.start()
    for pos in (1, 2, 3):
        arrived(q_half(pos, 1), q_sem.at[pos, 1])

    def third(i, carry):
        on(jnp.logical_and(i == 1, is1), lambda: swapped_kv(1))
        over([(0, 0, 0), (0, 1, 0), (0, 2, 0), (0, 3, 0), (0, 0, 1), (1, 0, 0)],
             rows_of(0, 528, i), 528, True)
        return carry

    lax.fori_loop(0, 2, third, 0)
    send_weights(1)
    sends.start(wov_ref, wob.at[ours], w_sem.at[0], sibling)
    on(is1, lambda: pass_last(1, 0, is1),
       lambda: from_sibling(0, [(1, 1), (2, 1)]))
    on(is0, lambda: pass_last(0, 1, is0), lambda: from_sibling(1, [(1, 0), (2, 0), (0, 1)]))

    limit = len_ref[0]
    text_limit = jnp.where(y == 0, limit, 0)
    for q0, count, most in ((TROW, TQ, text_limit), (q_row(0, 1), HALF, limit), (q_row(0, 0), HALF, limit)):
        mask = lax.broadcasted_iota(jnp.int32, (count, TXT), 1) < most
        attend(qb, q0, count, [tkv.at[0]], [tkv.at[1]], acc, False, mask)

    middle_blocks = [(0, 1, 1), (0, 2, 1), (1, 1, 0), (1, 2, 0), (1, 0, 1)]
    last_blocks = [(0, 3, 1), (1, 3, 0), (1, 1, 1), (1, 2, 1), (1, 3, 1)]

    def middle(i, carry):
        on(jnp.logical_and(i == 1, is1), lambda: pass_on(1, 1, is1))
        over(middle_blocks, rows_of(0, 528, i), 528)
        return carry

    lax.fori_loop(0, 2, middle, 0)
    on(is1, lambda: pass_last(1, 1, is1), lambda: from_sibling(0, [(3, 1)]))
    on(is0, lambda: from_sibling(1, [(3, 0), (1, 1), (2, 1), (3, 1)]))

    def fill_sums(pos, half):
        rows = pl.ds(q_row(pos, half), HALF)
        for h in range(NH):
            osend[pos - 1, half, :, h * HD : (h + 1) * HD] = acc[h, rows, :HD].astype(BF16)
        dsend[pos - 1, half] = jnp.transpose(coded_denoms(acc, rows))[:24]

    def send_far(half):
        fill_sums(3, half)
        for part, device in ((0, yps[1]), (1, yps[2])):
            cut = pl.ds(128 * part, 128)
            sends.start(lambda cut=cut: osend.at[2, half, cut], rrecv.at[part, half],
                        r_sem.at[part, half, 0], device)
            sends.start(lambda cut=cut: dsend.at[2, half, :, cut], rden.at[part, half],
                        r_sem.at[part, half, 1], device)

    def send_near(half):
        for pos, part in ((1, 0), (2, 1)):
            back = 1 - part
            fill_sums(pos, half)
            arrived(rrecv.at[part, half], r_sem.at[part, half, 0])
            arrived(rden.at[part, half], r_sem.at[part, half, 1])
            cut = slice(128 * part, 128 * part + 128)
            rows = pl.ds(q_row(pos, half) + 128 * part, 128)
            for h in range(NH):
                lanes = slice(h * HD, (h + 1) * HD)
                osend[pos - 1, half, cut, lanes] = (
                    acc[h, rows, :HD] + rrecv[part, half, :, lanes].astype(F32)).astype(BF16)
            dsend[pos - 1, half, :, cut] = dsend[pos - 1, half, :, cut] + rden[part, half]
            sends.start(lambda pos=pos: osend.at[pos - 1, half], orecv.at[back, half],
                        o_sem.at[back, half, 0], yps[pos])
            sends.start(lambda pos=pos: dsend.at[pos - 1, half], drecv.at[back, half],
                        o_sem.at[back, half, 1], yps[pos])

    acol = pl.ds(pl.multiple_of((2 * zl + zh) * W, HD), W)
    ahead = 1 - 2 * role

    def combine(half):
        for part in range(2):
            arrived(orecv.at[part, half], o_sem.at[part, half, 0])
            arrived(drecv.at[part, half], o_sem.at[part, half, 1])
        rows = pl.ds(q_row(0, half), HALF)
        denoms = drecv[0, half] + drecv[1, half]
        for h in range(NH):
            lanes = slice(h * HD, (h + 1) * HD)
            numer = acc[h, rows, :HD]
            for part in range(2):
                numer = numer + orecv[part, half, :, lanes].astype(F32)
            denom = acc[h, rows, HD:] + jnp.transpose(
                jnp.broadcast_to(denoms[8 * h : 8 * h + 1, :], (HD, HALF)))
            afin[half, :, lanes] = (numer / denom).astype(BF16)
        if half:
            for core in range(2):
                for first_row, step_z in ((0, ahead), (64, -ahead)):
                    rows = pl.ds(core * 128 + first_row, 64)
                    sends.start(lambda rows=rows: afin.at[half, rows],
                                attn.at[pl.ds(first_row, 64), acol], attn_sem.at[1],
                                dev(x, y, z + step_z, core))
            return
        for core in range(2):
            dst = attn.at[:, acol]
            across = jnp.logical_and(is0, c != core)

            def src(core=core):
                return afin.at[0, pl.ds(core * 128, 128)]

            @pl.when(is1)
            def _():
                sends.start(src, dst, attn_sem.at[0], dev(x, y, z + 2, core), is1)

            @pl.when(jnp.logical_and(is0, c == core))
            def _():
                pltpu.make_async_copy(src(), dst, attn_sem.at[0]).start()

            @pl.when(across)
            def _():
                sends.start(src, dst, attn_sem.at[0], sibling, across)

    over(last_blocks, TROW, TQ + HALF)

    trows = pl.ds(TROW, TQ)
    for h in range(NH):
        tsend[:, h * HD : (h + 1) * HD] = acc[h, trows, :HD].astype(BF16)
    tden[...] = coded_denoms(acc, trows)
    for pos, back in ((3, 3), (1, 2), (2, 1)):
        sends.start(tsend, trecv.at[back - 1], tr_sem.at[back - 1, 0], yps[pos])
        sends.start(tden, tdrecv.at[back - 1], tr_sem.at[back - 1, 1], yps[pos])
    send_far(1)
    over(last_blocks, q_row(1, 1), 512)
    over(last_blocks, q_row(0, 1), HALF)
    send_near(1)

    for pos in range(3):
        arrived(trecv.at[pos], tr_sem.at[pos, 0])
        arrived(tdrecv.at[pos], tr_sem.at[pos, 1])
    denoms = tden[...] + tdrecv[0] + tdrecv[1] + tdrecv[2]
    for h in range(NH):
        lanes = slice(h * HD, (h + 1) * HD)
        numer = acc[h, trows, :HD]
        for pos in range(3):
            numer = numer + trecv[pos, :, lanes].astype(F32)
        tfin[:, lanes] = (numer / denoms[:, 8 * h : 8 * h + 1]).astype(BF16)
    place = text.at[pl.ds(pl.multiple_of(lax.rem(x // 2, 2) * 64 + 32 * role, 32), TQ),
                    pl.ds(pl.multiple_of(zh * W, HD), W)]
    core_of = lax.rem(x, 2)
    for dx in range(4):
        for dz in range(2):
            if dx + dz:
                sends.start(tfin, place, text_sem.at[0], dev(x + dx, y, z + 2 * dz, core_of))
    elsewhere = core_of != c

    @pl.when(core_of == c)
    def _():
        pltpu.make_async_copy(tfin, place, text_sem.at[0]).start()

    @pl.when(elsewhere)
    def _():
        sends.start(tfin, place, text_sem.at[0], sibling, elsewhere)

    pass_weights(0)
    over(middle_blocks + last_blocks, q_row(3, 0), HALF)
    send_far(0)
    over(middle_blocks + last_blocks, q_row(1, 0), 512)
    send_near(0)
    combine(1)

    for copy in load_wo_text:
        copy.wait()
    arrived(text, text_sem.at[0])
    far_row = pl.multiple_of((1 - zl) * 64, 64)
    own_row = pl.multiple_of(zl * 64, 64)
    for i in range(8):
        weight = wtb[i * 2 * W : (i + 1) * 2 * W, :]
        gsend[:, i * W : (i + 1) * W] = jnp.dot(
            text[pl.ds(far_row, 64), :], weight, preferred_element_type=F32).astype(BF16)
    low, high = pl.ds(0, 32), pl.ds(32, 32)
    sends.start(gsend.at[low], grecv.at[low], out_sem.at[0], zp)
    sends.start(gsend.at[high], grecv.at[high], out_sem.at[0], zm)
    pass_weights(1)
    over(middle_blocks + last_blocks, q_row(0, 0), HALF)
    combine(0)

    for i in range(8):
        weight = wtb[i * 2 * W : (i + 1) * 2 * W, :]
        gown[:, i * W : (i + 1) * W] = jnp.dot(
            text[pl.ds(own_row, 64), :], weight, preferred_element_type=F32)
    load_wo.wait()
    arrived(wob.at[theirs], w_sem.at[0])
    for k in range(4):
        arrived(far_piece(1 - c, k), w_sem.at[6 + k])

    def product(group, cols):
        rows = pl.ds(pl.multiple_of(group * 2 * W, HD), 2 * W)
        return jnp.dot(attn[:, rows], wob[rows, cols], preferred_element_type=F32)

    arrived(attn.at[:, pl.ds(pl.multiple_of((1 - zl) * 2 * W, HD), 2 * W)], attn_sem.at[1])
    for i in range(NCH):
        cols = slice(i * CH, (i + 1) * CH)
        vown[:, cols] = product(1 - zl, cols)
    arrived(attn.at[:, pl.ds(pl.multiple_of(zl * 2 * W, HD), 2 * W)], attn_sem.at[0])
    for i in range(NCH):
        cols = slice(i * CH, (i + 1) * CH)
        video_out_ref[:, cols] = (
            mod1[0, pl.ds(step, 1), cols] * (vown[:, cols] + product(zl, cols))).astype(BF16)
    arrived(grecv, out_sem.at[0])
    row = lax.broadcasted_iota(jnp.int32, (64, CH), 0) + (zl * 2 + c) * 64
    valid = row < len_ref[0]
    for i in range(NCH):
        cols = slice(i * CH, (i + 1) * CH)
        text_out_ref[:, cols] = jnp.where(
            valid, mod2[1, pl.ds(step, 1), cols] * (gown[:, cols] + grecv[:, cols].astype(F32)),
            0.0).astype(BF16)
    sends.finish()


def place_kernel(video_ref, text_ref, video_out_ref, text_out_ref):
    video_out_ref[...] = video_ref[...]
    text_out_ref[...] = text_ref[...]


ANY = pl.BlockSpec(memory_space=pl.ANY)
VMEM = pl.BlockSpec(memory_space=pltpu.VMEM)
SMEM = pl.BlockSpec(memory_space=pltpu.SMEM)
DMA = pltpu.SemaphoreType.DMA


def body(x_video, x_text, w_qkv_video, w_qkv_text, w_out_video, w_out_text, qk_gains, modulation,
         text_len, timestep):
    wv = jnp.transpose(w_qkv_video, (1, 0, 2))
    wt = jnp.transpose(w_qkv_text, (1, 0, 2))
    mod = jnp.transpose(modulation, (1, 0, 2))
    shape = jax.ShapeDtypeStruct
    steps = modulation.shape[0]
    results = [shape((128, D), BF16), shape((64, D), BF16)]
    video, text, unused = pl.pallas_call(
        block_kernel,
        name="block",
        in_specs=[ANY, ANY, ANY, ANY, ANY, VMEM, ANY, ANY, SMEM, SMEM],
        out_specs=[VMEM, VMEM, ANY],
        out_shape=results + [shape((W, D), BF16)],
        scratch_shapes=[
            pltpu.VMEM((4, 128, D), BF16), pltpu.VMEM((TXT, D), BF16),
            pltpu.VMEM((D, 3 * W), BF16), pltpu.VMEM((3 * D, W), BF16),
            pltpu.VMEM((2, steps, D), F32), pltpu.VMEM((2, steps, D), F32), pltpu.VMEM((2, steps, D), F32),
            pltpu.VMEM((HALF, D), BF16),
            pltpu.VMEM((2, 3, HALF, W), BF16), pltpu.VMEM((TXT, W), BF16),
            pltpu.VMEM((QROWS, W), BF16), pltpu.VMEM((2, 4, 2, 2, HALF, W), BF16),
            pltpu.VMEM((2, TXT, W), BF16), pltpu.VMEM((NH, QROWS, 2 * HD), F32),
            pltpu.VMEM((3, 2, HALF, W), BF16), pltpu.VMEM((3, 2, 24, HALF), F32),
            pltpu.VMEM((2, 2, HALF, W), BF16), pltpu.VMEM((2, 2, 24, HALF), F32),
            pltpu.VMEM((2, 2, 128, W), BF16), pltpu.VMEM((2, 2, 24, 128), F32),
            pltpu.VMEM((TQ, W), BF16), pltpu.VMEM((TQ, HD), F32),
            pltpu.VMEM((3, TQ, W), BF16), pltpu.VMEM((3, TQ, HD), F32),
            pltpu.VMEM((2, HALF, W), BF16), pltpu.VMEM((TQ, W), BF16),
            pltpu.VMEM((128, 4 * W), BF16), pltpu.VMEM((128, 2 * W), BF16), pltpu.VMEM((4 * W, D), BF16),
            pltpu.VMEM((64, D), BF16), pltpu.VMEM((64, D), BF16),
            pltpu.VMEM((64, D), F32), pltpu.VMEM((128, D), F32),
            DMA((28,)), DMA((136,)), DMA((4,)), DMA((10,)), DMA((3, 2)), DMA((2, 4, 2, 2)), DMA((4, 2)),
            DMA((2,)), DMA((2, 2, 2)), DMA((2, 2, 2)), DMA((3, 2)), DMA((2,)), DMA((1,)), DMA((1,))],
        compiler_params=pltpu.CompilerParams(
            collective_id=1, has_side_effects=True, vmem_limit_bytes=VMEM_LIMIT),
    )(x_video, x_text, wv, wt, mod, qk_gains, w_out_video, w_out_text, text_len, timestep)
    return tuple(pl.pallas_call(
        place_kernel,
        name="place",
        in_specs=[VMEM, VMEM],
        out_specs=[VMEM, VMEM],
        out_shape=results,
    )(video, text))


def solution(mesh):
    grid = Mesh(mesh.devices.reshape(4, 4, 2, 2, 2), AXES)
    head = ("zl", "c")
    return jax.shard_map(
        body,
        mesh=grid,
        in_specs=(P(AXES, None), P(), P(None, None, head), P(None, None, head),
                  P(head, None), P(head, None), P(), P(), P(), P()),
        out_specs=(P(AXES, None), P(head, None)),
        check_vma=False,
    )
```

```python
import functools
import math

import jax
import jax.numpy as jnp
from jax import lax
from jax.experimental import pallas as pl
from jax.experimental.pallas import tpu as pltpu
from jax.sharding import Mesh, PartitionSpec as P

AXES = ("x", "y", "zh", "zl", "c")
MESH = pl.DeviceIdType.MESH
BF16, F32 = jnp.bfloat16, jnp.float32
D = 3072
HD = 128
NH = 3
W = NH * HD
HALF = 256
TXT = 256
TQ = 32
QROWS = 8 * HALF + TQ
ORDER = (3, 1, 2, 0)
CH = 768
NCH = D // CH
EXP_SCALE = math.log2(math.e) / math.sqrt(HD)
VMEM_LIMIT = 60 << 20


def coords():
    x, y, zh, zl, c = (lax.axis_index(a) for a in AXES)
    return x, y, zh * 2 + zl, c


def dev(x, y, z, c):
    z = lax.rem(z + 4, 4)
    return (lax.rem(x + 4, 4), lax.rem(y + 4, 4), z // 2, lax.rem(z, 2), c)


class Sends:
    def __init__(self, sems, peer):
        self.sems, self.peer, self.count, self.pending = sems, peer, 0, []

    def start(self, src, dst, recv_sem, device, pred=None):
        slot = self.count
        self.count += 1
        get = src if callable(src) else (lambda: src)

        pltpu.make_async_remote_copy(
            src_ref=get(), dst_ref=dst, send_sem=self.sems.at[slot], recv_sem=recv_sem,
            device_id=device, device_id_type=MESH).start()

        def wait():
            pltpu.make_async_remote_copy(
                src_ref=get(), dst_ref=get(), send_sem=self.sems.at[slot], recv_sem=self.sems.at[slot],
                device_id=self.peer, device_id_type=MESH).wait_send()

        self.pending.append((pred, wait))

    def finish(self):
        for pred, wait in self.pending:
            if pred is None:
                wait()
            else:
                pl.when(pred)(wait)


def signal(sem, device):
    pl.semaphore_signal(sem, inc=1, device_id=device, device_id_type=MESH)


def norm_rows(src, dst, dst_row, count, shift, scale1):
    def strip(i, carry):
        wide = src[pl.ds(pl.multiple_of(i * 16, 16), 16), :].astype(F32)
        centred = wide - jnp.mean(wide, axis=-1, keepdims=True)
        variance = jnp.mean(centred * centred, axis=-1, keepdims=True)
        out = centred * lax.rsqrt(variance + 1e-06) * scale1 + shift
        dst[pl.ds(pl.multiple_of(dst_row + i * 16, 16), 16), :] = out.astype(BF16)
        return carry

    lax.fori_loop(0, count // 16, strip, 0, unroll=2)


def project(rows, weights, outs, gain_query, gain_key):
    for part in range(3):
        flat = jnp.dot(rows, weights[part][...], preferred_element_type=F32)
        for h in range(NH):
            lanes = slice(h * HD, (h + 1) * HD)
            u = flat[:, lanes]
            if part < 2:
                gain = gain_query if part == 0 else gain_key
                meansq = jnp.mean(u * u, axis=-1, keepdims=True)
                u = u * lax.rsqrt(meansq + 1e-06) * gain
            outs[part][:, lanes] = u.astype(BF16)


def project_wide(rows, weight, out, gain_query, gain_key):
    flat = jnp.dot(rows, weight[...], preferred_element_type=F32)
    for part in range(3):
        for h in range(NH):
            u = flat[:, part * W + h * HD : part * W + (h + 1) * HD]
            if part < 2:
                gain = gain_query if part == 0 else gain_key
                meansq = jnp.mean(u * u, axis=-1, keepdims=True)
                u = u * lax.rsqrt(meansq + 1e-06) * gain
            out[part, :, h * HD : (h + 1) * HD] = u.astype(BF16)


def attend(qb, q0, count, keys, values, acc, first, mask=None):
    for h in range(NH):
        lanes = slice(h * HD, (h + 1) * HD)
        query = qb[pl.ds(q0, count), lanes]
        total = None
        for key_ref, value_ref in zip(keys, values):
            scores = lax.dot_general(
                query, key_ref[:, lanes], (((1,), (1,)), ((), ())), preferred_element_type=F32)
            expo = jnp.exp2(scores * EXP_SCALE)
            if mask is not None:
                expo = jnp.where(mask, expo, 0.0)
            value = value_ref[:, lanes]
            wide = jnp.concatenate([value, jnp.ones_like(value)], axis=1)
            part = jnp.dot(expo.astype(BF16), wide, preferred_element_type=F32)
            total = part if total is None else total + part
        if first:
            acc[h, pl.ds(q0, count), :] = total
        else:
            acc[h, pl.ds(q0, count), :] += total


def coded_denoms(acc, rows):
    parts = [acc[h, rows, HD:] for h in range(NH)]
    lane = lax.broadcasted_iota(jnp.int32, parts[0].shape, 1)
    return jnp.where(lane < 8, parts[0], jnp.where(lane < 16, parts[1], parts[2]))


def q_row(pos, half):
    return TQ + ORDER.index(pos) * HALF + (0 if half else 4 * HALF)


TROW = 0


def block_kernel(x_ref, xt_ref, wv_ref, wt_ref, mod_ref, gains_ref, wov_ref, wot_ref, len_ref, step_ref,
                 video_out_ref, text_out_ref, wst_ref,
                 xb, xtb, wvb, wtb, mod0, mod1, mod2, nb, stg, tqst, qb, kvb, tkv, acc, osend, dsend, orecv, drecv,
                 rrecv, rden, tsend, tden, trecv, tdrecv, afin, tfin, attn, text, wob, gsend, grecv, gown, vown,
                 load_sem, send_sem, x_sem, w_sem, own_sem, kv_sem, q_sem, t_sem, o_sem, r_sem, tr_sem,
                 attn_sem, text_sem, out_sem):
    x, y, z, c = coords()
    zh, zl = z // 2, lax.rem(z, 2)
    role = lax.rem(c + zh, 2)
    is0, is1 = role == 0, role == 1
    sibling = dev(x, y, z, 1 - c)
    partner = dev(x, y, z + 2, 1 - c)
    xp, xm = dev(x + 1, y, z, c), dev(x - 1, y, z, c)
    yps = {1: dev(x, y + 1, z, c), 2: dev(x, y - 1, z, c), 3: dev(x, y + 2, z, c)}
    zp, zm = dev(x, y, z + 1, c), dev(x, y, z - 1, c)

    load_x = pltpu.make_async_copy(x_ref, xb.at[c], load_sem.at[0])
    load_mod = [
        pltpu.make_async_copy(mod_ref.at[pl.ds(2 * i, 2)], part, load_sem.at[1 + i])
        for i, part in enumerate((mod0, mod1, mod2))]
    load_wv = [
        pltpu.make_async_copy(wv_ref.at[part], wvb.at[:, part * W : (part + 1) * W], load_sem.at[4 + part])
        for part in range(3)]
    load_xt = pltpu.make_async_copy(xt_ref, xtb, load_sem.at[7])
    load_wt = [
        pltpu.make_async_copy(wt_ref.at[part], wtb.at[pl.ds(part * D, D)], load_sem.at[8 + part])
        for part in range(3)]
    for copy in [load_x, load_mod[0]] + load_wv:
        copy.start()

    @pl.when(is0)
    def _():
        for copy in [load_xt] + load_wt:
            copy.start()

    load_mod[1].start()
    load_mod[2].start()

    barrier = pltpu.get_barrier_semaphore()
    for device in (sibling, xp, xm, yps[1], yps[2], yps[3], zp, zm, dev(x, y, z + 2, zh)):
        signal(barrier, device)

    @pl.when(is1)
    def _():
        signal(barrier, dev(x, y, z + 2, 1 - zh))

    step = step_ref[0]
    load_x.wait()
    load_mod[0].wait()
    shift, scale1 = mod0[0, pl.ds(step, 1), :], 1.0 + mod0[1, pl.ds(step, 1), :]
    norm_rows(xb.at[c], nb, 128 * c, 128, shift, scale1)
    pl.semaphore_wait(barrier, 9 + role)

    sends = Sends(send_sem, sibling)

    def arrived(dst, sem):
        pltpu.make_async_remote_copy(
            src_ref=dst, dst_ref=dst, send_sem=send_sem.at[0], recv_sem=sem,
            device_id=sibling, device_id_type=MESH).wait_recv()

    for rows, device, sem in ((pl.ds(0, 64), zm, x_sem.at[1]), (pl.ds(64, 64), zp, x_sem.at[2])):
        sends.start(lambda rows=rows: x_ref.at[rows], xb.at[2 + c, rows], sem, device)
    sends.start(x_ref, xb.at[c], x_sem.at[0], sibling)

    def q_half(pos, half):
        return qb.at[pl.ds(q_row(pos, half), HALF)]

    def send_queries(src, half, pred):
        for pos, back in ((3, 3), (1, 2), (2, 1)):
            sends.start(src, q_half(back, half), q_sem.at[back, half], yps[pos], pred)

    def send_keys(src, r, half, pred):
        sends.start(src, kvb.at[r, 2, half], kv_sem.at[r, 2, half, 0], xp, pred)
        sends.start(src, kvb.at[r, 1, half], kv_sem.at[r, 1, half, 0], xm, pred)
        sends.start(src, kvb.at[r, 0, half], kv_sem.at[r, 0, half, 0], sibling, pred)

    def stage_q(half):
        return stg.at[half, 0]

    def stage_kv(half):
        return stg.at[half, pl.ds(1, 2)]

    def send_half(half):
        copies = [
            pltpu.make_async_copy(stage_q(half), q_half(0, half), own_sem.at[half, 0]),
            pltpu.make_async_copy(stage_kv(half), kvb.at[0, 0, half], own_sem.at[half, 1])]
        for copy in copies:
            copy.start()
        send_keys(lambda: stage_kv(half), 0, half, is0)
        if half == 0:
            send_queries(lambda: stage_q(half), half, is0)
        for copy in copies:
            copy.wait()

    def swap_q(half):
        sends.start(lambda: stage_q(half), q_half(0, half), q_sem.at[0, half], partner, is1)

    def swap_kv(half):
        sends.start(lambda: stage_kv(half), kvb.at[1, 0, half], kv_sem.at[1, 0, half, 0], partner, is1)

    def swapped_q(half):
        arrived(q_half(0, half), q_sem.at[0, half])
        send_queries(lambda: q_half(0, half), half, is1)

    def swapped_kv(half):
        arrived(kvb.at[1, 0, half], kv_sem.at[1, 0, half, 0])
        send_keys(lambda: kvb.at[1, 0, half], 1, half, is1)

    def pass_on(r, half, pred):
        arrived(kvb.at[r, 1, half], kv_sem.at[r, 1, half, 0])
        sends.start(lambda: kvb.at[r, 1, half, 0], kvb.at[r, 3, half, 0], kv_sem.at[r, 3, half, 0], xm, pred)
        arrived(kvb.at[r, 2, half], kv_sem.at[r, 2, half, 0])
        sends.start(lambda: kvb.at[r, 2, half, 1], kvb.at[r, 3, half, 1], kv_sem.at[r, 3, half, 1], xp, pred)
        for pos in (1, 2):
            sends.start(lambda pos=pos: kvb.at[r, pos, half], kvb.at[r, pos, half],
                        kv_sem.at[r, pos, half, 0], sibling, pred)

    def pass_last(r, half, pred):
        for part in range(2):
            arrived(kvb.at[r, 3, half, part], kv_sem.at[r, 3, half, part])
        sends.start(lambda: kvb.at[r, 3, half], kvb.at[r, 3, half], kv_sem.at[r, 3, half, 0], sibling, pred)

    def from_sibling(r, blocks):
        for pos, half in blocks:
            arrived(kvb.at[r, pos, half], kv_sem.at[r, pos, half, 0])

    def on(pred, *steps):
        @pl.when(pred)
        def _():
            for step in steps:
                step()

    def over(blocks, q0, count, first=False):
        attend(qb, q0, count, [kvb.at[r, p, f, 0] for r, p, f in blocks],
               [kvb.at[r, p, f, 1] for r, p, f in blocks], acc, first)

    arrived(xb.at[1 - c], x_sem.at[0])
    norm_rows(xb.at[1 - c], nb, 128 * (1 - c), 128, shift, scale1)
    for copy in load_wv:
        copy.wait()
    project_wide(nb[...], wvb, stg.at[0], gains_ref[0:1, :], gains_ref[1:2, :])
    on(is0, lambda: send_half(0))
    on(is1, lambda: swap_q(0))
    ours = pl.ds(pl.multiple_of((2 * zl + c) * W, 16), W)
    theirs = pl.ds(pl.multiple_of((2 * zl + 1 - c) * W, 16), W)
    quarter = W // 4

    def send_weights(piece):
        for side, device in ((0, zp), (1, zm)):
            first_row = (2 * side + piece) * quarter
            place = pl.multiple_of((2 * zl + c) * W + first_row, 16)
            sends.start(lambda first_row=first_row: wov_ref.at[pl.ds(first_row, quarter)],
                        wob.at[pl.ds(place, quarter)], w_sem.at[2 + 2 * side + piece], device)

    def far_piece(core, k):
        return wob.at[pl.ds(pl.multiple_of((2 - 2 * zl + core) * W + k * quarter, 16), quarter)]

    def pass_weights(piece):
        for k in (piece, 2 + piece):
            arrived(far_piece(c, k), w_sem.at[2 + k])
            sends.start(lambda k=k: far_piece(c, k), far_piece(c, k), w_sem.at[6 + k], sibling)

    sends.start(wot_ref, wst_ref, w_sem.at[1], sibling)
    load_wo = pltpu.make_async_copy(wov_ref, wob.at[ours], load_sem.at[11])
    load_wo.start()
    load_mod[1].wait()
    load_mod[2].wait()

    tq_row = pl.multiple_of(64 * x, 64)
    tq_other = tqst.at[pl.ds(pl.multiple_of(64 * x + TQ, TQ), TQ)]
    tq_own = qb.at[pl.ds(TROW, TQ)]

    @pl.when(is0)
    def _():
        load_xt.wait()
        for copy in load_wt:
            copy.wait()
        norm_rows(xtb, nb, 0, TXT, mod1[1, pl.ds(step, 1), :], 1.0 + mod2[0, pl.ds(step, 1), :])
        project(nb[...], [wtb.at[pl.ds(part * D, D)] for part in range(3)],
                [tqst, tkv.at[0], tkv.at[1]], gains_ref[2:3, :], gains_ref[3:4, :])
        copy = pltpu.make_async_copy(tqst.at[pl.ds(tq_row, TQ)], tq_own, own_sem.at[2, 0])
        copy.start()
        sends.start(tq_other, tq_own, t_sem.at[0], sibling, is0)
        sends.start(tkv, tkv, t_sem.at[1], sibling, is0)
        copy.wait()

    arrived(xb.at[2 + c, pl.ds(0, 64)], x_sem.at[1])
    arrived(xb.at[2 + c, pl.ds(64, 64)], x_sem.at[2])
    sends.start(xb.at[2 + c], xb.at[2 + c], x_sem.at[3], sibling)
    on(is1, lambda: swap_kv(0))
    norm_rows(xb.at[2 + c], nb, 128 * c, 128, shift, scale1)
    on(is1, lambda: swapped_q(0))
    arrived(xb.at[3 - c], x_sem.at[3])
    norm_rows(xb.at[3 - c], nb, 128 * (1 - c), 128, shift, scale1)
    on(is0, lambda: pass_on(0, 0, is0))
    project_wide(nb[...], wvb, stg.at[1], gains_ref[0:1, :], gains_ref[1:2, :])
    on(is0, lambda: send_half(1))
    on(is1, lambda: swap_q(1), lambda: swap_kv(1), lambda: swapped_kv(0))

    first_rows = q_row(ORDER[0], 0)

    def rows_of(base, size, i):
        return pl.multiple_of(base + i * size, 16)

    on(is1, lambda: from_sibling(0, [(0, 0), (1, 0), (2, 0)]))
    for pos in (1, 2, 3):
        arrived(q_half(pos, 0), q_sem.at[pos, 0])

    def first(i, carry):
        on(jnp.logical_and(i == 1, is0), lambda: send_queries(lambda: stage_q(1), 1, is0),
           lambda: pass_last(0, 0, is0))
        on(jnp.logical_and(i == 1, is1), lambda: swapped_q(1))
        over([(0, 0, 0), (0, 1, 0), (0, 2, 0)], rows_of(first_rows, 512, i), 512, True)
        return carry

    lax.fori_loop(0, 2, first, 0)
    on(is0, lambda: from_sibling(1, [(0, 0)]))
    on(is1, lambda: from_sibling(0, [(3, 0), (0, 1)]))

    def second(i, carry):
        over([(0, 3, 0), (0, 0, 1), (1, 0, 0)], rows_of(first_rows, 512, i), 512)
        return carry

    lax.fori_loop(0, 2, second, 0)
    on(is0, lambda: pass_on(0, 1, is0))
    on(is1, lambda: pass_on(1, 0, is1), lambda: swapped_kv(1),
       lambda: arrived(tq_own, t_sem.at[0]), lambda: arrived(tkv, t_sem.at[1]))
    send_weights(0)

    arrived(wst_ref, w_sem.at[1])
    load_wo_text = []
    for i in range(8):
        cols = slice(i * W, (i + 1) * W)
        for k, (src, place) in enumerate(((wot_ref, c), (wst_ref, 1 - c))):
            rows = pl.ds(pl.multiple_of(i * 2 * W + place * W, 16), W)
            load_wo_text.append(pltpu.make_async_copy(
                src.at[:, cols], wtb.at[rows], load_sem.at[12 + 2 * i + k]))
    for copy in load_wo_text:
        copy.start()
    for pos in (1, 2, 3):
        arrived(q_half(pos, 1), q_sem.at[pos, 1])

    def third(i, carry):
        over([(0, 0, 0), (0, 1, 0), (0, 2, 0), (0, 3, 0), (0, 0, 1), (1, 0, 0)],
             rows_of(0, 528, i), 528, True)
        return carry

    lax.fori_loop(0, 2, third, 0)
    send_weights(1)
    sends.start(wov_ref, wob.at[ours], w_sem.at[0], sibling)
    on(is1, lambda: pass_last(1, 0, is1),
       lambda: from_sibling(0, [(1, 1), (2, 1)]))
    on(is0, lambda: pass_last(0, 1, is0), lambda: from_sibling(1, [(1, 0), (2, 0), (0, 1)]))

    limit = len_ref[0]
    text_limit = jnp.where(y == 0, limit, 0)
    for q0, count, most in ((TROW, TQ, text_limit), (q_row(0, 1), HALF, limit), (q_row(0, 0), HALF, limit)):
        mask = lax.broadcasted_iota(jnp.int32, (count, TXT), 1) < most
        attend(qb, q0, count, [tkv.at[0]], [tkv.at[1]], acc, False, mask)

    middle_blocks = [(0, 1, 1), (0, 2, 1), (1, 1, 0), (1, 2, 0), (1, 0, 1)]
    last_blocks = [(0, 3, 1), (1, 3, 0), (1, 1, 1), (1, 2, 1), (1, 3, 1)]

    on(is1, lambda: pass_on(1, 1, is1))

    def middle(i, carry):
        over(middle_blocks, rows_of(0, 528, i), 528)
        return carry

    lax.fori_loop(0, 2, middle, 0)
    on(is1, lambda: pass_last(1, 1, is1), lambda: from_sibling(0, [(3, 1)]))
    on(is0, lambda: from_sibling(1, [(3, 0), (1, 1), (2, 1), (3, 1)]))

    def fill_sums(pos, half):
        rows = pl.ds(q_row(pos, half), HALF)
        for h in range(NH):
            osend[pos - 1, half, :, h * HD : (h + 1) * HD] = acc[h, rows, :HD].astype(BF16)
        dsend[pos - 1, half] = jnp.transpose(coded_denoms(acc, rows))[:24]

    def send_far(half):
        fill_sums(3, half)
        for part, device in ((0, yps[1]), (1, yps[2])):
            cut = pl.ds(128 * part, 128)
            sends.start(lambda cut=cut: osend.at[2, half, cut], rrecv.at[part, half],
                        r_sem.at[part, half, 0], device)
            sends.start(lambda cut=cut: dsend.at[2, half, :, cut], rden.at[part, half],
                        r_sem.at[part, half, 1], device)

    def send_near(half):
        for pos, part in ((1, 0), (2, 1)):
            back = 1 - part
            fill_sums(pos, half)
            arrived(rrecv.at[part, half], r_sem.at[part, half, 0])
            arrived(rden.at[part, half], r_sem.at[part, half, 1])
            cut = slice(128 * part, 128 * part + 128)
            rows = pl.ds(q_row(pos, half) + 128 * part, 128)
            for h in range(NH):
                lanes = slice(h * HD, (h + 1) * HD)
                osend[pos - 1, half, cut, lanes] = (
                    acc[h, rows, :HD] + rrecv[part, half, :, lanes].astype(F32)).astype(BF16)
            dsend[pos - 1, half, :, cut] = dsend[pos - 1, half, :, cut] + rden[part, half]
            sends.start(lambda pos=pos: osend.at[pos - 1, half], orecv.at[back, half],
                        o_sem.at[back, half, 0], yps[pos])
            sends.start(lambda pos=pos: dsend.at[pos - 1, half], drecv.at[back, half],
                        o_sem.at[back, half, 1], yps[pos])

    acol = pl.ds(pl.multiple_of((2 * zl + zh) * W, HD), W)
    ahead = 1 - 2 * role

    def combine(half):
        for part in range(2):
            arrived(orecv.at[part, half], o_sem.at[part, half, 0])
            arrived(drecv.at[part, half], o_sem.at[part, half, 1])
        rows = pl.ds(q_row(0, half), HALF)
        denoms = drecv[0, half] + drecv[1, half]
        for h in range(NH):
            lanes = slice(h * HD, (h + 1) * HD)
            numer = acc[h, rows, :HD]
            for part in range(2):
                numer = numer + orecv[part, half, :, lanes].astype(F32)
            denom = acc[h, rows, HD:] + jnp.transpose(
                jnp.broadcast_to(denoms[8 * h : 8 * h + 1, :], (HD, HALF)))
            afin[half, :, lanes] = (numer / denom).astype(BF16)
        if half:
            for core in range(2):
                for first_row, step_z in ((0, ahead), (64, -ahead)):
                    rows = pl.ds(core * 128 + first_row, 64)
                    sends.start(lambda rows=rows: afin.at[half, rows],
                                attn.at[pl.ds(first_row, 64), acol], attn_sem.at[1],
                                dev(x, y, z + step_z, core))
            return
        for core in range(2):
            dst = attn.at[:, acol]
            across = jnp.logical_and(is0, c != core)

            def src(core=core):
                return afin.at[0, pl.ds(core * 128, 128)]

            @pl.when(is1)
            def _():
                sends.start(src, dst, attn_sem.at[0], dev(x, y, z + 2, core), is1)

            @pl.when(jnp.logical_and(is0, c == core))
            def _():
                pltpu.make_async_copy(src(), dst, attn_sem.at[0]).start()

            @pl.when(across)
            def _():
                sends.start(src, dst, attn_sem.at[0], sibling, across)

    over(last_blocks, TROW, TQ + HALF)

    trows = pl.ds(TROW, TQ)
    for h in range(NH):
        tsend[:, h * HD : (h + 1) * HD] = acc[h, trows, :HD].astype(BF16)
    tden[...] = coded_denoms(acc, trows)
    for pos, back in ((3, 3), (1, 2), (2, 1)):
        sends.start(tsend, trecv.at[back - 1], tr_sem.at[back - 1, 0], yps[pos])
        sends.start(tden, tdrecv.at[back - 1], tr_sem.at[back - 1, 1], yps[pos])
    send_far(1)
    over(last_blocks, q_row(1, 1), 512)
    over(last_blocks, q_row(0, 1), HALF)
    send_near(1)

    for pos in range(3):
        arrived(trecv.at[pos], tr_sem.at[pos, 0])
        arrived(tdrecv.at[pos], tr_sem.at[pos, 1])
    denoms = tden[...] + tdrecv[0] + tdrecv[1] + tdrecv[2]
    for h in range(NH):
        lanes = slice(h * HD, (h + 1) * HD)
        numer = acc[h, trows, :HD]
        for pos in range(3):
            numer = numer + trecv[pos, :, lanes].astype(F32)
        tfin[:, lanes] = (numer / denoms[:, 8 * h : 8 * h + 1]).astype(BF16)
    place = text.at[pl.ds(pl.multiple_of(lax.rem(x // 2, 2) * 64 + 32 * role, 32), TQ),
                    pl.ds(pl.multiple_of(zh * W, HD), W)]
    core_of = lax.rem(x, 2)
    for dx in range(4):
        for dz in range(2):
            if dx + dz:
                sends.start(tfin, place, text_sem.at[0], dev(x + dx, y, z + 2 * dz, core_of))
    elsewhere = core_of != c

    @pl.when(core_of == c)
    def _():
        pltpu.make_async_copy(tfin, place, text_sem.at[0]).start()

    @pl.when(elsewhere)
    def _():
        sends.start(tfin, place, text_sem.at[0], sibling, elsewhere)

    pass_weights(0)
    over(middle_blocks + last_blocks, q_row(3, 0), HALF)
    send_far(0)
    over(middle_blocks + last_blocks, q_row(1, 0), 512)
    send_near(0)
    combine(1)

    for copy in load_wo_text:
        copy.wait()
    arrived(text, text_sem.at[0])
    far_row = pl.multiple_of((1 - zl) * 64, 64)
    own_row = pl.multiple_of(zl * 64, 64)
    for i in range(8):
        weight = wtb[i * 2 * W : (i + 1) * 2 * W, :]
        gsend[:, i * W : (i + 1) * W] = jnp.dot(
            text[pl.ds(far_row, 64), :], weight, preferred_element_type=F32).astype(BF16)
    low, high = pl.ds(0, 32), pl.ds(32, 32)
    sends.start(gsend.at[low], grecv.at[low], out_sem.at[0], zp)
    sends.start(gsend.at[high], grecv.at[high], out_sem.at[0], zm)
    pass_weights(1)
    over(middle_blocks + last_blocks, q_row(0, 0), HALF)
    combine(0)

    for i in range(8):
        weight = wtb[i * 2 * W : (i + 1) * 2 * W, :]
        gown[:, i * W : (i + 1) * W] = jnp.dot(
            text[pl.ds(own_row, 64), :], weight, preferred_element_type=F32)
    load_wo.wait()
    arrived(wob.at[theirs], w_sem.at[0])
    for k in range(4):
        arrived(far_piece(1 - c, k), w_sem.at[6 + k])

    def product(group, cols):
        rows = pl.ds(pl.multiple_of(group * 2 * W, HD), 2 * W)
        return jnp.dot(attn[:, rows], wob[rows, cols], preferred_element_type=F32)

    arrived(attn.at[:, pl.ds(pl.multiple_of((1 - zl) * 2 * W, HD), 2 * W)], attn_sem.at[1])
    for i in range(NCH):
        cols = slice(i * CH, (i + 1) * CH)
        vown[:, cols] = product(1 - zl, cols)
    arrived(attn.at[:, pl.ds(pl.multiple_of(zl * 2 * W, HD), 2 * W)], attn_sem.at[0])
    for i in range(NCH):
        cols = slice(i * CH, (i + 1) * CH)
        video_out_ref[:, cols] = (
            mod1[0, pl.ds(step, 1), cols] * (vown[:, cols] + product(zl, cols))).astype(BF16)
    arrived(grecv, out_sem.at[0])
    row = lax.broadcasted_iota(jnp.int32, (64, CH), 0) + (zl * 2 + c) * 64
    valid = row < len_ref[0]
    for i in range(NCH):
        cols = slice(i * CH, (i + 1) * CH)
        text_out_ref[:, cols] = jnp.where(
            valid, mod2[1, pl.ds(step, 1), cols] * (gown[:, cols] + grecv[:, cols].astype(F32)),
            0.0).astype(BF16)
    sends.finish()


def place_kernel(video_ref, text_ref, video_out_ref, text_out_ref):
    video_out_ref[...] = video_ref[...]
    text_out_ref[...] = text_ref[...]


ANY = pl.BlockSpec(memory_space=pl.ANY)
VMEM = pl.BlockSpec(memory_space=pltpu.VMEM)
SMEM = pl.BlockSpec(memory_space=pltpu.SMEM)
DMA = pltpu.SemaphoreType.DMA


def body(x_video, x_text, w_qkv_video, w_qkv_text, w_out_video, w_out_text, qk_gains, modulation,
         text_len, timestep):
    wv = jnp.transpose(w_qkv_video, (1, 0, 2))
    wt = jnp.transpose(w_qkv_text, (1, 0, 2))
    mod = jnp.transpose(modulation, (1, 0, 2))
    shape = jax.ShapeDtypeStruct
    steps = modulation.shape[0]
    results = [shape((128, D), BF16), shape((64, D), BF16)]
    video, text, unused = pl.pallas_call(
        block_kernel,
        name="block",
        in_specs=[ANY, ANY, ANY, ANY, ANY, VMEM, ANY, ANY, SMEM, SMEM],
        out_specs=[VMEM, VMEM, ANY],
        out_shape=results + [shape((W, D), BF16)],
        scratch_shapes=[
            pltpu.VMEM((4, 128, D), BF16), pltpu.VMEM((TXT, D), BF16),
            pltpu.VMEM((D, 3 * W), BF16), pltpu.VMEM((3 * D, W), BF16),
            pltpu.VMEM((2, steps, D), F32), pltpu.VMEM((2, steps, D), F32), pltpu.VMEM((2, steps, D), F32),
            pltpu.VMEM((HALF, D), BF16),
            pltpu.VMEM((2, 3, HALF, W), BF16), pltpu.VMEM((TXT, W), BF16),
            pltpu.VMEM((QROWS, W), BF16), pltpu.VMEM((2, 4, 2, 2, HALF, W), BF16),
            pltpu.VMEM((2, TXT, W), BF16), pltpu.VMEM((NH, QROWS, 2 * HD), F32),
            pltpu.VMEM((3, 2, HALF, W), BF16), pltpu.VMEM((3, 2, 24, HALF), F32),
            pltpu.VMEM((2, 2, HALF, W), BF16), pltpu.VMEM((2, 2, 24, HALF), F32),
            pltpu.VMEM((2, 2, 128, W), BF16), pltpu.VMEM((2, 2, 24, 128), F32),
            pltpu.VMEM((TQ, W), BF16), pltpu.VMEM((TQ, HD), F32),
            pltpu.VMEM((3, TQ, W), BF16), pltpu.VMEM((3, TQ, HD), F32),
            pltpu.VMEM((2, HALF, W), BF16), pltpu.VMEM((TQ, W), BF16),
            pltpu.VMEM((128, 4 * W), BF16), pltpu.VMEM((128, 2 * W), BF16), pltpu.VMEM((4 * W, D), BF16),
            pltpu.VMEM((64, D), BF16), pltpu.VMEM((64, D), BF16),
            pltpu.VMEM((64, D), F32), pltpu.VMEM((128, D), F32),
            DMA((28,)), DMA((136,)), DMA((4,)), DMA((10,)), DMA((3, 2)), DMA((2, 4, 2, 2)), DMA((4, 2)),
            DMA((2,)), DMA((2, 2, 2)), DMA((2, 2, 2)), DMA((3, 2)), DMA((2,)), DMA((1,)), DMA((1,))],
        compiler_params=pltpu.CompilerParams(
            collective_id=1, has_side_effects=True, vmem_limit_bytes=VMEM_LIMIT),
    )(x_video, x_text, wv, wt, mod, qk_gains, w_out_video, w_out_text, text_len, timestep)
    return tuple(pl.pallas_call(
        place_kernel,
        name="place",
        in_specs=[VMEM, VMEM],
        out_specs=[VMEM, VMEM],
        out_shape=results,
    )(video, text))


def solution(mesh):
    grid = Mesh(mesh.devices.reshape(4, 4, 2, 2, 2), AXES)
    head = ("zl", "c")
    return jax.shard_map(
        body,
        mesh=grid,
        in_specs=(P(AXES, None), P(), P(None, None, head), P(None, None, head),
                  P(head, None), P(head, None), P(), P(), P(), P()),
        out_specs=(P(AXES, None), P(head, None)),
        check_vma=False,
    )
```

```python
import functools
import math

import jax
import jax.numpy as jnp
from jax import lax
from jax.experimental import pallas as pl
from jax.experimental.pallas import tpu as pltpu
from jax.sharding import Mesh, PartitionSpec as P

AXES = ("x", "y", "zh", "zl", "c")
MESH = pl.DeviceIdType.MESH
BF16, F32 = jnp.bfloat16, jnp.float32
D = 3072
HD = 128
NH = 3
W = NH * HD
HALF = 256
TXT = 256
TQ = 32
QROWS = 8 * HALF + TQ
ORDER = (3, 1, 2, 0)
CH = 768
NCH = D // CH
EXP_SCALE = math.log2(math.e) / math.sqrt(HD)
VMEM_LIMIT = 60 << 20


def coords():
    x, y, zh, zl, c = (lax.axis_index(a) for a in AXES)
    return x, y, zh * 2 + zl, c


def dev(x, y, z, c):
    z = lax.rem(z + 4, 4)
    return (lax.rem(x + 4, 4), lax.rem(y + 4, 4), z // 2, lax.rem(z, 2), c)


class Sends:
    def __init__(self, sems, peer):
        self.sems, self.peer, self.count, self.pending = sems, peer, 0, []

    def start(self, src, dst, recv_sem, device, pred=None):
        slot = self.count
        self.count += 1
        get = src if callable(src) else (lambda: src)

        pltpu.make_async_remote_copy(
            src_ref=get(), dst_ref=dst, send_sem=self.sems.at[slot], recv_sem=recv_sem,
            device_id=device, device_id_type=MESH).start()

        def wait():
            pltpu.make_async_remote_copy(
                src_ref=get(), dst_ref=get(), send_sem=self.sems.at[slot], recv_sem=self.sems.at[slot],
                device_id=self.peer, device_id_type=MESH).wait_send()

        self.pending.append((pred, wait))

    def finish(self):
        for pred, wait in self.pending:
            if pred is None:
                wait()
            else:
                pl.when(pred)(wait)


def signal(sem, device):
    pl.semaphore_signal(sem, inc=1, device_id=device, device_id_type=MESH)


def norm_rows(src, dst, dst_row, count, shift, scale1):
    def strip(i, carry):
        wide = src[pl.ds(pl.multiple_of(i * 16, 16), 16), :].astype(F32)
        centred = wide - jnp.mean(wide, axis=-1, keepdims=True)
        variance = jnp.mean(centred * centred, axis=-1, keepdims=True)
        out = centred * lax.rsqrt(variance + 1e-06) * scale1 + shift
        dst[pl.ds(pl.multiple_of(dst_row + i * 16, 16), 16), :] = out.astype(BF16)
        return carry

    lax.fori_loop(0, count // 16, strip, 0, unroll=2)


def project(rows, weights, outs, gain_query, gain_key):
    for part in range(3):
        flat = jnp.dot(rows, weights[part][...], preferred_element_type=F32)
        for h in range(NH):
            lanes = slice(h * HD, (h + 1) * HD)
            u = flat[:, lanes]
            if part < 2:
                gain = gain_query if part == 0 else gain_key
                meansq = jnp.mean(u * u, axis=-1, keepdims=True)
                u = u * lax.rsqrt(meansq + 1e-06) * gain
            outs[part][:, lanes] = u.astype(BF16)


def project_wide(rows, weight, out, gain_query, gain_key):
    flat = jnp.dot(rows, weight[...], preferred_element_type=F32)
    for part in range(3):
        for h in range(NH):
            u = flat[:, part * W + h * HD : part * W + (h + 1) * HD]
            if part < 2:
                gain = gain_query if part == 0 else gain_key
                meansq = jnp.mean(u * u, axis=-1, keepdims=True)
                u = u * lax.rsqrt(meansq + 1e-06) * gain
            out[part, :, h * HD : (h + 1) * HD] = u.astype(BF16)


def attend(qb, q0, count, keys, values, acc, first, mask=None):
    for h in range(NH):
        lanes = slice(h * HD, (h + 1) * HD)
        query = qb[pl.ds(q0, count), lanes]
        total = None
        for key_ref, value_ref in zip(keys, values):
            scores = lax.dot_general(
                query, key_ref[:, lanes], (((1,), (1,)), ((), ())), preferred_element_type=F32)
            expo = jnp.exp2(scores * EXP_SCALE)
            if mask is not None:
                expo = jnp.where(mask, expo, 0.0)
            value = value_ref[:, lanes]
            wide = jnp.concatenate([value, jnp.ones_like(value)], axis=1)
            part = jnp.dot(expo.astype(BF16), wide, preferred_element_type=F32)
            total = part if total is None else total + part
        if first:
            acc[h, pl.ds(q0, count), :] = total
        else:
            acc[h, pl.ds(q0, count), :] += total


def coded_denoms(acc, rows):
    parts = [acc[h, rows, HD:] for h in range(NH)]
    lane = lax.broadcasted_iota(jnp.int32, parts[0].shape, 1)
    return jnp.where(lane < 8, parts[0], jnp.where(lane < 16, parts[1], parts[2]))


def q_row(pos, half):
    return TQ + ORDER.index(pos) * HALF + (0 if half else 4 * HALF)


TROW = 0


def block_kernel(x_ref, xt_ref, wv_ref, wt_ref, mod_ref, gains_ref, wov_ref, wot_ref, len_ref, step_ref,
                 video_out_ref, text_out_ref, wst_ref,
                 xb, xtb, wvb, wtb, mod0, mod1, mod2, nb, stg, tqst, qb, kvb, tkv, acc, osend, dsend, orecv, drecv,
                 rrecv, rden, tsend, tden, trecv, tdrecv, afin, tfin, attn, text, wob, gsend, grecv, gown, vown,
                 load_sem, send_sem, x_sem, w_sem, own_sem, kv_sem, q_sem, t_sem, o_sem, r_sem, tr_sem,
                 attn_sem, text_sem, out_sem):
    x, y, z, c = coords()
    zh, zl = z // 2, lax.rem(z, 2)
    role = lax.rem(c + zh, 2)
    is0, is1 = role == 0, role == 1
    sibling = dev(x, y, z, 1 - c)
    partner = dev(x, y, z + 2, 1 - c)
    xp, xm = dev(x + 1, y, z, c), dev(x - 1, y, z, c)
    yps = {1: dev(x, y + 1, z, c), 2: dev(x, y - 1, z, c), 3: dev(x, y + 2, z, c)}
    zp, zm = dev(x, y, z + 1, c), dev(x, y, z - 1, c)

    load_x = pltpu.make_async_copy(x_ref, xb.at[c], load_sem.at[0])
    load_mod = [
        pltpu.make_async_copy(mod_ref.at[pl.ds(2 * i, 2)], part, load_sem.at[1 + i])
        for i, part in enumerate((mod0, mod1, mod2))]
    load_wv = [
        pltpu.make_async_copy(wv_ref.at[part], wvb.at[:, part * W : (part + 1) * W], load_sem.at[4 + part])
        for part in range(3)]
    load_xt = pltpu.make_async_copy(xt_ref, xtb, load_sem.at[7])
    load_wt = [
        pltpu.make_async_copy(wt_ref.at[part], wtb.at[pl.ds(part * D, D)], load_sem.at[8 + part])
        for part in range(3)]
    for copy in [load_x, load_mod[0]] + load_wv:
        copy.start()

    @pl.when(is0)
    def _():
        for copy in [load_xt] + load_wt:
            copy.start()

    load_mod[1].start()
    load_mod[2].start()

    barrier = pltpu.get_barrier_semaphore()
    for device in (sibling, xp, xm, yps[1], yps[2], yps[3], zp, zm, dev(x, y, z + 2, zh)):
        signal(barrier, device)

    @pl.when(is1)
    def _():
        signal(barrier, dev(x, y, z + 2, 1 - zh))

    step = step_ref[0]
    load_x.wait()
    load_mod[0].wait()
    shift, scale1 = mod0[0, pl.ds(step, 1), :], 1.0 + mod0[1, pl.ds(step, 1), :]
    norm_rows(xb.at[c], nb, 128 * c, 128, shift, scale1)
    pl.semaphore_wait(barrier, 9 + role)

    sends = Sends(send_sem, sibling)

    def arrived(dst, sem):
        pltpu.make_async_remote_copy(
            src_ref=dst, dst_ref=dst, send_sem=send_sem.at[0], recv_sem=sem,
            device_id=sibling, device_id_type=MESH).wait_recv()

    for rows, device, sem in ((pl.ds(0, 64), zm, x_sem.at[1]), (pl.ds(64, 64), zp, x_sem.at[2])):
        sends.start(lambda rows=rows: x_ref.at[rows], xb.at[2 + c, rows], sem, device)
    sends.start(x_ref, xb.at[c], x_sem.at[0], sibling)

    def q_half(pos, half):
        return qb.at[pl.ds(q_row(pos, half), HALF)]

    def send_queries(src, half, pred):
        for pos, back in ((3, 3), (1, 2), (2, 1)):
            sends.start(src, q_half(back, half), q_sem.at[back, half], yps[pos], pred)

    def send_keys(src, r, half, pred):
        sends.start(src, kvb.at[r, 2, half], kv_sem.at[r, 2, half, 0], xp, pred)
        sends.start(src, kvb.at[r, 1, half], kv_sem.at[r, 1, half, 0], xm, pred)
        sends.start(src, kvb.at[r, 0, half], kv_sem.at[r, 0, half, 0], sibling, pred)

    def stage_q(half):
        return stg.at[half, 0]

    def stage_kv(half):
        return stg.at[half, pl.ds(1, 2)]

    def send_half(half):
        copies = [
            pltpu.make_async_copy(stage_q(half), q_half(0, half), own_sem.at[half, 0]),
            pltpu.make_async_copy(stage_kv(half), kvb.at[0, 0, half], own_sem.at[half, 1])]
        for copy in copies:
            copy.start()
        send_keys(lambda: stage_kv(half), 0, half, is0)
        if half == 0:
            send_queries(lambda: stage_q(half), half, is0)
        for copy in copies:
            copy.wait()

    def swap_q(half):
        sends.start(lambda: stage_q(half), q_half(0, half), q_sem.at[0, half], partner, is1)

    def swap_kv(half):
        sends.start(lambda: stage_kv(half), kvb.at[1, 0, half], kv_sem.at[1, 0, half, 0], partner, is1)

    def swapped_q(half):
        arrived(q_half(0, half), q_sem.at[0, half])
        send_queries(lambda: q_half(0, half), half, is1)

    def swapped_kv(half):
        arrived(kvb.at[1, 0, half], kv_sem.at[1, 0, half, 0])
        send_keys(lambda: kvb.at[1, 0, half], 1, half, is1)

    def pass_on(r, half, pred):
        arrived(kvb.at[r, 1, half], kv_sem.at[r, 1, half, 0])
        sends.start(lambda: kvb.at[r, 1, half, 0], kvb.at[r, 3, half, 0], kv_sem.at[r, 3, half, 0], xm, pred)
        arrived(kvb.at[r, 2, half], kv_sem.at[r, 2, half, 0])
        sends.start(lambda: kvb.at[r, 2, half, 1], kvb.at[r, 3, half, 1], kv_sem.at[r, 3, half, 1], xp, pred)
        for pos in (1, 2):
            sends.start(lambda pos=pos: kvb.at[r, pos, half], kvb.at[r, pos, half],
                        kv_sem.at[r, pos, half, 0], sibling, pred)

    def pass_last(r, half, pred):
        for part in range(2):
            arrived(kvb.at[r, 3, half, part], kv_sem.at[r, 3, half, part])
        sends.start(lambda: kvb.at[r, 3, half], kvb.at[r, 3, half], kv_sem.at[r, 3, half, 0], sibling, pred)

    def from_sibling(r, blocks):
        for pos, half in blocks:
            arrived(kvb.at[r, pos, half], kv_sem.at[r, pos, half, 0])

    def on(pred, *steps):
        @pl.when(pred)
        def _():
            for step in steps:
                step()

    def over(blocks, q0, count, first=False):
        attend(qb, q0, count, [kvb.at[r, p, f, 0] for r, p, f in blocks],
               [kvb.at[r, p, f, 1] for r, p, f in blocks], acc, first)

    arrived(xb.at[1 - c], x_sem.at[0])
    norm_rows(xb.at[1 - c], nb, 128 * (1 - c), 128, shift, scale1)
    for copy in load_wv:
        copy.wait()
    project_wide(nb[...], wvb, stg.at[0], gains_ref[0:1, :], gains_ref[1:2, :])
    on(is0, lambda: send_half(0))
    on(is1, lambda: swap_q(0))
    ours = pl.ds(pl.multiple_of((2 * zl + c) * W, 16), W)
    theirs = pl.ds(pl.multiple_of((2 * zl + 1 - c) * W, 16), W)
    quarter = W // 4

    def send_weights(piece):
        for side, device in ((0, zp), (1, zm)):
            first_row = (2 * side + piece) * quarter
            place = pl.multiple_of((2 * zl + c) * W + first_row, 16)
            sends.start(lambda first_row=first_row: wov_ref.at[pl.ds(first_row, quarter)],
                        wob.at[pl.ds(place, quarter)], w_sem.at[2 + 2 * side + piece], device)

    def far_piece(core, k):
        return wob.at[pl.ds(pl.multiple_of((2 - 2 * zl + core) * W + k * quarter, 16), quarter)]

    def pass_weights(piece):
        for k in (piece, 2 + piece):
            arrived(far_piece(c, k), w_sem.at[2 + k])
            sends.start(lambda k=k: far_piece(c, k), far_piece(c, k), w_sem.at[6 + k], sibling)

    sends.start(wot_ref, wst_ref, w_sem.at[1], sibling)
    load_wo = pltpu.make_async_copy(wov_ref, wob.at[ours], load_sem.at[11])
    load_wo.start()
    load_mod[1].wait()
    load_mod[2].wait()

    tq_row = pl.multiple_of(64 * x, 64)
    tq_other = tqst.at[pl.ds(pl.multiple_of(64 * x + TQ, TQ), TQ)]
    tq_own = qb.at[pl.ds(TROW, TQ)]

    @pl.when(is0)
    def _():
        load_xt.wait()
        for copy in load_wt:
            copy.wait()
        norm_rows(xtb, nb, 0, TXT, mod1[1, pl.ds(step, 1), :], 1.0 + mod2[0, pl.ds(step, 1), :])
        project(nb[...], [wtb.at[pl.ds(part * D, D)] for part in range(3)],
                [tqst, tkv.at[0], tkv.at[1]], gains_ref[2:3, :], gains_ref[3:4, :])
        copy = pltpu.make_async_copy(tqst.at[pl.ds(tq_row, TQ)], tq_own, own_sem.at[2, 0])
        copy.start()
        sends.start(tq_other, tq_own, t_sem.at[0], sibling, is0)
        sends.start(tkv, tkv, t_sem.at[1], sibling, is0)
        copy.wait()

    arrived(xb.at[2 + c, pl.ds(0, 64)], x_sem.at[1])
    arrived(xb.at[2 + c, pl.ds(64, 64)], x_sem.at[2])
    sends.start(xb.at[2 + c], xb.at[2 + c], x_sem.at[3], sibling)
    on(is1, lambda: swap_kv(0))
    norm_rows(xb.at[2 + c], nb, 128 * c, 128, shift, scale1)
    on(is1, lambda: swapped_q(0))
    arrived(xb.at[3 - c], x_sem.at[3])
    norm_rows(xb.at[3 - c], nb, 128 * (1 - c), 128, shift, scale1)
    on(is0, lambda: pass_on(0, 0, is0))
    project_wide(nb[...], wvb, stg.at[1], gains_ref[0:1, :], gains_ref[1:2, :])
    on(is0, lambda: send_half(1))
    on(is1, lambda: swap_q(1), lambda: swap_kv(1), lambda: swapped_kv(0))

    first_rows = q_row(ORDER[0], 0)

    def rows_of(base, size, i):
        return pl.multiple_of(base + i * size, 16)

    on(is1, lambda: from_sibling(0, [(0, 0), (1, 0), (2, 0)]))
    for pos in (1, 2, 3):
        arrived(q_half(pos, 0), q_sem.at[pos, 0])

    def first(i, carry):
        on(jnp.logical_and(i == 1, is0), lambda: send_queries(lambda: stage_q(1), 1, is0),
           lambda: pass_last(0, 0, is0))
        on(jnp.logical_and(i == 1, is1), lambda: swapped_q(1))
        over([(0, 0, 0), (0, 1, 0), (0, 2, 0)], rows_of(first_rows, 512, i), 512, True)
        return carry

    lax.fori_loop(0, 2, first, 0)
    on(is0, lambda: from_sibling(1, [(0, 0)]))
    on(is1, lambda: from_sibling(0, [(3, 0), (0, 1)]))

    def second(i, carry):
        over([(0, 3, 0), (0, 0, 1), (1, 0, 0)], rows_of(first_rows, 512, i), 512)
        return carry

    lax.fori_loop(0, 2, second, 0)
    on(is0, lambda: pass_on(0, 1, is0))
    on(is1, lambda: pass_on(1, 0, is1), lambda: swapped_kv(1),
       lambda: arrived(tq_own, t_sem.at[0]), lambda: arrived(tkv, t_sem.at[1]))
    send_weights(0)

    arrived(wst_ref, w_sem.at[1])
    load_wo_text = []
    for i in range(8):
        cols = slice(i * W, (i + 1) * W)
        for k, (src, place) in enumerate(((wot_ref, c), (wst_ref, 1 - c))):
            rows = pl.ds(pl.multiple_of(i * 2 * W + place * W, 16), W)
            load_wo_text.append(pltpu.make_async_copy(
                src.at[:, cols], wtb.at[rows], load_sem.at[12 + 2 * i + k]))
    for copy in load_wo_text:
        copy.start()
    for pos in (1, 2, 3):
        arrived(q_half(pos, 1), q_sem.at[pos, 1])

    def third(i, carry):
        over([(0, 0, 0), (0, 1, 0), (0, 2, 0), (0, 3, 0), (0, 0, 1), (1, 0, 0)],
             rows_of(0, 528, i), 528, True)
        return carry

    lax.fori_loop(0, 2, third, 0)
    send_weights(1)
    sends.start(wov_ref, wob.at[ours], w_sem.at[0], sibling)
    on(is1, lambda: pass_last(1, 0, is1),
       lambda: from_sibling(0, [(1, 1), (2, 1)]))
    on(is0, lambda: pass_last(0, 1, is0), lambda: from_sibling(1, [(1, 0), (2, 0), (0, 1)]))

    limit = len_ref[0]
    text_limit = jnp.where(y == 0, limit, 0)
    for q0, count, most in ((TROW, TQ, text_limit), (q_row(0, 1), HALF, limit), (q_row(0, 0), HALF, limit)):
        mask = lax.broadcasted_iota(jnp.int32, (count, TXT), 1) < most
        attend(qb, q0, count, [tkv.at[0]], [tkv.at[1]], acc, False, mask)

    middle_blocks = [(0, 1, 1), (0, 2, 1), (1, 1, 0), (1, 2, 0), (1, 0, 1)]
    last_blocks = [(0, 3, 1), (1, 3, 0), (1, 1, 1), (1, 2, 1), (1, 3, 1)]

    on(is1, lambda: pass_on(1, 1, is1))

    def middle(i, carry):
        on(jnp.logical_and(i == 1, is1), lambda: pass_last(1, 1, is1))
        over(middle_blocks, rows_of(0, 528, i), 528)
        return carry

    lax.fori_loop(0, 2, middle, 0)
    on(is1, lambda: from_sibling(0, [(3, 1)]))
    on(is0, lambda: from_sibling(1, [(3, 0), (1, 1), (2, 1), (3, 1)]))

    def fill_sums(pos, half):
        rows = pl.ds(q_row(pos, half), HALF)
        for h in range(NH):
            osend[pos - 1, half, :, h * HD : (h + 1) * HD] = acc[h, rows, :HD].astype(BF16)
        dsend[pos - 1, half] = jnp.transpose(coded_denoms(acc, rows))[:24]

    def send_far(half):
        fill_sums(3, half)
        for part, device in ((0, yps[1]), (1, yps[2])):
            cut = pl.ds(128 * part, 128)
            sends.start(lambda cut=cut: osend.at[2, half, cut], rrecv.at[part, half],
                        r_sem.at[part, half, 0], device)
            sends.start(lambda cut=cut: dsend.at[2, half, :, cut], rden.at[part, half],
                        r_sem.at[part, half, 1], device)

    def send_near(half):
        for pos, part in ((1, 0), (2, 1)):
            back = 1 - part
            fill_sums(pos, half)
            arrived(rrecv.at[part, half], r_sem.at[part, half, 0])
            arrived(rden.at[part, half], r_sem.at[part, half, 1])
            cut = slice(128 * part, 128 * part + 128)
            rows = pl.ds(q_row(pos, half) + 128 * part, 128)
            for h in range(NH):
                lanes = slice(h * HD, (h + 1) * HD)
                osend[pos - 1, half, cut, lanes] = (
                    acc[h, rows, :HD] + rrecv[part, half, :, lanes].astype(F32)).astype(BF16)
            dsend[pos - 1, half, :, cut] = dsend[pos - 1, half, :, cut] + rden[part, half]
            sends.start(lambda pos=pos: osend.at[pos - 1, half], orecv.at[back, half],
                        o_sem.at[back, half, 0], yps[pos])
            sends.start(lambda pos=pos: dsend.at[pos - 1, half], drecv.at[back, half],
                        o_sem.at[back, half, 1], yps[pos])

    acol = pl.ds(pl.multiple_of((2 * zl + zh) * W, HD), W)
    ahead = 1 - 2 * role

    def combine(half):
        for part in range(2):
            arrived(orecv.at[part, half], o_sem.at[part, half, 0])
            arrived(drecv.at[part, half], o_sem.at[part, half, 1])
        rows = pl.ds(q_row(0, half), HALF)
        denoms = drecv[0, half] + drecv[1, half]
        for h in range(NH):
            lanes = slice(h * HD, (h + 1) * HD)
            numer = acc[h, rows, :HD]
            for part in range(2):
                numer = numer + orecv[part, half, :, lanes].astype(F32)
            denom = acc[h, rows, HD:] + jnp.transpose(
                jnp.broadcast_to(denoms[8 * h : 8 * h + 1, :], (HD, HALF)))
            afin[half, :, lanes] = (numer / denom).astype(BF16)
        if half:
            for core in range(2):
                for first_row, step_z in ((0, ahead), (64, -ahead)):
                    rows = pl.ds(core * 128 + first_row, 64)
                    sends.start(lambda rows=rows: afin.at[half, rows],
                                attn.at[pl.ds(first_row, 64), acol], attn_sem.at[1],
                                dev(x, y, z + step_z, core))
            return
        for core in range(2):
            dst = attn.at[:, acol]
            across = jnp.logical_and(is0, c != core)

            def src(core=core):
                return afin.at[0, pl.ds(core * 128, 128)]

            @pl.when(is1)
            def _():
                sends.start(src, dst, attn_sem.at[0], dev(x, y, z + 2, core), is1)

            @pl.when(jnp.logical_and(is0, c == core))
            def _():
                pltpu.make_async_copy(src(), dst, attn_sem.at[0]).start()

            @pl.when(across)
            def _():
                sends.start(src, dst, attn_sem.at[0], sibling, across)

    over(last_blocks, TROW, TQ + HALF)

    trows = pl.ds(TROW, TQ)
    for h in range(NH):
        tsend[:, h * HD : (h + 1) * HD] = acc[h, trows, :HD].astype(BF16)
    tden[...] = coded_denoms(acc, trows)
    for pos, back in ((3, 3), (1, 2), (2, 1)):
        sends.start(tsend, trecv.at[back - 1], tr_sem.at[back - 1, 0], yps[pos])
        sends.start(tden, tdrecv.at[back - 1], tr_sem.at[back - 1, 1], yps[pos])
    send_far(1)
    over(last_blocks, q_row(1, 1), 512)
    over(last_blocks, q_row(0, 1), HALF)
    send_near(1)

    for pos in range(3):
        arrived(trecv.at[pos], tr_sem.at[pos, 0])
        arrived(tdrecv.at[pos], tr_sem.at[pos, 1])
    denoms = tden[...] + tdrecv[0] + tdrecv[1] + tdrecv[2]
    for h in range(NH):
        lanes = slice(h * HD, (h + 1) * HD)
        numer = acc[h, trows, :HD]
        for pos in range(3):
            numer = numer + trecv[pos, :, lanes].astype(F32)
        tfin[:, lanes] = (numer / denoms[:, 8 * h : 8 * h + 1]).astype(BF16)
    place = text.at[pl.ds(pl.multiple_of(lax.rem(x // 2, 2) * 64 + 32 * role, 32), TQ),
                    pl.ds(pl.multiple_of(zh * W, HD), W)]
    core_of = lax.rem(x, 2)
    for dx in range(4):
        for dz in range(2):
            if dx + dz:
                sends.start(tfin, place, text_sem.at[0], dev(x + dx, y, z + 2 * dz, core_of))
    elsewhere = core_of != c

    @pl.when(core_of == c)
    def _():
        pltpu.make_async_copy(tfin, place, text_sem.at[0]).start()

    @pl.when(elsewhere)
    def _():
        sends.start(tfin, place, text_sem.at[0], sibling, elsewhere)

    pass_weights(0)
    over(middle_blocks + last_blocks, q_row(3, 0), HALF)
    send_far(0)
    over(middle_blocks + last_blocks, q_row(1, 0), 512)
    send_near(0)
    combine(1)

    for copy in load_wo_text:
        copy.wait()
    arrived(text, text_sem.at[0])
    far_row = pl.multiple_of((1 - zl) * 64, 64)
    own_row = pl.multiple_of(zl * 64, 64)
    for i in range(8):
        weight = wtb[i * 2 * W : (i + 1) * 2 * W, :]
        gsend[:, i * W : (i + 1) * W] = jnp.dot(
            text[pl.ds(far_row, 64), :], weight, preferred_element_type=F32).astype(BF16)
    low, high = pl.ds(0, 32), pl.ds(32, 32)
    sends.start(gsend.at[low], grecv.at[low], out_sem.at[0], zp)
    sends.start(gsend.at[high], grecv.at[high], out_sem.at[0], zm)
    pass_weights(1)
    over(middle_blocks + last_blocks, q_row(0, 0), HALF)
    combine(0)

    for i in range(8):
        weight = wtb[i * 2 * W : (i + 1) * 2 * W, :]
        gown[:, i * W : (i + 1) * W] = jnp.dot(
            text[pl.ds(own_row, 64), :], weight, preferred_element_type=F32)
    load_wo.wait()
    arrived(wob.at[theirs], w_sem.at[0])
    for k in range(4):
        arrived(far_piece(1 - c, k), w_sem.at[6 + k])

    def product(group, cols):
        rows = pl.ds(pl.multiple_of(group * 2 * W, HD), 2 * W)
        return jnp.dot(attn[:, rows], wob[rows, cols], preferred_element_type=F32)

    arrived(attn.at[:, pl.ds(pl.multiple_of((1 - zl) * 2 * W, HD), 2 * W)], attn_sem.at[1])
    for i in range(NCH):
        cols = slice(i * CH, (i + 1) * CH)
        vown[:, cols] = product(1 - zl, cols)
    arrived(attn.at[:, pl.ds(pl.multiple_of(zl * 2 * W, HD), 2 * W)], attn_sem.at[0])
    for i in range(NCH):
        cols = slice(i * CH, (i + 1) * CH)
        video_out_ref[:, cols] = (
            mod1[0, pl.ds(step, 1), cols] * (vown[:, cols] + product(zl, cols))).astype(BF16)
    arrived(grecv, out_sem.at[0])
    row = lax.broadcasted_iota(jnp.int32, (64, CH), 0) + (zl * 2 + c) * 64
    valid = row < len_ref[0]
    for i in range(NCH):
        cols = slice(i * CH, (i + 1) * CH)
        text_out_ref[:, cols] = jnp.where(
            valid, mod2[1, pl.ds(step, 1), cols] * (gown[:, cols] + grecv[:, cols].astype(F32)),
            0.0).astype(BF16)
    sends.finish()


def place_kernel(video_ref, text_ref, video_out_ref, text_out_ref):
    video_out_ref[...] = video_ref[...]
    text_out_ref[...] = text_ref[...]


ANY = pl.BlockSpec(memory_space=pl.ANY)
VMEM = pl.BlockSpec(memory_space=pltpu.VMEM)
SMEM = pl.BlockSpec(memory_space=pltpu.SMEM)
DMA = pltpu.SemaphoreType.DMA


def body(x_video, x_text, w_qkv_video, w_qkv_text, w_out_video, w_out_text, qk_gains, modulation,
         text_len, timestep):
    wv = jnp.transpose(w_qkv_video, (1, 0, 2))
    wt = jnp.transpose(w_qkv_text, (1, 0, 2))
    mod = jnp.transpose(modulation, (1, 0, 2))
    shape = jax.ShapeDtypeStruct
    steps = modulation.shape[0]
    results = [shape((128, D), BF16), shape((64, D), BF16)]
    video, text, unused = pl.pallas_call(
        block_kernel,
        name="block",
        in_specs=[ANY, ANY, ANY, ANY, ANY, VMEM, ANY, ANY, SMEM, SMEM],
        out_specs=[VMEM, VMEM, ANY],
        out_shape=results + [shape((W, D), BF16)],
        scratch_shapes=[
            pltpu.VMEM((4, 128, D), BF16), pltpu.VMEM((TXT, D), BF16),
            pltpu.VMEM((D, 3 * W), BF16), pltpu.VMEM((3 * D, W), BF16),
            pltpu.VMEM((2, steps, D), F32), pltpu.VMEM((2, steps, D), F32), pltpu.VMEM((2, steps, D), F32),
            pltpu.VMEM((HALF, D), BF16),
            pltpu.VMEM((2, 3, HALF, W), BF16), pltpu.VMEM((TXT, W), BF16),
            pltpu.VMEM((QROWS, W), BF16), pltpu.VMEM((2, 4, 2, 2, HALF, W), BF16),
            pltpu.VMEM((2, TXT, W), BF16), pltpu.VMEM((NH, QROWS, 2 * HD), F32),
            pltpu.VMEM((3, 2, HALF, W), BF16), pltpu.VMEM((3, 2, 24, HALF), F32),
            pltpu.VMEM((2, 2, HALF, W), BF16), pltpu.VMEM((2, 2, 24, HALF), F32),
            pltpu.VMEM((2, 2, 128, W), BF16), pltpu.VMEM((2, 2, 24, 128), F32),
            pltpu.VMEM((TQ, W), BF16), pltpu.VMEM((TQ, HD), F32),
            pltpu.VMEM((3, TQ, W), BF16), pltpu.VMEM((3, TQ, HD), F32),
            pltpu.VMEM((2, HALF, W), BF16), pltpu.VMEM((TQ, W), BF16),
            pltpu.VMEM((128, 4 * W), BF16), pltpu.VMEM((128, 2 * W), BF16), pltpu.VMEM((4 * W, D), BF16),
            pltpu.VMEM((64, D), BF16), pltpu.VMEM((64, D), BF16),
            pltpu.VMEM((64, D), F32), pltpu.VMEM((128, D), F32),
            DMA((28,)), DMA((136,)), DMA((4,)), DMA((10,)), DMA((3, 2)), DMA((2, 4, 2, 2)), DMA((4, 2)),
            DMA((2,)), DMA((2, 2, 2)), DMA((2, 2, 2)), DMA((3, 2)), DMA((2,)), DMA((1,)), DMA((1,))],
        compiler_params=pltpu.CompilerParams(
            collective_id=1, has_side_effects=True, vmem_limit_bytes=VMEM_LIMIT),
    )(x_video, x_text, wv, wt, mod, qk_gains, w_out_video, w_out_text, text_len, timestep)
    return tuple(pl.pallas_call(
        place_kernel,
        name="place",
        in_specs=[VMEM, VMEM],
        out_specs=[VMEM, VMEM],
        out_shape=results,
    )(video, text))


def solution(mesh):
    grid = Mesh(mesh.devices.reshape(4, 4, 2, 2, 2), AXES)
    head = ("zl", "c")
    return jax.shard_map(
        body,
        mesh=grid,
        in_specs=(P(AXES, None), P(), P(None, None, head), P(None, None, head),
                  P(head, None), P(head, None), P(), P(), P(), P()),
        out_specs=(P(AXES, None), P(head, None)),
        check_vma=False,
    )
```
